32 devices in a mesh: head: 2 (over y), batch: 16 (over z, x, core).
Axes of the slice: x: 2, y: 2, z: 4, core: 2. Of those that a mesh axis runs over, the one named last changes fastest.
Arguments:
- short_rows: bfloat16 [32, 512, 1024], P('batch', 'head'), may hold values from -6 to 6
- medium_rows: bfloat16 [16, 1024, 1024], P('batch', 'head'), may hold values from -6 to 6
- long_rows: bfloat16 [16, 2048, 1024], P('batch', 'head'), may hold values from -6 to 6
- short_len: int32 [32], P('batch'), may hold values from 256 to 512, as said below
- medium_len: int32 [16], P('batch'), may hold values from 512 to 1024, as said below
- long_len: int32 [16], P('batch'), may hold values from 1024 to 2048, as said below
- short_cotangent: bfloat16 [32, 512, 1024], P('batch', 'head'), may hold values from -6 to 6
- medium_cotangent: bfloat16 [16, 1024, 1024], P('batch', 'head'), may hold values from -6 to 6
- long_cotangent: bfloat16 [16, 2048, 1024], P('batch', 'head'), may hold values from -6 to 6
- norm_gains: float32 [3, 1024], replicated, may hold values from 0.1 to 1.9
- norm_shifts: float32 [5, 1024], replicated, may hold values from -3 to 3
- head_weights: bfloat16 [3, 1024, 1024], P(None, None, 'head'), may hold values from -0.1875 to 0.1875
- head_biases: float32 [2, 1024], P(None, 'head'), may hold values from -3 to 3
- head_scale: float32 [16], P('head'), may hold values from 0.1 to 1.9
- out_weight: bfloat16 [1024, 1024], P('head'), may hold values from -0.75 to 0.75
- up_weight: bfloat16 [4096, 1024], P(('head', 'batch')), may hold values from -0.1875 to 0.1875
- mid_gain: float32 [4096], replicated, may hold values from 0.1 to 1.9
- mid_shifts: float32 [2, 4096], replicated, may hold values from -3 to 3
- down_weight: bfloat16 [4096, 1024], P(('head', 'batch')), may hold values from -0.09375 to 0.09375
Outputs:
- short_out: bfloat16 [32, 512, 1024], P('batch', 'head')
- medium_out: bfloat16 [16, 1024, 1024], P('batch', 'head')
- long_out: bfloat16 [16, 2048, 1024], P('batch', 'head')
- short_grad: bfloat16 [32, 512, 1024], P('batch', 'head')
- medium_grad: bfloat16 [16, 1024, 1024], P('batch', 'head')
- long_grad: bfloat16 [16, 2048, 1024], P('batch', 'head')
- grad_norm_gains: float32 [3, 1024], replicated
- grad_norm_shifts: float32 [5, 1024], replicated
- grad_head_weights: float32 [3, 1024, 1024], P(None, None, 'head')
- grad_head_biases: float32 [2, 1024], P(None, 'head')
- grad_head_scale: float32 [16], P('head')
- grad_out_weight: float32 [1024, 1024], P('head')
- grad_up_weight: float32 [4096, 1024], P(('head', 'batch'))
- grad_mid_gain: float32 [4096], replicated
- grad_mid_shifts: float32 [2, 4096], replicated
- grad_down_weight: float32 [4096, 1024], P(('head', 'batch'))
The draws below stay inside these ranges and needn't reach their ends.
Inputs may be any that keep to these rules, and one draw needn't show every extreme that they name: `short_len`: lengths of the rows of the first tensor; in each of the 16 groups of rows of one index of batch, at least one row of the three tensors together is used to its full length. `medium_len`: lengths of the rows of the second tensor, drawn as the first. `long_len`: lengths of the rows of the third tensor, drawn as the first.
All inputs are finite; a program needn't handle non-finite values.
Results may differ from the reference program's by a relative error of at most 0.02.
Values may be sent and summed in bfloat16 or wider, within the bound.
A program may use at most 384 MiB of HBM per device.

```python
import jax
import jax.numpy as jnp
from jax import lax

HEADS = 16
HEAD_DIM = 64
D = 1024
FF = 4096
LEN_S = 512
LEN_M = 1024
LEN_L = 2048
ROWS_S = 2
ROWS_M = 1
ROWS_L = 1
GROUPS = 16
SEQS_S = 32
SEQS_M = 16
SEQS_L = 16
N_HEAD = 2


def full_pick(key):
    return jax.random.randint(key, (GROUPS,), 0, ROWS_S + ROWS_M + ROWS_L)


def ragged(key, pick, rows, offset, span):
    drawn = jax.random.randint(key, (GROUPS, rows), span // 2, span + 1)
    chosen = pick[:, None] - offset == jnp.arange(rows, dtype=jnp.int32)[None, :]
    return jnp.where(chosen, span, drawn).reshape(GROUPS * rows).astype(jnp.int32)


def draw_short_len(key, part):
    pick = full_pick(key)
    key = jax.random.fold_in(key, 11)
    return ragged(key, pick, ROWS_S, 0, LEN_S)


def draw_medium_len(key, part):
    pick = full_pick(key)
    key = jax.random.fold_in(key, 12)
    return ragged(key, pick, ROWS_M, ROWS_S, LEN_M)


def draw_long_len(key, part):
    pick = full_pick(key)
    key = jax.random.fold_in(key, 13)
    return ragged(key, pick, ROWS_L, ROWS_S + ROWS_M, LEN_L)


def block_scale(stream_key, shape, cuts, smallest, high):
    def one(axis_at, parts):
        steps = jax.random.uniform(jax.random.fold_in(jax.random.fold_in(stream_key, 6), axis_at), (parts,), jnp.float32, smallest / len(cuts), high / len(cuts))
        return jnp.repeat(jnp.exp(steps), shape[axis_at] // parts).reshape((-1,) + (1,) * (len(shape) - axis_at - 1))

    level = one(*cuts[0])
    for cut in cuts[1:]:
        level = level * one(*cut)
    return level


def scatter_about(stream_key, dims, scale, bound, split=(), kind=jnp.bfloat16):
    loudness = block_scale(stream_key, dims, split, -0.22, 0.18) if split else 1.0
    entries = jax.random.normal(stream_key, dims, jnp.float32) * scale * loudness
    return jnp.minimum(jnp.maximum(entries, -bound), bound).astype(kind)


def setup_inputs(seed: int = 0) -> dict:
    streams_of = jax.random.split(jax.random.key(seed), 20)
    short_rows = scatter_about(streams_of[0], (SEQS_S, LEN_S, D), 1.0, 6.0, ((0, 16), (1, 2)))
    medium_rows = scatter_about(streams_of[1], (SEQS_M, LEN_M, D), 1.0, 6.0, ((0, 16), (1, 2)))
    long_rows = scatter_about(streams_of[2], (SEQS_L, LEN_L, D), 1.0, 6.0, ((0, 16), (1, 2)))
    short_len = draw_short_len(jax.random.fold_in(streams_of[19], 71), 0)
    medium_len = draw_medium_len(jax.random.fold_in(streams_of[19], 71), 0)
    long_len = draw_long_len(jax.random.fold_in(streams_of[19], 71), 0)
    short_cotangent = scatter_about(streams_of[6], (SEQS_S, LEN_S, D), 1.0, 6.0, ((0, 16), (1, 2)))
    medium_cotangent = scatter_about(streams_of[7], (SEQS_M, LEN_M, D), 1.0, 6.0, ((0, 16), (1, 2)))
    long_cotangent = scatter_about(streams_of[8], (SEQS_L, LEN_L, D), 1.0, 6.0, ((0, 16), (1, 2)))
    norm_gains = jnp.clip(1.0 + 0.18 * jax.random.normal(streams_of[9], (3, D), jnp.float32), 0.1, 1.9)
    norm_shifts = scatter_about(streams_of[10], (5, D), 0.3, 3.0, (), jnp.float32)
    head_weights = scatter_about(streams_of[11], (3, D, D), D ** -0.5, 0.1875, ((2, 2),))
    head_biases = scatter_about(streams_of[12], (2, D), 0.3, 3.0, ((1, 2),), jnp.float32)
    head_scale = jnp.clip(1.0 + 0.18 * jax.random.normal(streams_of[13], (HEADS,), jnp.float32), 0.1, 1.9)
    out_weight = scatter_about(streams_of[14], (D, D), (D // 16) ** -0.5, 0.75, ((0, 2),))
    up_weight = scatter_about(streams_of[15], (FF, D), D ** -0.5, 0.1875, ((0, 32),))
    mid_gain = jnp.clip(1.0 + 0.18 * jax.random.normal(streams_of[16], (FF,), jnp.float32), 0.1, 1.9)
    mid_shifts = scatter_about(streams_of[17], (2, FF), 0.3, 3.0, (), jnp.float32)
    down_weight = scatter_about(streams_of[18], (FF, D), FF ** -0.5, 0.09375, ((0, 32),))
    return dict(short_rows=short_rows, medium_rows=medium_rows, long_rows=long_rows, short_len=short_len, medium_len=medium_len, long_len=long_len, short_cotangent=short_cotangent, medium_cotangent=medium_cotangent, long_cotangent=long_cotangent, norm_gains=norm_gains, norm_shifts=norm_shifts, head_weights=head_weights, head_biases=head_biases, head_scale=head_scale, out_weight=out_weight, up_weight=up_weight, mid_gain=mid_gain, mid_shifts=mid_shifts, down_weight=down_weight)


@jax.custom_vjp
def low(v):
    return lax.optimization_barrier(v.astype(jnp.bfloat16)).astype(jnp.float32)

@jax.custom_vjp
def low_back(v):
    return v

def low_keep(v):
    return (low(v), None)

def low_pass(kept, grad):
    return (grad,)

def back_keep(v):
    return (v, None)

def back_low(kept, grad):
    return (low(grad),)
low.defvjp(low_keep, low_pass)
low_back.defvjp(back_keep, back_low)
HIGHEST = lax.Precision.HIGHEST
EPSILON = 1e-05

def layer_norm(value, gain, shift):
    centred = value - lax.optimization_barrier(jnp.mean(value, axis=-1, keepdims=True))
    spread = lax.optimization_barrier(jnp.mean(centred * centred, axis=-1, keepdims=True))
    return centred * lax.rsqrt(spread + EPSILON) * gain + shift

def attend(query, keys, values, lengths):
    rows, span, heads, width = query.shape
    block = min(512, span)
    count = span // block
    blocks = query.reshape(rows * count, block, heads, width)
    scale = width ** (-0.5)

    def one_block(item):
        query_block, index = item
        row = index // count
        start = index % count * block
        scores = low_back(jnp.einsum('qhd,khd->hqk', query_block, keys[row], precision=HIGHEST) * scale)
        query_place = start + jnp.arange(block, dtype=jnp.int32)[:, None]
        key_place = jnp.arange(span, dtype=jnp.int32)[None, :]
        allowed = (key_place <= query_place) & (key_place < lengths[row])
        scores = jnp.where(allowed[None], scores, -1e+30)
        top = lax.optimization_barrier(jnp.max(scores, axis=-1, keepdims=True))
        weights = jnp.exp(scores - top)
        shares = low(weights / lax.optimization_barrier(jnp.sum(weights, axis=-1, keepdims=True)))
        return jnp.einsum('hqk,khd->qhd', shares, values[row], precision=HIGHEST)
    mixed = lax.map(jax.checkpoint(one_block), (blocks, jnp.arange(rows * count, dtype=jnp.int32)))
    return mixed.reshape(rows, span, heads, width)

def tensor_attention(normed, lengths, head_weights, head_biases, head_scale, out_weight):
    rows, span, width = normed.shape
    part = width // N_HEAD
    per_group = HEADS // N_HEAD
    flat_rows = normed.reshape(rows * span, width)
    total = jnp.zeros((rows * span, width), jnp.float32)
    for group in range(N_HEAD):
        low_col = group * part
        high_col = low_col + part
        mine = low_back(flat_rows)
        query = low(low_back(jnp.dot(mine, head_weights[0][:, low_col:high_col], precision=HIGHEST) + head_biases[0, low_col:high_col]))
        keys = low(low_back(jnp.dot(mine, head_weights[1][:, low_col:high_col], precision=HIGHEST)))
        values = low(low_back(jnp.dot(mine, head_weights[2][:, low_col:high_col], precision=HIGHEST) + head_biases[1, low_col:high_col]))
        shape = (rows, span, per_group, HEAD_DIM)
        mixed = low_back(attend(query.reshape(shape), keys.reshape(shape), values.reshape(shape), lengths))
        scales = head_scale[group * per_group:(group + 1) * per_group]
        scaled = low((mixed * scales[:, None]).reshape(rows * span, part))
        total = total + low(jnp.dot(scaled, out_weight[low_col:high_col, :], precision=HIGHEST))
    return low_back(total).reshape(rows, span, width)

def layer_forward(params, inputs, lengths):
    norm_gains, norm_shifts, head_weights, head_biases, head_scale, out_weight, up_weight, mid_gain, mid_shifts, down_weight = params
    pieces = []
    for rows_in, length in zip(inputs, lengths):
        normed = low(layer_norm(rows_in, norm_gains[0], norm_shifts[0]))
        attended = tensor_attention(normed, length, head_weights, head_biases, head_scale, out_weight)
        after = rows_in + layer_norm(attended + norm_shifts[3], norm_gains[1], norm_shifts[1])
        pieces.append(after.reshape(-1, D))
    residual = jnp.concatenate(pieces, 0)
    dense_in = low(layer_norm(residual, norm_gains[2], norm_shifts[2]))
    hidden = low_back(jnp.dot(dense_in, up_weight.T, precision=HIGHEST) + mid_shifts[0])
    middle = low(layer_norm(jax.nn.gelu(hidden), mid_gain, mid_shifts[1]))
    result = residual + jnp.dot(middle, down_weight, precision=HIGHEST) + norm_shifts[4]
    outputs = []
    offset = 0
    for rows_in in inputs:
        number = rows_in.shape[0] * rows_in.shape[1]
        outputs.append(result[offset:offset + number].reshape(rows_in.shape))
        offset += number
    return tuple(outputs)

def reference(short_rows, medium_rows, long_rows, short_len, medium_len, long_len, short_cotangent, medium_cotangent, long_cotangent, norm_gains, norm_shifts, head_weights, head_biases, head_scale, out_weight, up_weight, mid_gain, mid_shifts, down_weight):
    params = (norm_gains.astype(jnp.float32), norm_shifts.astype(jnp.float32), head_weights.astype(jnp.float32), head_biases.astype(jnp.float32), head_scale.astype(jnp.float32), out_weight.astype(jnp.float32), up_weight.astype(jnp.float32), mid_gain.astype(jnp.float32), mid_shifts.astype(jnp.float32), down_weight.astype(jnp.float32))
    shapes = ((ROWS_S, LEN_S), (ROWS_M, LEN_M), (ROWS_L, LEN_L))

    def grouped(arrays):
        return tuple((array.reshape((GROUPS,) + shape + (D,)) for array, shape in zip(arrays, shapes)))
    inputs = grouped((short_rows, medium_rows, long_rows))
    cotangents = grouped((short_cotangent, medium_cotangent, long_cotangent))
    lengths = tuple((array.reshape(GROUPS, shape[0]) for array, shape in zip((short_len, medium_len, long_len), shapes)))

    def one_group(totals, item):
        rows_in, lens_in, cots_in = item
        wide_rows = tuple((array.astype(jnp.float32) for array in rows_in))

        def forward(weights, first, second, third):
            return layer_forward(weights, (first, second, third), lens_in)
        outputs, pull = jax.vjp(forward, params, *wide_rows)
        grads = pull(tuple((array.astype(jnp.float32) for array in cots_in)))
        totals = jax.tree.map(jnp.add, totals, grads[0])
        return (totals, (tuple((array.astype(jnp.bfloat16) for array in outputs)), tuple((array.astype(jnp.bfloat16) for array in grads[1:]))))
    zeros = jax.tree.map(jnp.zeros_like, params)
    totals, (outputs, input_grads) = lax.scan(one_group, zeros, (inputs, lengths, cotangents))
    seqs = (SEQS_S, SEQS_M, SEQS_L)
    lens_all = (LEN_S, LEN_M, LEN_L)
    outputs = tuple((array.reshape(rows, span, D) for array, rows, span in zip(outputs, seqs, lens_all)))
    input_grads = tuple((array.reshape(rows, span, D) for array, rows, span in zip(input_grads, seqs, lens_all)))
    return (outputs[0], outputs[1], outputs[2], input_grads[0], input_grads[1], input_grads[2], totals[0], totals[1], totals[2], totals[3], totals[4], totals[5], totals[6], totals[7], totals[8], totals[9])
```

```python
import functools

import jax
import jax.numpy as jnp
from jax import lax
from jax.experimental import pallas as pl
from jax.experimental.pallas import tpu as pltpu
from jax.sharding import PartitionSpec as P

EPSILON = 1e-05
ROW_PAIRS = (((0,), (0,)), ((), ()))
COLUMN_PAIRS = (((1,), (1,)), ((), ()))
LANES = 128
HEAD = 64
LOG2E = 1.4426950408889634
EXPONENT_SCALE = HEAD ** (-0.5) * LOG2E
MASKED = -1e30
GELU_SCALE = 0.7978845608028654
GELU_CUBE = 0.044715
BF = jnp.bfloat16
F32 = jnp.float32


def dot(a, b, dims=(((1,), (0,)), ((), ()))):
    return lax.dot_general(a, b, dims, preferred_element_type=F32)


def normalize(value, gain, shift):
    centred = value - jnp.mean(value, axis=-1, keepdims=True)
    inverse = lax.rsqrt(jnp.mean(centred * centred, axis=-1, keepdims=True) + EPSILON)
    unit = centred * inverse
    return (unit * gain + shift, unit, inverse)


def normalize_back(grad, unit, inverse, gain):
    scaled = grad * gain
    inner = (
        scaled
        - jnp.mean(scaled, axis=-1, keepdims=True)
        - unit * jnp.mean(scaled * unit, axis=-1, keepdims=True)
    )
    return (inner * inverse, jnp.sum(grad * unit, axis=0), jnp.sum(grad, axis=0))


def place(me, slot, slots, part):
    return pl.multiple_of(lax.rem(me + slot, slots) * part, part)


def attend_forward_kernel(slots, span, block, kept, me_ref, len_ref, *refs):
    qkv = refs[:slots]
    scale_ref = refs[slots]
    refs = refs[kept:]
    outs = refs[slots + 1 : 2 * slots + 1]
    total_ref = refs[2 * slots + 1]
    query, keys, values, mixed = refs[2 * slots + 2 :]
    part = span // slots
    me = me_ref[0]
    length = len_ref[pl.program_id(0)]
    for slot in range(slots):
        at = pl.ds(place(me, slot, slots, part), part)
        query[at, :] = qkv[slot][:, :LANES]
        keys[at, :] = qkv[slot][:, LANES : 2 * LANES]
        values[at, :] = qkv[slot][:, 2 * LANES :]
    first = lax.broadcasted_iota(jnp.int32, (1, LANES), 1) < HEAD
    for i in range(span // block):
        rows = slice(i * block, (i + 1) * block)
        query_block = query[rows, :]
        halves = []
        for head in range(2):
            mine = first if head == 0 else jnp.logical_not(first)
            query_head = jnp.where(mine, query_block, jnp.zeros_like(query_block))
            scores = []
            for j in range(i + 1):
                key_block = keys[j * block : (j + 1) * block, :]
                score = dot(query_head, key_block, COLUMN_PAIRS)
                key_place = lax.broadcasted_iota(jnp.int32, (block, block), 1)
                allowed = None
                if i == j:
                    allowed = key_place <= lax.broadcasted_iota(jnp.int32, (block, block), 0)
                if (j + 1) * block > span // 2:
                    short = key_place < length - j * block
                    allowed = short if allowed is None else allowed & short
                if allowed is not None:
                    score = jnp.where(allowed, score, MASKED)
                scores.append(score)
            top = functools.reduce(jnp.maximum, scores)
            top = jnp.max(top, axis=-1, keepdims=True) * EXPONENT_SCALE
            weights = [jnp.exp2(score * EXPONENT_SCALE - top) for score in scores]
            total = jnp.sum(functools.reduce(jnp.add, weights), axis=-1, keepdims=True)
            result = None
            for j in range(i + 1):
                term = dot(weights[j].astype(BF), values[j * block : (j + 1) * block, :])
                result = term if result is None else result + term
            halves.append(result / total)
            log_total = jnp.broadcast_to(top + jnp.log2(total), (block, LANES))
            total_ref[0, 0, head : head + 1, rows] = jnp.transpose(log_total)[:1, :]
        mixed[rows, :] = (jnp.where(first, halves[0], halves[1]) * scale_ref[...]).astype(BF)
    for slot in range(slots):
        outs[slot][...] = mixed[pl.ds(place(me, slot, slots, part), part), :]


def attend_backward_kernel(slots, span, block, kept, me_ref, len_ref, *refs):
    qkv = refs[:slots]
    out = refs[slots : 2 * slots]
    grads = refs[2 * slots : 3 * slots]
    scale_ref, total_ref = refs[3 * slots : 3 * slots + 2]
    refs = refs[kept:]
    results = refs[3 * slots + 2 : 4 * slots + 2]
    sums_ref = refs[4 * slots + 2]
    query, keys, values, mixed_grad, product, query_grad, key_grad, value_grad = refs[4 * slots + 3 :]
    part = span // slots
    me = me_ref[0]
    length = len_ref[pl.program_id(0)]
    for slot in range(slots):
        at = pl.ds(place(me, slot, slots, part), part)
        query[at, :] = qkv[slot][:, :LANES]
        keys[at, :] = qkv[slot][:, LANES : 2 * LANES]
        values[at, :] = qkv[slot][:, 2 * LANES :]
        grad = grads[slot][...].astype(F32)
        mixed_grad[at, :] = (grad * scale_ref[...]).astype(BF)
        product[at, :] = grad * out[slot][...].astype(F32)
    first = lax.broadcasted_iota(jnp.int32, (1, LANES), 1) < HEAD
    which = lax.broadcasted_iota(jnp.int32, (8, LANES), 0)
    lane_head = lax.broadcasted_iota(jnp.int32, (8, LANES), 1) // HEAD
    picks = jnp.where(which == lane_head, 1.0, 0.0).astype(BF)
    inner = product[...]
    inner_high = inner.astype(BF)
    inner_low = (inner - inner_high.astype(F32)).astype(BF)
    inner_sum = dot(picks, inner_high, COLUMN_PAIRS) + dot(picks, inner_low, COLUMN_PAIRS)
    scale_sum = jnp.sum(inner, axis=0, keepdims=True) / scale_ref[...]
    count = span // block
    for j in range(count):
        cols = slice(j * block, (j + 1) * block)
        key_block, value_block = keys[cols, :], values[cols, :]
        key_parts, value_parts = [], []
        for head in range(2):
            mine = first if head == 0 else jnp.logical_not(first)
            key_head = jnp.where(mine, key_block, jnp.zeros_like(key_block))
            value_head = jnp.where(mine, value_block, jnp.zeros_like(value_block))
            key_sum = value_sum = None
            for i in range(j, count):
                rows = slice(i * block, (i + 1) * block)
                query_block, grad_block = query[rows, :], mixed_grad[rows, :]
                score = dot(key_head, query_block, COLUMN_PAIRS)
                shares = jnp.exp2(score * EXPONENT_SCALE - total_ref[0, 0, head : head + 1, rows])
                key_place = lax.broadcasted_iota(jnp.int32, (block, block), 0)
                allowed = None
                if i == j:
                    allowed = key_place <= lax.broadcasted_iota(jnp.int32, (block, block), 1)
                if (j + 1) * block > span // 2:
                    short = key_place < length - j * block
                    allowed = short if allowed is None else allowed & short
                if allowed is not None:
                    shares = jnp.where(allowed, shares, 0.0)
                share_grad = dot(value_head, grad_block, COLUMN_PAIRS)
                score_grad = shares * (share_grad - inner_sum[head : head + 1, rows])
                score_grad = score_grad.astype(BF)
                term = dot(shares.astype(BF), grad_block)
                value_sum = term if value_sum is None else value_sum + term
                term = dot(score_grad, query_block)
                key_sum = term if key_sum is None else key_sum + term
                term = dot(score_grad, key_head, ROW_PAIRS)
                if j == 0 and head == 0:
                    query_grad[rows, :] = term
                else:
                    query_grad[rows, :] += term
            key_parts.append(key_sum)
            value_parts.append(value_sum)
        key_grad[cols, :] = (jnp.where(first, *key_parts) * HEAD ** (-0.5)).astype(BF)
        value_grad[cols, :] = jnp.where(first, *value_parts).astype(BF)
    query_sum = value_sum = jnp.zeros((1, LANES), F32)
    for slot in range(slots):
        at = pl.ds(place(me, slot, slots, part), part)
        piece = (query_grad[at, :] * HEAD ** (-0.5)).astype(BF)
        results[slot][:, :LANES] = piece
        results[slot][:, LANES : 2 * LANES] = key_grad[at, :]
        results[slot][:, 2 * LANES :] = value_grad[at, :]
        query_sum += jnp.sum(piece.astype(F32), axis=0, keepdims=True)
        value_sum += jnp.sum(value_grad[at, :].astype(F32), axis=0, keepdims=True)
    sums_ref[0, 0, 0:1, :] = query_sum
    sums_ref[0, 0, 1:2, :] = value_sum
    sums_ref[0, 0, 2:3, :] = scale_sum
    sums_ref[0, 0, 3:, :] = jnp.zeros((5, LANES), F32)


def sum_everywhere(value, axes):
    for name, size in axes:
        if size & (size - 1):
            value = lax.psum(value, name)
            continue
        step = 1
        while step < size:
            pairs = [(d, d ^ step) for d in range(size)]
            value = value + lax.ppermute(value, name, pairs)
            step *= 2
    return value


def attention_specs(slots, span, first_block, width):
    part = span // slots
    return pl.BlockSpec((part, width), lambda r, p, *_: (first_block + r, p))


def attend_forward(me, lengths, qkv, scale_lanes, kept, rows, span, first_block):
    slots = len(qkv)
    tokens = qkv[0].shape[0]
    pairs = qkv[0].shape[1] // (3 * LANES)
    block = min(512, span)
    call = pl.pallas_call(
        functools.partial(attend_forward_kernel, slots, span, block, len(kept)),
        grid_spec=pltpu.PrefetchScalarGridSpec(
            num_scalar_prefetch=2,
            grid=(rows, pairs),
            in_specs=[attention_specs(slots, span, first_block, 3 * LANES)] * slots
            + [pl.BlockSpec((1, LANES), lambda r, p, *_: (0, p))]
            + [pl.BlockSpec(memory_space=pl.ANY)] * len(kept),
            out_specs=[attention_specs(slots, span, first_block, LANES)] * slots
            + [pl.BlockSpec((1, 1, 2, span), lambda r, p, *_: (p, r, 0, 0))],
            scratch_shapes=[pltpu.VMEM((span, LANES), BF)] * 4,
        ),
        out_shape=[jax.ShapeDtypeStruct((tokens, pairs * LANES), BF)] * slots
        + [jax.ShapeDtypeStruct((pairs, rows, 2, span), F32)],
        input_output_aliases={3 + slots + k: k for k in range(len(kept))},
        compiler_params=pltpu.CompilerParams(vmem_limit_bytes=56 * 2**20),
        name="attend_forward",
    )
    *outs, log_total = call(me, lengths, *qkv, scale_lanes, *kept)
    return outs, log_total


def attend_backward(
    me, lengths, qkv, outs, grads, scale_lanes, log_total, kept, rows, span, first_block
):
    slots = len(qkv)
    tokens = qkv[0].shape[0]
    pairs = qkv[0].shape[1] // (3 * LANES)
    block = min(512, span)
    call = pl.pallas_call(
        functools.partial(attend_backward_kernel, slots, span, block, len(kept)),
        grid_spec=pltpu.PrefetchScalarGridSpec(
            num_scalar_prefetch=2,
            grid=(rows, pairs),
            in_specs=[attention_specs(slots, span, first_block, 3 * LANES)] * slots
            + [attention_specs(slots, span, first_block, LANES)] * (2 * slots)
            + [
                pl.BlockSpec((1, LANES), lambda r, p, *_: (0, p)),
                pl.BlockSpec((1, 1, 2, span), lambda r, p, *_: (p, r, 0, 0)),
            ]
            + [pl.BlockSpec(memory_space=pl.ANY)] * len(kept),
            out_specs=[attention_specs(slots, span, first_block, 3 * LANES)] * slots
            + [pl.BlockSpec((1, 1, 8, LANES), lambda r, p, *_: (r, p, 0, 0))],
            scratch_shapes=[pltpu.VMEM((span, LANES), BF)] * 4
            + [pltpu.VMEM((span, LANES), F32)] * 2
            + [pltpu.VMEM((span, LANES), BF)] * 2,
        ),
        out_shape=[jax.ShapeDtypeStruct((tokens, pairs * 3 * LANES), BF)] * slots
        + [jax.ShapeDtypeStruct((rows, pairs, 8, LANES), F32)],
        input_output_aliases={4 + 3 * slots + k: k for k in range(len(kept))},
        compiler_params=pltpu.CompilerParams(vmem_limit_bytes=56 * 2**20),
        name="attend_backward",
    )
    *results, sums = call(me, lengths, *qkv, *outs, *grads, scale_lanes, log_total, *kept)
    return results, sums


def fold(value):
    return functools.reduce(
        jnp.add, [value[:, k : k + LANES] for k in range(0, value.shape[1], LANES)]
    )


def row_sum(value):
    return jnp.sum(value, axis=-1, keepdims=True)


def column_sum(value):
    return jnp.sum(value, axis=0, keepdims=True)


def middle_kernel(slots, chunk, *refs):
    rows_ref, cot_ref = refs[:2]
    scaled = refs[2 : 2 + slots]
    out_weights = refs[2 + slots : 2 + 2 * slots]
    feed_ref, gains, shifts, mid_gain, mid_shifts = refs[2 + 2 * slots : 7 + 2 * slots]
    results = refs[7 + 2 * slots :]
    out_ref, residual_grad_ref, dense_ref, attended_grad_ref = results[:4]
    middle_ref, hidden_grad_ref, sums_ref, mid_sums_ref = results[4:8]
    scaled_grads = results[8 : 8 + slots]
    gelu_ref, slope_ref, grad_ref = results[8 + slots :]

    @pl.when(pl.program_id(0) == 0)
    def _():
        sums_ref[...] = jnp.zeros_like(sums_ref)
        mid_sums_ref[...] = jnp.zeros_like(mid_sums_ref)

    attended = shifts[3:4, :]
    for rows, matrix in zip(scaled, out_weights):
        attended = attended + dot(rows[...], matrix[...]).astype(BF).astype(F32)
    post, post_unit, post_inverse = normalize(attended, gains[1:2, :], shifts[1:2, :])
    residual = rows_ref[...].astype(F32) + post
    dense, dense_unit, dense_inverse = normalize(residual, gains[2:3, :], shifts[2:3, :])
    dense = dense.astype(BF)
    dense_ref[...] = dense
    cotangent = cot_ref[...]
    total = mid_gain.shape[1]

    def up(start):
        return feed_ref[2 * start : 2 * start + chunk, :]

    def down(start):
        return feed_ref[2 * start + chunk : 2 * start + 2 * chunk, :]

    base = first = second = third = fourth = None
    for start in range(0, total, chunk):
        cols = slice(start, start + chunk)
        hidden = dot(dense, up(start), COLUMN_PAIRS) + mid_shifts[0:1, cols]
        square = hidden * hidden
        bent = jnp.tanh(hidden * (GELU_SCALE + GELU_SCALE * GELU_CUBE * square))
        half = 0.5 * hidden
        active = half + half * bent
        slope = (0.5 + 0.5 * bent) + (half * (1.0 - bent * bent)) * (
            GELU_SCALE + 3.0 * GELU_SCALE * GELU_CUBE * square
        )
        grad = dot(cotangent, down(start), COLUMN_PAIRS)
        gelu_ref[:, cols] = active
        slope_ref[:, cols] = slope
        grad_ref[:, cols] = grad
        if base is None:
            base = row_sum(fold(active)) / chunk
        away = active - base
        weighted = grad * mid_gain[:, cols]
        terms = [fold(away), fold(away * away), fold(weighted), fold(weighted * away)]
        if first is None:
            first, second, third, fourth = terms
        else:
            first, second, third, fourth = [
                a + b for a, b in zip((first, second, third, fourth), terms)
            ]
    offset = row_sum(first) / total
    mean = base + offset
    inverse = lax.rsqrt(jnp.maximum(row_sum(second) / total - offset * offset, 0.0) + EPSILON)
    grad_mean = row_sum(third) / total
    grad_unit = inverse * (row_sum(fourth) / total - offset * grad_mean)
    branch = dense_grad = None
    for start in range(0, total, chunk):
        cols = slice(start, start + chunk)
        unit = (gelu_ref[:, cols] - mean) * inverse
        gain = mid_gain[:, cols]
        middle = (unit * gain + mid_shifts[1:2, cols]).astype(BF)
        middle_ref[:, cols] = middle
        term = dot(middle, down(start))
        branch = term if branch is None else branch + term
        grad = grad_ref[:, cols]
        inner = inverse * (grad * gain - grad_mean - unit * grad_unit)
        hidden_grad = (inner * slope_ref[:, cols]).astype(BF)
        hidden_grad_ref[:, cols] = hidden_grad
        mid_sums_ref[0:1, cols] += column_sum(grad * unit)
        mid_sums_ref[1:2, cols] += column_sum(grad)
        mid_sums_ref[2:3, cols] += column_sum(hidden_grad.astype(F32))
        term = dot(hidden_grad, up(start))
        dense_grad = term if dense_grad is None else dense_grad + term
    out_ref[...] = (residual + branch + shifts[4:5, :]).astype(BF)
    cot_wide = cotangent.astype(F32)

    def back(grad, unit, inverse, row):
        scaled = grad * gains[row : row + 1, :]
        inner = (
            scaled
            - jnp.mean(scaled, axis=-1, keepdims=True)
            - unit * jnp.mean(scaled * unit, axis=-1, keepdims=True)
        )
        sums_ref[row : row + 1, :] += column_sum(grad * unit)
        sums_ref[row + 2 : row + 3, :] += column_sum(grad)
        return inner * inverse

    residual_grad = cot_wide + back(dense_grad, dense_unit, dense_inverse, 2)
    residual_grad_ref[...] = residual_grad
    attended_grad = back(residual_grad, post_unit, post_inverse, 1)
    sums_ref[5:6, :] += column_sum(attended_grad)
    sums_ref[6:7, :] += column_sum(cot_wide)
    attended_grad = attended_grad.astype(BF)
    attended_grad_ref[...] = attended_grad
    for result, matrix in zip(scaled_grads, out_weights):
        result[...] = dot(attended_grad, matrix[...], COLUMN_PAIRS).astype(BF)


def middle_pass(
    chunk, rows, cotangent, scaled, out_weights, feed, gains, shifts, mid_gain, mid_shifts
):
    slots = len(scaled)
    tokens, width = rows.shape
    part = scaled[0].shape[1]
    hidden = mid_gain.shape[1]
    block = min(256, tokens)

    def tiles(columns):
        return pl.BlockSpec((block, columns), lambda i: (i, 0))

    def whole(array):
        return pl.BlockSpec(array.shape, lambda i: (0, 0), pipeline_mode=pl.Buffered(1))

    call = pl.pallas_call(
        functools.partial(middle_kernel, slots, chunk),
        grid=(tokens // block,),
        in_specs=[tiles(width), tiles(width)]
        + [tiles(part)] * slots
        + [whole(item) for item in (*out_weights, feed, gains, shifts, mid_gain, mid_shifts)],
        out_specs=[tiles(width)] * 4
        + [tiles(hidden)] * 2
        + [pl.BlockSpec((8, width), lambda i: (0, 0)), pl.BlockSpec((8, hidden), lambda i: (0, 0))]
        + [tiles(part)] * slots,
        out_shape=[
            jax.ShapeDtypeStruct((tokens, width), BF),
            jax.ShapeDtypeStruct((tokens, width), F32),
            jax.ShapeDtypeStruct((tokens, width), BF),
            jax.ShapeDtypeStruct((tokens, width), BF),
            jax.ShapeDtypeStruct((tokens, hidden), BF),
            jax.ShapeDtypeStruct((tokens, hidden), BF),
            jax.ShapeDtypeStruct((8, width), F32),
            jax.ShapeDtypeStruct((8, hidden), F32),
        ]
        + [jax.ShapeDtypeStruct((tokens, part), BF)] * slots,
        scratch_shapes=[pltpu.VMEM((block, hidden), F32)] * 3,
        compiler_params=pltpu.CompilerParams(vmem_limit_bytes=60 * 2**20),
        name="middle_pass",
    )
    return call(rows, cotangent, *scaled, *out_weights, feed, gains, shifts, mid_gain, mid_shifts)


def feed_grads_kernel(groups, *refs):
    middles, hidden_grads = refs[:groups], refs[groups : 2 * groups]
    cots, denses = refs[2 * groups : 3 * groups], refs[3 * groups : 4 * groups]
    result = refs[4 * groups]
    width = cots[0].shape[1]
    for at, lefts, rights in ((0, middles, cots), (width, hidden_grads, denses)):
        total = functools.reduce(
            jnp.add, [dot(a[...], b[...], ROW_PAIRS) for a, b in zip(lefts, rights)]
        )
        result[:, at : at + width] = total.astype(BF)


def feed_grads(middles, hidden_grads, cots, denses):
    groups = len(middles)
    hidden, width = middles[0].shape[1], cots[0].shape[1]
    block = min(256, hidden)

    def columns(array):
        return pl.BlockSpec((array.shape[0], block), lambda i: (0, i))

    def whole(array):
        return pl.BlockSpec(array.shape, lambda i: (0, 0), pipeline_mode=pl.Buffered(1))

    return pl.pallas_call(
        functools.partial(feed_grads_kernel, groups),
        grid=(hidden // block,),
        in_specs=[columns(item) for item in (*middles, *hidden_grads)]
        + [whole(item) for item in (*cots, *denses)],
        out_specs=pl.BlockSpec((block, 2 * width), lambda i: (i, 0)),
        out_shape=jax.ShapeDtypeStruct((hidden, 2 * width), BF),
        compiler_params=pltpu.CompilerParams(vmem_limit_bytes=56 * 2**20),
        name="feed_grads",
    )(*middles, *hidden_grads, *cots, *denses)


def shards(
    slots,
    short_rows,
    medium_rows,
    long_rows,
    short_len,
    medium_len,
    long_len,
    short_cotangent,
    medium_cotangent,
    long_cotangent,
    norm_gains,
    norm_shifts,
    head_weights,
    head_biases,
    head_scale,
    out_weight,
    up_weight,
    mid_gain,
    mid_shifts,
    down_weight,
):
    shapes = tuple((item.shape for item in (short_rows, medium_rows, long_rows)))
    width = short_rows.shape[2]
    part = head_weights.shape[2]
    pairs = part // LANES
    me = lax.axis_index("head").astype(jnp.int32).reshape(1)

    def fetch(value, slot):
        return lax.ppermute(value, "head", [((d + slot) % slots, d) for d in range(slots)])

    def deliver(value, slot):
        return lax.ppermute(value, "head", [(d, (d + slot) % slots) for d in range(slots)])

    def spread(own, move):
        return [own[slot] if slot == 0 else move(own[slot], slot) for slot in range(slots)]

    def grouped(short, medium, long):
        return [
            long.reshape(-1, width),
            jnp.concatenate([short.reshape(-1, width), medium.reshape(-1, width)], 0),
        ]

    inputs = grouped(short_rows, medium_rows, long_rows)
    cots = grouped(short_cotangent, medium_cotangent, long_cotangent)
    short_tokens = shapes[0][0] * shapes[0][1]
    spans = tuple(shape[1] * slots for shape in shapes)
    counts = tuple(shape[0] for shape in shapes)
    long_job = (long_len, counts[2], spans[2], 0)
    short_job = (short_len, counts[0], spans[0], 0)
    medium_job = (medium_len, counts[1], spans[1], short_tokens // shapes[1][1])
    jobs = ([long_job], [short_job, medium_job])

    weights = (
        head_weights.reshape(3, width, pairs, LANES).transpose(1, 2, 0, 3).reshape(width, 3 * part)
    )
    biases = (
        jnp.stack([head_biases[0], jnp.zeros_like(head_biases[0]), head_biases[1]])
        .reshape(3, pairs, LANES)
        .transpose(1, 0, 2)
        .reshape(3 * part)
    )
    scale_lanes = jnp.repeat(head_scale, HEAD).reshape(1, part)

    share = up_weight.shape[0]
    batches = mid_gain.shape[0] // (slots * share)
    own_feed = jnp.stack([up_weight, down_weight])
    feed_slots = [own_feed] + [fetch(own_feed, slot) for slot in range(1, slots)]
    feed = lax.all_gather(
        jnp.stack(feed_slots, 1).reshape(2 * slots * share, width), "batch", axis=0, tiled=True
    )

    def turn(values, places):
        return jnp.roll(values, places, axis=1)

    mid_rows = jnp.concatenate([mid_gain[None], mid_shifts], 0).reshape(3, slots, batches, share)
    mid_rows = turn(mid_rows, -me[0]).transpose(0, 2, 1, 3).reshape(3, -1)

    units, inverses, normed_slots = [], [], []
    for rows in inputs:
        value, unit, inverse = normalize(rows.astype(F32), norm_gains[0], norm_shifts[0])
        low = value.astype(BF)
        if normed_slots:
            low, normed_slots[-1] = lax.optimization_barrier((low, normed_slots[-1]))
        normed_slots.append([low] + [fetch(low, slot) for slot in range(1, slots)])
        units.append(unit)
        inverses.append(inverse)
    out_weights, _ = lax.optimization_barrier((out_weight, normed_slots[-1]))
    out_weights = [out_weight] + [deliver(out_weights, slot) for slot in range(1, slots)]

    qkv, saved, scaled = [], [], []
    for group in range(2):
        projected = [(dot(rows, weights) + biases).astype(BF) for rows in normed_slots[group]]
        qkv.append(projected)
        outs, totals = [], []
        for job in jobs[group]:
            outs, log_total = attend_forward(me, job[0], projected, scale_lanes, outs, *job[1:])
            totals.append(log_total)
        saved.append((outs, totals))
        scaled.append(spread(outs, deliver))

    outputs, residual_grads, grad_slots, sums, mid_sums, out_grads = [], [], [], [], [], []
    middles, hidden_grads, denses = [], [], []
    for group in range(2):
        results = middle_pass(
            slots * share,
            inputs[group],
            cots[group],
            scaled[group],
            out_weights,
            feed,
            norm_gains,
            norm_shifts,
            mid_rows[:1],
            mid_rows[1:],
        )
        outputs.append(results[0])
        residual_grads.append(results[1])
        denses.append(results[2])
        middles.append(results[4])
        hidden_grads.append(results[5])
        sums.append(results[6])
        mid_sums.append(results[7])
        grad_slots.append(spread(results[8:], fetch))
        terms = [dot(rows, results[3], ROW_PAIRS) for rows in scaled[group]]
        out_grads = terms if not out_grads else [a + b for a, b in zip(out_grads, terms)]
    both = feed_grads(middles, hidden_grads, cots, denses)
    out_grad = out_grads[0]
    for slot in range(1, slots):
        out_grad = out_grad + fetch(out_grads[slot].astype(BF), slot).astype(F32)
    grad_slots, both = lax.optimization_barrier((grad_slots, both))
    both = lax.psum_scatter(both, "batch", scatter_dimension=0, tiled=True)

    weight_grad = jnp.zeros((width, 3 * part), F32)
    bias_sums = jnp.zeros((8, part), F32)
    normed_grads = []
    for group in range(2):
        qkv_grad = []
        outs, totals = saved[group]
        for job, log_total in zip(jobs[group], totals):
            qkv_grad, back_sums = attend_backward(
                me,
                job[0],
                qkv[group],
                outs,
                grad_slots[group],
                scale_lanes,
                log_total,
                qkv_grad,
                *job[1:],
            )
            bias_sums = bias_sums + jnp.sum(back_sums, axis=0).transpose(1, 0, 2).reshape(8, part)
        terms = [dot(piece, weights, COLUMN_PAIRS).astype(BF) for piece in qkv_grad]
        terms = spread(terms, deliver)
        normed_grad = terms[0].astype(F32)
        for term in terms[1:]:
            normed_grad = normed_grad + term.astype(F32)
        normed_grads.append(normed_grad)
        for rows, piece in zip(normed_slots[group], qkv_grad):
            weight_grad = weight_grad + dot(rows, piece, ROW_PAIRS)

    weight_grad, out_grad = weight_grad.astype(BF), out_grad.astype(BF)
    weight_grad, out_grad, both = lax.optimization_barrier((weight_grad, out_grad, both))
    summed_weight, summed_out = lax.psum((weight_grad, out_grad), "batch")
    both = both.reshape(slots, share, 2 * width)
    both_grads = both[0].astype(F32)
    for slot in range(1, slots):
        both_grads = both_grads + deliver(both[slot], slot).astype(F32)
    grad_head_weights = (
        summed_weight.reshape(width, pairs, 3, LANES)
        .transpose(2, 0, 1, 3)
        .reshape(3, width, part)
        .astype(F32)
    )

    grads = []
    first_gain = first_shift = jnp.zeros((1, width), F32)
    for group in range(2):
        inner, gain_term, shift_term = normalize_back(
            normed_grads[group], units[group], inverses[group], norm_gains[0]
        )
        first_gain = first_gain + gain_term
        first_shift = first_shift + shift_term
        grads.append((residual_grads[group] + inner).astype(BF))
    sums = sums[0] + sums[1]
    mid_terms = (mid_sums[0] + mid_sums[1])[:3].reshape(3, batches, slots, share)
    mid_terms = turn(mid_terms.transpose(0, 2, 1, 3), me[0])
    shared = jnp.concatenate(
        [
            first_gain.reshape(-1),
            sums[1:3].reshape(-1),
            first_shift.reshape(-1),
            sums[3:7].reshape(-1),
            mid_terms.reshape(-1),
        ]
    )
    shared_size = shared.shape[0]
    own_sums = lax.dynamic_update_slice(
        jnp.zeros((slots, 3 * part), F32), bias_sums[:3].reshape(1, -1), (me[0], jnp.int32(0))
    )
    summed = sum_everywhere(
        jnp.concatenate([shared, own_sums.reshape(-1)]), (("head", slots), ("batch", batches))
    )
    norm_sums = summed[: 8 * width].reshape(8, width)
    mid_terms = summed[8 * width : shared_size].reshape(3, -1)
    own_sums = lax.dynamic_slice(
        summed[shared_size:].reshape(slots, 3 * part), (me[0], jnp.int32(0)), (1, 3 * part)
    ).reshape(3, part)
    return (
        outputs[1][:short_tokens].reshape(shapes[0]),
        outputs[1][short_tokens:].reshape(shapes[1]),
        outputs[0].reshape(shapes[2]),
        grads[1][:short_tokens].reshape(shapes[0]),
        grads[1][short_tokens:].reshape(shapes[1]),
        grads[0].reshape(shapes[2]),
        norm_sums[:3],
        norm_sums[3:],
        grad_head_weights,
        own_sums[:2],
        jnp.sum(own_sums[2].reshape(-1, HEAD), axis=1),
        summed_out.astype(F32),
        both_grads[:, width:],
        mid_terms[0],
        jnp.stack([mid_terms[2], mid_terms[1]]),
        both_grads[:, :width],
    )


def solution(mesh):
    in_specs = (
        P("batch", "head", None),
        P("batch", "head", None),
        P("batch", "head", None),
        P("batch"),
        P("batch"),
        P("batch"),
        P("batch", "head", None),
        P("batch", "head", None),
        P("batch", "head", None),
        P(),
        P(),
        P(None, None, "head"),
        P(None, "head"),
        P("head"),
        P("head", None),
        P(("head", "batch"), None),
        P(),
        P(),
        P(("head", "batch"), None),
    )
    out_specs = (
        P("batch", "head", None),
        P("batch", "head", None),
        P("batch", "head", None),
        P("batch", "head", None),
        P("batch", "head", None),
        P("batch", "head", None),
        P(),
        P(),
        P(None, None, "head"),
        P(None, "head"),
        P("head"),
        P("head", None),
        P(("head", "batch"), None),
        P(),
        P(),
        P(("head", "batch"), None),
    )
    return jax.shard_map(
        functools.partial(shards, mesh.shape["head"]),
        mesh=mesh,
        in_specs=in_specs,
        out_specs=out_specs,
        check_vma=False,
    )
```

```python
import functools

import jax
import jax.numpy as jnp
from jax import lax
from jax.experimental import pallas as pl
from jax.experimental.pallas import tpu as pltpu
from jax.sharding import PartitionSpec as P

EPSILON = 1e-05
ROW_PAIRS = (((0,), (0,)), ((), ()))
COLUMN_PAIRS = (((1,), (1,)), ((), ()))
LANES = 128
HEAD = 64
LOG2E = 1.4426950408889634
EXPONENT_SCALE = HEAD ** (-0.5) * LOG2E
MASKED = -1e30
GELU_SCALE = 0.7978845608028654
GELU_CUBE = 0.044715
BF = jnp.bfloat16
F32 = jnp.float32
MESH = pl.DeviceIdType.MESH


def dot(a, b, dims=(((1,), (0,)), ((), ()))):
    return lax.dot_general(a, b, dims, preferred_element_type=F32)


def normalize(value, gain, shift):
    centred = value - jnp.mean(value, axis=-1, keepdims=True)
    inverse = lax.rsqrt(jnp.mean(centred * centred, axis=-1, keepdims=True) + EPSILON)
    unit = centred * inverse
    return (unit * gain + shift, unit, inverse)


def normalize_back(grad, unit, inverse, gain):
    scaled = grad * gain
    inner = (
        scaled
        - jnp.mean(scaled, axis=-1, keepdims=True)
        - unit * jnp.mean(scaled * unit, axis=-1, keepdims=True)
    )
    return (inner * inverse, jnp.sum(grad * unit, axis=0), jnp.sum(grad, axis=0))


def place(me, slot, slots, part):
    return pl.multiple_of(lax.rem(me + slot, slots) * part, part)


def attend_forward_kernel(slots, span, block, kept, me_ref, len_ref, *refs):
    qkv = refs[:slots]
    scale_ref = refs[slots]
    refs = refs[kept:]
    outs = refs[slots + 1 : 2 * slots + 1]
    total_ref = refs[2 * slots + 1]
    query, keys, values, mixed = refs[2 * slots + 2 :]
    part = span // slots
    me = me_ref[0]
    length = len_ref[pl.program_id(0)]
    for slot in range(slots):
        at = pl.ds(place(me, slot, slots, part), part)
        query[at, :] = qkv[slot][:, :LANES]
        keys[at, :] = qkv[slot][:, LANES : 2 * LANES]
        values[at, :] = qkv[slot][:, 2 * LANES :]
    first = lax.broadcasted_iota(jnp.int32, (1, LANES), 1) < HEAD
    for i in range(span // block):
        rows = slice(i * block, (i + 1) * block)
        query_block = query[rows, :]
        halves = []
        for head in range(2):
            mine = first if head == 0 else jnp.logical_not(first)
            query_head = jnp.where(mine, query_block, jnp.zeros_like(query_block))
            scores = []
            for j in range(i + 1):
                key_block = keys[j * block : (j + 1) * block, :]
                score = dot(query_head, key_block, COLUMN_PAIRS)
                key_place = lax.broadcasted_iota(jnp.int32, (block, block), 1)
                allowed = None
                if i == j:
                    allowed = key_place <= lax.broadcasted_iota(jnp.int32, (block, block), 0)
                if (j + 1) * block > span // 2:
                    short = key_place < length - j * block
                    allowed = short if allowed is None else allowed & short
                if allowed is not None:
                    score = jnp.where(allowed, score, MASKED)
                scores.append(score)
            top = functools.reduce(jnp.maximum, scores)
            top = jnp.max(top, axis=-1, keepdims=True) * EXPONENT_SCALE
            weights = [jnp.exp2(score * EXPONENT_SCALE - top) for score in scores]
            total = jnp.sum(functools.reduce(jnp.add, weights), axis=-1, keepdims=True)
            result = None
            for j in range(i + 1):
                term = dot(weights[j].astype(BF), values[j * block : (j + 1) * block, :])
                result = term if result is None else result + term
            halves.append(result / total)
            log_total = jnp.broadcast_to(top + jnp.log2(total), (block, LANES))
            total_ref[0, 0, head : head + 1, rows] = jnp.transpose(log_total)[:1, :]
        mixed[rows, :] = (jnp.where(first, halves[0], halves[1]) * scale_ref[...]).astype(BF)
    for slot in range(slots):
        outs[slot][...] = mixed[pl.ds(place(me, slot, slots, part), part), :]


def attend_backward_kernel(slots, span, block, kept, me_ref, len_ref, *refs):
    qkv = refs[:slots]
    out = refs[slots : 2 * slots]
    grads = refs[2 * slots : 3 * slots]
    scale_ref, total_ref = refs[3 * slots : 3 * slots + 2]
    refs = refs[kept:]
    results = refs[3 * slots + 2 : 4 * slots + 2]
    sums_ref = refs[4 * slots + 2]
    query, keys, values, mixed_grad, product, query_grad, key_grad, value_grad = refs[4 * slots + 3 :]
    part = span // slots
    me = me_ref[0]
    length = len_ref[pl.program_id(0)]
    for slot in range(slots):
        at = pl.ds(place(me, slot, slots, part), part)
        query[at, :] = qkv[slot][:, :LANES]
        keys[at, :] = qkv[slot][:, LANES : 2 * LANES]
        values[at, :] = qkv[slot][:, 2 * LANES :]
        grad = grads[slot][...].astype(F32)
        mixed_grad[at, :] = (grad * scale_ref[...]).astype(BF)
        product[at, :] = grad * out[slot][...].astype(F32)
    first = lax.broadcasted_iota(jnp.int32, (1, LANES), 1) < HEAD
    which = lax.broadcasted_iota(jnp.int32, (8, LANES), 0)
    lane_head = lax.broadcasted_iota(jnp.int32, (8, LANES), 1) // HEAD
    picks = jnp.where(which == lane_head, 1.0, 0.0).astype(BF)
    inner = product[...]
    inner_high = inner.astype(BF)
    inner_low = (inner - inner_high.astype(F32)).astype(BF)
    inner_sum = dot(picks, inner_high, COLUMN_PAIRS) + dot(picks, inner_low, COLUMN_PAIRS)
    scale_sum = jnp.sum(inner, axis=0, keepdims=True) / scale_ref[...]
    count = span // block
    for j in range(count):
        cols = slice(j * block, (j + 1) * block)
        key_block, value_block = keys[cols, :], values[cols, :]
        key_parts, value_parts = [], []
        for head in range(2):
            mine = first if head == 0 else jnp.logical_not(first)
            key_head = jnp.where(mine, key_block, jnp.zeros_like(key_block))
            value_head = jnp.where(mine, value_block, jnp.zeros_like(value_block))
            key_sum = value_sum = None
            for i in range(j, count):
                rows = slice(i * block, (i + 1) * block)
                query_block, grad_block = query[rows, :], mixed_grad[rows, :]
                score = dot(key_head, query_block, COLUMN_PAIRS)
                shares = jnp.exp2(score * EXPONENT_SCALE - total_ref[0, 0, head : head + 1, rows])
                key_place = lax.broadcasted_iota(jnp.int32, (block, block), 0)
                allowed = None
                if i == j:
                    allowed = key_place <= lax.broadcasted_iota(jnp.int32, (block, block), 1)
                if (j + 1) * block > span // 2:
                    short = key_place < length - j * block
                    allowed = short if allowed is None else allowed & short
                if allowed is not None:
                    shares = jnp.where(allowed, shares, 0.0)
                share_grad = dot(value_head, grad_block, COLUMN_PAIRS)
                score_grad = shares * (share_grad - inner_sum[head : head + 1, rows])
                score_grad = score_grad.astype(BF)
                term = dot(shares.astype(BF), grad_block)
                value_sum = term if value_sum is None else value_sum + term
                term = dot(score_grad, query_block)
                key_sum = term if key_sum is None else key_sum + term
                term = dot(score_grad, key_head, ROW_PAIRS)
                if j == 0 and head == 0:
                    query_grad[rows, :] = term
                else:
                    query_grad[rows, :] += term
            key_parts.append(key_sum)
            value_parts.append(value_sum)
        key_grad[cols, :] = (jnp.where(first, *key_parts) * HEAD ** (-0.5)).astype(BF)
        value_grad[cols, :] = jnp.where(first, *value_parts).astype(BF)
    query_sum = value_sum = jnp.zeros((1, LANES), F32)
    for slot in range(slots):
        at = pl.ds(place(me, slot, slots, part), part)
        piece = (query_grad[at, :] * HEAD ** (-0.5)).astype(BF)
        results[slot][:, :LANES] = piece
        results[slot][:, LANES : 2 * LANES] = key_grad[at, :]
        results[slot][:, 2 * LANES :] = value_grad[at, :]
        query_sum += jnp.sum(piece.astype(F32), axis=0, keepdims=True)
        value_sum += jnp.sum(value_grad[at, :].astype(F32), axis=0, keepdims=True)
    sums_ref[0, 0, 0:1, :] = query_sum
    sums_ref[0, 0, 1:2, :] = value_sum
    sums_ref[0, 0, 2:3, :] = scale_sum
    sums_ref[0, 0, 3:, :] = jnp.zeros((5, LANES), F32)


def attention_specs(slots, span, first_block, width):
    part = span // slots
    return pl.BlockSpec((part, width), lambda r, p, *_: (first_block + r, p))


def attend_forward(me, lengths, qkv, scale_lanes, kept, rows, span, first_block):
    slots = len(qkv)
    tokens = qkv[0].shape[0]
    pairs = qkv[0].shape[1] // (3 * LANES)
    block = min(512, span)
    call = pl.pallas_call(
        functools.partial(attend_forward_kernel, slots, span, block, len(kept)),
        grid_spec=pltpu.PrefetchScalarGridSpec(
            num_scalar_prefetch=2,
            grid=(rows, pairs),
            in_specs=[attention_specs(slots, span, first_block, 3 * LANES)] * slots
            + [pl.BlockSpec((1, LANES), lambda r, p, *_: (0, p))]
            + [pl.BlockSpec(memory_space=pl.ANY)] * len(kept),
            out_specs=[attention_specs(slots, span, first_block, LANES)] * slots
            + [pl.BlockSpec((1, 1, 2, span), lambda r, p, *_: (p, r, 0, 0))],
            scratch_shapes=[pltpu.VMEM((span, LANES), BF)] * 4,
        ),
        out_shape=[jax.ShapeDtypeStruct((tokens, pairs * LANES), BF)] * slots
        + [jax.ShapeDtypeStruct((pairs, rows, 2, span), F32)],
        input_output_aliases={3 + slots + k: k for k in range(len(kept))},
        compiler_params=pltpu.CompilerParams(vmem_limit_bytes=56 * 2**20),
        name="attend_forward",
    )
    *outs, log_total = call(me, lengths, *qkv, scale_lanes, *kept)
    return outs, log_total


def attend_backward(
    me, lengths, qkv, outs, grads, scale_lanes, log_total, kept, rows, span, first_block
):
    slots = len(qkv)
    tokens = qkv[0].shape[0]
    pairs = qkv[0].shape[1] // (3 * LANES)
    block = min(512, span)
    call = pl.pallas_call(
        functools.partial(attend_backward_kernel, slots, span, block, len(kept)),
        grid_spec=pltpu.PrefetchScalarGridSpec(
            num_scalar_prefetch=2,
            grid=(rows, pairs),
            in_specs=[attention_specs(slots, span, first_block, 3 * LANES)] * slots
            + [attention_specs(slots, span, first_block, LANES)] * (2 * slots)
            + [
                pl.BlockSpec((1, LANES), lambda r, p, *_: (0, p)),
                pl.BlockSpec((1, 1, 2, span), lambda r, p, *_: (p, r, 0, 0)),
            ]
            + [pl.BlockSpec(memory_space=pl.ANY)] * len(kept),
            out_specs=[attention_specs(slots, span, first_block, 3 * LANES)] * slots
            + [pl.BlockSpec((1, 1, 8, LANES), lambda r, p, *_: (r, p, 0, 0))],
            scratch_shapes=[pltpu.VMEM((span, LANES), BF)] * 4
            + [pltpu.VMEM((span, LANES), F32)] * 2
            + [pltpu.VMEM((span, LANES), BF)] * 2,
        ),
        out_shape=[jax.ShapeDtypeStruct((tokens, pairs * 3 * LANES), BF)] * slots
        + [jax.ShapeDtypeStruct((rows, pairs, 8, LANES), F32)],
        input_output_aliases={4 + 3 * slots + k: k for k in range(len(kept))},
        compiler_params=pltpu.CompilerParams(vmem_limit_bytes=56 * 2**20),
        name="attend_backward",
    )
    *results, sums = call(me, lengths, *qkv, *outs, *grads, scale_lanes, log_total, *kept)
    return results, sums


def fold(value):
    return functools.reduce(
        jnp.add, [value[:, k : k + LANES] for k in range(0, value.shape[1], LANES)]
    )


def row_sum(value):
    return jnp.sum(value, axis=-1, keepdims=True)


def column_sum(value):
    return jnp.sum(value, axis=0, keepdims=True)


def middle_kernel(slots, chunk, *refs):
    rows_ref, cot_ref = refs[:2]
    scaled = refs[2 : 2 + slots]
    out_weights = refs[2 + slots : 2 + 2 * slots]
    feed_ref, gains, shifts, mid_gain, mid_shifts = refs[2 + 2 * slots : 7 + 2 * slots]
    results = refs[7 + 2 * slots :]
    out_ref, residual_grad_ref, dense_ref, attended_grad_ref = results[:4]
    middle_ref, hidden_grad_ref, sums_ref, mid_sums_ref = results[4:8]
    scaled_grads = results[8 : 8 + slots]
    gelu_ref, slope_ref, grad_ref = results[8 + slots :]

    @pl.when(pl.program_id(0) == 0)
    def _():
        sums_ref[...] = jnp.zeros_like(sums_ref)
        mid_sums_ref[...] = jnp.zeros_like(mid_sums_ref)

    attended = shifts[3:4, :]
    for rows, matrix in zip(scaled, out_weights):
        attended = attended + dot(rows[...], matrix[...]).astype(BF).astype(F32)
    post, post_unit, post_inverse = normalize(attended, gains[1:2, :], shifts[1:2, :])
    residual = rows_ref[...].astype(F32) + post
    dense, dense_unit, dense_inverse = normalize(residual, gains[2:3, :], shifts[2:3, :])
    dense = dense.astype(BF)
    dense_ref[...] = dense
    cotangent = cot_ref[...]
    total = mid_gain.shape[1]

    def up(start):
        return feed_ref[2 * start : 2 * start + chunk, :]

    def down(start):
        return feed_ref[2 * start + chunk : 2 * start + 2 * chunk, :]

    base = first = second = third = fourth = None
    for start in range(0, total, chunk):
        cols = slice(start, start + chunk)
        hidden = dot(dense, up(start), COLUMN_PAIRS) + mid_shifts[0:1, cols]
        square = hidden * hidden
        bent = jnp.tanh(hidden * (GELU_SCALE + GELU_SCALE * GELU_CUBE * square))
        half = 0.5 * hidden
        active = half + half * bent
        slope = (0.5 + 0.5 * bent) + (half * (1.0 - bent * bent)) * (
            GELU_SCALE + 3.0 * GELU_SCALE * GELU_CUBE * square
        )
        grad = dot(cotangent, down(start), COLUMN_PAIRS)
        gelu_ref[:, cols] = active
        slope_ref[:, cols] = slope
        grad_ref[:, cols] = grad
        if base is None:
            base = row_sum(fold(active)) / chunk
        away = active - base
        weighted = grad * mid_gain[:, cols]
        terms = [fold(away), fold(away * away), fold(weighted), fold(weighted * away)]
        if first is None:
            first, second, third, fourth = terms
        else:
            first, second, third, fourth = [
                a + b for a, b in zip((first, second, third, fourth), terms)
            ]
    offset = row_sum(first) / total
    mean = base + offset
    inverse = lax.rsqrt(jnp.maximum(row_sum(second) / total - offset * offset, 0.0) + EPSILON)
    grad_mean = row_sum(third) / total
    grad_unit = inverse * (row_sum(fourth) / total - offset * grad_mean)
    branch = dense_grad = None
    for start in range(0, total, chunk):
        cols = slice(start, start + chunk)
        unit = (gelu_ref[:, cols] - mean) * inverse
        gain = mid_gain[:, cols]
        middle = (unit * gain + mid_shifts[1:2, cols]).astype(BF)
        middle_ref[:, cols] = middle
        term = dot(middle, down(start))
        branch = term if branch is None else branch + term
        grad = grad_ref[:, cols]
        inner = inverse * (grad * gain - grad_mean - unit * grad_unit)
        hidden_grad = (inner * slope_ref[:, cols]).astype(BF)
        hidden_grad_ref[:, cols] = hidden_grad
        mid_sums_ref[0:1, cols] += column_sum(grad * unit)
        mid_sums_ref[1:2, cols] += column_sum(grad)
        mid_sums_ref[2:3, cols] += column_sum(hidden_grad.astype(F32))
        term = dot(hidden_grad, up(start))
        dense_grad = term if dense_grad is None else dense_grad + term
    out_ref[...] = (residual + branch + shifts[4:5, :]).astype(BF)
    cot_wide = cotangent.astype(F32)

    def back(grad, unit, inverse, row):
        scaled = grad * gains[row : row + 1, :]
        inner = (
            scaled
            - jnp.mean(scaled, axis=-1, keepdims=True)
            - unit * jnp.mean(scaled * unit, axis=-1, keepdims=True)
        )
        sums_ref[row : row + 1, :] += column_sum(grad * unit)
        sums_ref[row + 2 : row + 3, :] += column_sum(grad)
        return inner * inverse

    residual_grad = cot_wide + back(dense_grad, dense_unit, dense_inverse, 2)
    residual_grad_ref[...] = residual_grad
    attended_grad = back(residual_grad, post_unit, post_inverse, 1)
    sums_ref[5:6, :] += column_sum(attended_grad)
    sums_ref[6:7, :] += column_sum(cot_wide)
    attended_grad = attended_grad.astype(BF)
    attended_grad_ref[...] = attended_grad
    for result, matrix in zip(scaled_grads, out_weights):
        result[...] = dot(attended_grad, matrix[...], COLUMN_PAIRS).astype(BF)


def middle_pass(
    chunk, rows, cotangent, scaled, out_weights, feed, gains, shifts, mid_gain, mid_shifts
):
    slots = len(scaled)
    tokens, width = rows.shape
    part = scaled[0].shape[1]
    hidden = mid_gain.shape[1]
    block = min(256, tokens)

    def tiles(columns):
        return pl.BlockSpec((block, columns), lambda i: (i, 0))

    def whole(array):
        return pl.BlockSpec(array.shape, lambda i: (0, 0), pipeline_mode=pl.Buffered(1))

    call = pl.pallas_call(
        functools.partial(middle_kernel, slots, chunk),
        grid=(tokens // block,),
        in_specs=[tiles(width), tiles(width)]
        + [tiles(part)] * slots
        + [whole(item) for item in (*out_weights, feed, gains, shifts, mid_gain, mid_shifts)],
        out_specs=[tiles(width)] * 4
        + [tiles(hidden)] * 2
        + [pl.BlockSpec((8, width), lambda i: (0, 0)), pl.BlockSpec((8, hidden), lambda i: (0, 0))]
        + [tiles(part)] * slots,
        out_shape=[
            jax.ShapeDtypeStruct((tokens, width), BF),
            jax.ShapeDtypeStruct((tokens, width), F32),
            jax.ShapeDtypeStruct((tokens, width), BF),
            jax.ShapeDtypeStruct((tokens, width), BF),
            jax.ShapeDtypeStruct((tokens, hidden), BF),
            jax.ShapeDtypeStruct((tokens, hidden), BF),
            jax.ShapeDtypeStruct((8, width), F32),
            jax.ShapeDtypeStruct((8, hidden), F32),
        ]
        + [jax.ShapeDtypeStruct((tokens, part), BF)] * slots,
        scratch_shapes=[pltpu.VMEM((block, hidden), F32)] * 3,
        compiler_params=pltpu.CompilerParams(vmem_limit_bytes=60 * 2**20),
        name="middle_pass",
    )
    return call(rows, cotangent, *scaled, *out_weights, feed, gains, shifts, mid_gain, mid_shifts)


def feed_grads_kernel(groups, *refs):
    middles, hidden_grads = refs[:groups], refs[groups : 2 * groups]
    cots, denses = refs[2 * groups : 3 * groups], refs[3 * groups : 4 * groups]
    result = refs[4 * groups]
    width = cots[0].shape[1]
    for at, lefts, rights in ((0, middles, cots), (width, hidden_grads, denses)):
        total = functools.reduce(
            jnp.add, [dot(a[...], b[...], ROW_PAIRS) for a, b in zip(lefts, rights)]
        )
        result[:, at : at + width] = total.astype(BF)


def feed_grads(middles, hidden_grads, cots, denses):
    groups = len(middles)
    hidden, width = middles[0].shape[1], cots[0].shape[1]
    block = min(256, hidden)

    def columns(array):
        return pl.BlockSpec((array.shape[0], block), lambda i: (0, i))

    def whole(array):
        return pl.BlockSpec(array.shape, lambda i: (0, 0), pipeline_mode=pl.Buffered(1))

    return pl.pallas_call(
        functools.partial(feed_grads_kernel, groups),
        grid=(hidden // block,),
        in_specs=[columns(item) for item in (*middles, *hidden_grads)]
        + [whole(item) for item in (*cots, *denses)],
        out_specs=pl.BlockSpec((block, 2 * width), lambda i: (i, 0)),
        out_shape=jax.ShapeDtypeStruct((hidden, 2 * width), BF),
        compiler_params=pltpu.CompilerParams(vmem_limit_bytes=56 * 2**20),
        name="feed_grads",
    )(*middles, *hidden_grads, *cots, *denses)


def head_grads_kernel(count, *refs):
    rows, grads = refs[:count], refs[count : 2 * count]
    out_grad, result, total = refs[2 * count :]

    @pl.when(pl.program_id(0) == 0)
    def _():
        total[...] = jnp.zeros_like(total)

    wide = 2 * LANES
    for at in range(0, total.shape[1], wide):
        cols = slice(at, at + wide)
        total[:, cols] += functools.reduce(
            jnp.add,
            [dot(left[...], right[:, cols], ROW_PAIRS) for left, right in zip(rows, grads)],
        )

    @pl.when(pl.program_id(0) == pl.num_programs(0) - 1)
    def _():
        for at in range(0, total.shape[1], LANES):
            pair, kind = divmod(at // LANES, 3)
            result[kind, :, pair * LANES : (pair + 1) * LANES] = total[:, at : at + LANES].astype(BF)
        part, width = out_grad.shape
        for at in range(0, width, part):
            result[3, at : at + part, :] = out_grad[:, at : at + part].astype(BF)


def head_grads(rows, grads, out_grad):
    tokens, width = rows[0].shape
    columns = grads[0].shape[1]
    block = min(512, tokens)
    return pl.pallas_call(
        functools.partial(head_grads_kernel, len(rows)),
        grid=(tokens // block,),
        in_specs=[pl.BlockSpec((block, width), lambda i: (i, 0))] * len(rows)
        + [pl.BlockSpec((block, columns), lambda i: (i, 0))] * len(grads)
        + [pl.BlockSpec(out_grad.shape, lambda i: (0, 0))],
        out_specs=pl.BlockSpec((4, width, columns // 3), lambda i: (0, 0, 0)),
        out_shape=jax.ShapeDtypeStruct((4, width, columns // 3), BF),
        scratch_shapes=[pltpu.VMEM((width, columns), F32)],
        compiler_params=pltpu.CompilerParams(vmem_limit_bytes=56 * 2**20),
        name="head_grads",
    )(*rows, *grads, out_grad)


def partner(name, bit):
    me = lax.axis_index(name)
    mine = lax.rem(me // (1 << bit), 2)
    return mine, {name: me + (1 - 2 * mine) * (1 << bit)}


def greet(places):
    barrier = pltpu.get_barrier_semaphore()
    for place_of in places:
        pl.semaphore_signal(barrier, inc=1, device_id=place_of, device_id_type=MESH)
    pl.semaphore_wait(barrier, len(places))


def batch_sum_kernel(bits, chunks, steps, source, extra, result, extra_result, *refs):
    levels, arrivals = refs[:bits], refs[bits : 2 * bits]
    extra_totals, extra_arrivals = refs[2 * bits : 2 * bits + 2]
    send_sems, recv_sems, extra_send_sems, extra_recv_sems = refs[2 * bits + 2 :]
    rows = source.shape[0] // chunks
    partners = [partner("batch", bit) for bit in range(bits)]
    extra_partners = [partner(name, bit)[1] for name, bit in steps]
    greet(extra_partners)
    offsets, offset = [], 0
    for bit in range(bits):
        offset = offset + partners[bit][0] * (rows >> (bit + 1))
        offsets.append(offset)

    def aligned(value, size):
        return pl.ds(pl.multiple_of(value, size), size)

    def piece(chunk, bit, mine):
        size = rows >> (bit + 1)
        if bit == 0:
            return source.at[aligned(chunk * rows + mine * size, size), :]
        return levels[bit - 1].at[chunk, aligned(mine * size, size), :]

    def final(chunk, bit):
        return result.at[aligned(chunk * rows + offsets[bit], rows >> (bit + 1)), :]

    copies = {}

    def start(chunk, stage):
        if stage < bits:
            mine, other = partners[stage]
            here, there = piece(chunk, stage, 1 - mine), arrivals[stage].at[chunk]
        else:
            bit = 2 * bits - 1 - stage
            other = partners[bit][1]
            here = there = final(chunk, bit)
        copies[chunk, stage] = pltpu.make_async_remote_copy(
            src_ref=here,
            dst_ref=there,
            send_sem=send_sems.at[chunk, stage],
            recv_sem=recv_sems.at[chunk, stage],
            device_id=other,
            device_id_type=MESH,
        )
        copies[chunk, stage].start()

    def finish(chunk, stage):
        copies[chunk, stage].wait_recv()
        if stage < bits:
            kept = piece(chunk, stage, partners[stage][0])[...].astype(F32)
            total = (kept + arrivals[stage][chunk].astype(F32)).astype(BF)
            if stage == bits - 1:
                final(chunk, stage)[...] = total
            else:
                levels[stage][chunk] = total

    def extra_total(step):
        if step == 0:
            return extra
        return extra_result if step == len(steps) else extra_totals.at[step - 1]

    def extra_copy(step):
        return pltpu.make_async_remote_copy(
            src_ref=extra_total(step),
            dst_ref=extra_arrivals.at[step],
            send_sem=extra_send_sems.at[step],
            recv_sem=extra_recv_sems.at[step],
            device_id=extra_partners[step],
            device_id_type=MESH,
        )

    extra_copies = []
    for tick in range(max(chunks + 2 * bits, len(steps) + 1)):
        if 0 < tick <= len(steps):
            extra_copies[tick - 1].wait_recv()
            extra_total(tick)[...] = extra_total(tick - 1)[...] + extra_arrivals[tick - 1]
        if tick < len(steps):
            extra_copies.append(extra_copy(tick))
            extra_copies[tick].start()
        for chunk in range(chunks):
            stage = tick - chunk
            if 0 < stage <= 2 * bits:
                finish(chunk, stage - 1)
            if 0 <= stage < 2 * bits:
                start(chunk, stage)
    for copy in (*copies.values(), *extra_copies):
        copy.wait_send()


def halving_steps(axes):
    return [(name, bit) for name, size in axes for bit in range(size.bit_length() - 1)]


def batch_sum(value, extra, axes):
    bits = axes[0][1].bit_length() - 1
    if bits == 0 or any(size & (size - 1) for _, size in axes):
        return lax.psum(value, "batch"), lax.psum(extra, tuple(name for name, _ in axes))
    steps = halving_steps(axes)
    rows, columns = value.shape
    chunks = 4
    halves = [
        pltpu.VMEM((chunks, rows // chunks >> (bit + 1), columns), BF) for bit in range(bits)
    ]
    return pl.pallas_call(
        functools.partial(batch_sum_kernel, bits, chunks, steps),
        in_specs=[pl.BlockSpec(memory_space=pltpu.VMEM)] * 2,
        out_specs=[pl.BlockSpec(memory_space=pltpu.VMEM)] * 2,
        out_shape=[
            jax.ShapeDtypeStruct(value.shape, BF),
            jax.ShapeDtypeStruct(extra.shape, F32),
        ],
        scratch_shapes=halves * 2
        + [pltpu.VMEM((len(steps), *extra.shape), F32)] * 2
        + [pltpu.SemaphoreType.DMA((chunks, 2 * bits))] * 2
        + [pltpu.SemaphoreType.DMA((len(steps),))] * 2,
        compiler_params=pltpu.CompilerParams(
            collective_id=0, has_side_effects=True, vmem_limit_bytes=40 * 2**20
        ),
        name="batch_sum",
    )(value, extra)


def small_sum_kernel(steps, source, result, *refs):
    totals, arrivals = refs[:-2][: len(steps) - 1], refs[:-2][len(steps) - 1 :]
    send_sems, recv_sems = refs[-2:]
    partners = [partner(name, bit)[1] for name, bit in steps]
    greet(partners)
    here = source
    copies = []
    for step, other in enumerate(partners):
        copy = pltpu.make_async_remote_copy(
            src_ref=here,
            dst_ref=arrivals[step],
            send_sem=send_sems.at[step],
            recv_sem=recv_sems.at[step],
            device_id=other,
            device_id_type=MESH,
        )
        copy.start()
        copies.append(copy)
        copy.wait_recv()
        there = result if step == len(partners) - 1 else totals[step]
        there[...] = here[...] + arrivals[step][...]
        here = there
    for copy in copies:
        copy.wait_send()


def small_sum(value, axes):
    steps = halving_steps(axes)
    if not steps or any(size & (size - 1) for _, size in axes):
        return lax.psum(value, tuple(name for name, _ in axes))
    return pl.pallas_call(
        functools.partial(small_sum_kernel, steps),
        in_specs=[pl.BlockSpec(memory_space=pltpu.VMEM)],
        out_specs=pl.BlockSpec(memory_space=pltpu.VMEM),
        out_shape=jax.ShapeDtypeStruct(value.shape, F32),
        scratch_shapes=[pltpu.VMEM(value.shape, F32)] * (2 * len(steps) - 1)
        + [pltpu.SemaphoreType.DMA((len(steps),))] * 2,
        compiler_params=pltpu.CompilerParams(
            collective_id=1, has_side_effects=True, vmem_limit_bytes=40 * 2**20
        ),
        name="small_sum",
    )(value)


def first_back_kernel(count, rows_ref, grad_ref, weights, gains, shifts, residual_ref, *refs):
    arrived = refs[:count]
    result, sums_ref = refs[count:]

    @pl.when(pl.program_id(0) == 0)
    def _():
        sums_ref[...] = jnp.zeros_like(sums_ref)

    grad = dot(grad_ref[...], weights[...], COLUMN_PAIRS).astype(BF).astype(F32)
    for term in arrived:
        grad = grad + term[...].astype(F32)
    gain = gains[0:1, :]
    _, unit, inverse = normalize(rows_ref[...].astype(F32), gain, shifts[0:1, :])
    scaled = grad * gain
    inner = (
        scaled
        - jnp.mean(scaled, axis=-1, keepdims=True)
        - unit * jnp.mean(scaled * unit, axis=-1, keepdims=True)
    )
    sums_ref[0:1, :] += column_sum(grad * unit)
    sums_ref[1:2, :] += column_sum(grad)
    result[...] = (residual_ref[...] + inner * inverse).astype(BF)


def first_back(rows, qkv_grad, weights, gains, shifts, residual_grad, arrived):
    tokens, width = rows.shape
    block = min(256, tokens)

    def tiles(columns):
        return pl.BlockSpec((block, columns), lambda i: (i, 0))

    def whole(array):
        return pl.BlockSpec(array.shape, lambda i: (0, 0), pipeline_mode=pl.Buffered(1))

    return pl.pallas_call(
        functools.partial(first_back_kernel, len(arrived)),
        grid=(tokens // block,),
        in_specs=[
            tiles(width),
            tiles(qkv_grad.shape[1]),
            whole(weights),
            whole(gains),
            whole(shifts),
            tiles(width),
        ]
        + [tiles(width)] * len(arrived),
        out_specs=[tiles(width), pl.BlockSpec((8, width), lambda i: (0, 0))],
        out_shape=[
            jax.ShapeDtypeStruct((tokens, width), BF),
            jax.ShapeDtypeStruct((8, width), F32),
        ],
        compiler_params=pltpu.CompilerParams(vmem_limit_bytes=40 * 2**20),
        name="first_back",
    )(rows, qkv_grad, weights, gains, shifts, residual_grad, *arrived)


def project_kernel(rows_ref, weights, biases, result):
    rows = rows_ref[...]
    for kind in range(3):
        value = (dot(rows, weights[kind]) + biases[kind : kind + 1, :]).astype(BF)
        for pair in range(value.shape[1] // LANES):
            at = (3 * pair + kind) * LANES
            result[:, at : at + LANES] = value[:, pair * LANES : (pair + 1) * LANES]


def project(rows, weights, biases):
    tokens, width = rows.shape
    columns = 3 * weights.shape[2]
    block = min(256, tokens)
    return pl.pallas_call(
        project_kernel,
        grid=(tokens // block,),
        in_specs=[
            pl.BlockSpec((block, width), lambda i: (i, 0)),
            pl.BlockSpec(weights.shape, lambda i: (0, 0, 0), pipeline_mode=pl.Buffered(1)),
            pl.BlockSpec(biases.shape, lambda i: (0, 0), pipeline_mode=pl.Buffered(1)),
        ],
        out_specs=pl.BlockSpec((block, columns), lambda i: (i, 0)),
        out_shape=jax.ShapeDtypeStruct((tokens, columns), BF),
        compiler_params=pltpu.CompilerParams(vmem_limit_bytes=40 * 2**20),
        name="project",
    )(rows, weights, biases)


def shards(
    slots,
    short_rows,
    medium_rows,
    long_rows,
    short_len,
    medium_len,
    long_len,
    short_cotangent,
    medium_cotangent,
    long_cotangent,
    norm_gains,
    norm_shifts,
    head_weights,
    head_biases,
    head_scale,
    out_weight,
    up_weight,
    mid_gain,
    mid_shifts,
    down_weight,
):
    shapes = tuple((item.shape for item in (short_rows, medium_rows, long_rows)))
    width = short_rows.shape[2]
    part = head_weights.shape[2]
    pairs = part // LANES
    me = lax.axis_index("head").astype(jnp.int32).reshape(1)

    def fetch(value, slot):
        return lax.ppermute(value, "head", [((d + slot) % slots, d) for d in range(slots)])

    def deliver(value, slot):
        return lax.ppermute(value, "head", [(d, (d + slot) % slots) for d in range(slots)])

    def spread(own, move):
        return [own[slot] if slot == 0 else move(own[slot], slot) for slot in range(slots)]

    def grouped(short, medium, long):
        return [
            long.reshape(-1, width),
            jnp.concatenate([short.reshape(-1, width), medium.reshape(-1, width)], 0),
        ]

    inputs = grouped(short_rows, medium_rows, long_rows)
    cots = grouped(short_cotangent, medium_cotangent, long_cotangent)
    short_tokens = shapes[0][0] * shapes[0][1]
    spans = tuple(shape[1] * slots for shape in shapes)
    counts = tuple(shape[0] for shape in shapes)
    long_job = (long_len, counts[2], spans[2], 0)
    short_job = (short_len, counts[0], spans[0], 0)
    medium_job = (medium_len, counts[1], spans[1], short_tokens // shapes[1][1])
    jobs = ([long_job], [short_job, medium_job])

    weights = (
        head_weights.reshape(3, width, pairs, LANES).transpose(1, 2, 0, 3).reshape(width, 3 * part)
    )
    biases = jnp.stack([head_biases[0], jnp.zeros_like(head_biases[0]), head_biases[1]])
    scale_lanes = jnp.repeat(head_scale, HEAD).reshape(1, part)

    share = up_weight.shape[0]
    batches = mid_gain.shape[0] // (slots * share)
    own_feed = jnp.stack([up_weight, down_weight])
    feed_slots = [own_feed] + [fetch(own_feed, slot) for slot in range(1, slots)]
    feed = jnp.stack(feed_slots, 1).reshape(2 * slots * share, width)

    def turn(values, places):
        return jnp.roll(values, places, axis=1)

    mid_rows = jnp.concatenate([mid_gain[None], mid_shifts], 0).reshape(3, slots, batches, share)
    mid_rows = turn(mid_rows, -me[0]).transpose(0, 2, 1, 3).reshape(3, -1)

    lows = []
    for rows in inputs:
        value, _, _ = normalize(rows.astype(F32), norm_gains[0], norm_shifts[0])
        lows.append(value.astype(BF))
    lows[0], feed = lax.optimization_barrier((lows[0], feed))
    feed = lax.all_gather(feed, "batch", axis=0, tiled=True)
    own_qkv = [project(rows, head_weights, biases) for rows in lows]
    arrived = [fetch(lows[0], slot) for slot in range(1, slots)]
    own_qkv, arrived, lows[1], weights = lax.optimization_barrier(
        (own_qkv, arrived, lows[1], weights)
    )
    normed_slots = [
        [lows[0], *arrived],
        [lows[1]] + [fetch(lows[1], slot) for slot in range(1, slots)],
    ]
    out_weights, _ = lax.optimization_barrier((out_weight, normed_slots[-1][1:]))
    out_weights = [out_weight] + [deliver(out_weights, slot) for slot in range(1, slots)]

    qkv, saved, scaled = [], [], []
    for group in range(2):
        projected = [own_qkv[group]]
        projected += [project(rows, head_weights, biases) for rows in normed_slots[group][1:]]
        qkv.append(projected)
        outs, totals = [], []
        for job in jobs[group]:
            outs, log_total = attend_forward(me, job[0], projected, scale_lanes, outs, *job[1:])
            totals.append(log_total)
        saved.append((outs, totals))
        scaled.append(spread(outs, deliver))

    outputs, residual_grads, grad_slots, sums, mid_sums, out_grads = [], [], [], [], [], []
    middles, hidden_grads, denses = [], [], []
    for group in range(2):
        results = middle_pass(
            slots * share,
            inputs[group],
            cots[group],
            scaled[group],
            out_weights,
            feed,
            norm_gains,
            norm_shifts,
            mid_rows[:1],
            mid_rows[1:],
        )
        outputs.append(results[0])
        residual_grads.append(results[1])
        denses.append(results[2])
        middles.append(results[4])
        hidden_grads.append(results[5])
        sums.append(results[6])
        mid_sums.append(results[7])
        grad_slots.append(spread(results[8:], fetch))
        terms = [dot(rows, results[3], ROW_PAIRS) for rows in scaled[group]]
        out_grads = terms if not out_grads else [a + b for a, b in zip(out_grads, terms)]
    both = feed_grads(middles, hidden_grads, cots, denses)
    out_grad = out_grads[0]
    for slot in range(1, slots):
        out_grad = out_grad + fetch(out_grads[slot].astype(BF), slot).astype(F32)
    grad_slots, both = lax.optimization_barrier((grad_slots, both))
    both = lax.psum_scatter(both, "batch", scatter_dimension=0, tiled=True)

    bias_sums = jnp.zeros((8, part), F32)
    grads, first_sums, qkv_grads = [], [], []

    def send_back(qkv_grad):
        return [
            deliver(dot(qkv_grad[slot], weights, COLUMN_PAIRS).astype(BF), slot)
            for slot in range(1, slots)
        ]

    def finish_back(group, arrived):
        grad, group_sums = first_back(
            inputs[group],
            qkv_grads[group][0],
            weights,
            norm_gains,
            norm_shifts,
            residual_grads[group],
            arrived,
        )
        grads.append(grad)
        first_sums.append(group_sums)

    for group in range(2):
        if group == 1:
            grad_slots[1], qkv_grads[0] = lax.optimization_barrier((grad_slots[1], qkv_grads[0]))
        qkv_grad = []
        outs, totals = saved[group]
        for job, log_total in zip(jobs[group], totals):
            qkv_grad, back_sums = attend_backward(
                me,
                job[0],
                qkv[group],
                outs,
                grad_slots[group],
                scale_lanes,
                log_total,
                qkv_grad,
                *job[1:],
            )
            bias_sums = bias_sums + jnp.sum(back_sums, axis=0).transpose(1, 0, 2).reshape(8, part)
        qkv_grads.append(qkv_grad)
        if group == 0:
            arrived = send_back(qkv_grad)
    weight_grad = head_grads(
        [rows for group in normed_slots for rows in group],
        [piece for group in qkv_grads for piece in group],
        out_grad,
    )
    qkv_grads[1], weight_grad = lax.optimization_barrier((qkv_grads[1], weight_grad))
    arrived_last = send_back(qkv_grads[1])
    finish_back(0, arrived)
    mid_terms = (mid_sums[0] + mid_sums[1])[:3].reshape(3, batches, slots, share)
    mid_terms = turn(mid_terms.transpose(0, 2, 1, 3), me[0])
    norm_sums = sums[0] + sums[1]
    own_sums = lax.dynamic_update_slice(
        jnp.zeros((slots, 3 * part), F32), bias_sums[:3].reshape(1, -1), (me[0], jnp.int32(0))
    )
    shared = jnp.concatenate(
        [norm_sums[1:7].reshape(-1), mid_terms.reshape(-1), own_sums.reshape(-1)]
    ).reshape(-1, LANES)
    axes = (("batch", batches), ("head", slots))
    weight_grad, shared, grads[0] = lax.optimization_barrier((weight_grad, shared, grads[0]))
    summed_weight, summed = batch_sum(weight_grad.reshape(4 * width, part), shared, axes)
    arrived_last, summed_weight, both = lax.optimization_barrier(
        (arrived_last, summed_weight, both)
    )
    summed_weight = summed_weight.reshape(4, width, part)
    both = both.reshape(slots, share, 2 * width)
    both_grads = both[0].astype(F32)
    for slot in range(1, slots):
        both_grads = both_grads + deliver(both[slot], slot).astype(F32)
    finish_back(1, arrived_last)
    late = first_sums[0] + first_sums[1]
    late, both_grads = lax.optimization_barrier((late, both_grads))
    late = small_sum(late[:2].reshape(-1, LANES), axes).reshape(2, width)
    summed = summed.reshape(-1)
    norm_sums, mid_terms, own_sums = jnp.split(
        summed, [6 * width, 6 * width + 3 * mid_gain.shape[0]]
    )
    norm_sums = norm_sums.reshape(6, width)
    mid_terms = mid_terms.reshape(3, -1)
    own_sums = lax.dynamic_slice(
        own_sums.reshape(slots, 3 * part), (me[0], jnp.int32(0)), (1, 3 * part)
    ).reshape(3, part)
    return (
        outputs[1][:short_tokens].reshape(shapes[0]),
        outputs[1][short_tokens:].reshape(shapes[1]),
        outputs[0].reshape(shapes[2]),
        grads[1][:short_tokens].reshape(shapes[0]),
        grads[1][short_tokens:].reshape(shapes[1]),
        grads[0].reshape(shapes[2]),
        jnp.concatenate([late[:1], norm_sums[:2]], 0),
        jnp.concatenate([late[1:], norm_sums[2:]], 0),
        summed_weight[:3].astype(F32),
        own_sums[:2],
        jnp.sum(own_sums[2].reshape(-1, HEAD), axis=1),
        jnp.concatenate(
            [summed_weight[3, at : at + part] for at in range(0, width, part)], 1
        ).astype(F32),
        both_grads[:, width:],
        mid_terms[0],
        jnp.stack([mid_terms[2], mid_terms[1]]),
        both_grads[:, :width],
    )


def solution(mesh):
    in_specs = (
        P("batch", "head", None),
        P("batch", "head", None),
        P("batch", "head", None),
        P("batch"),
        P("batch"),
        P("batch"),
        P("batch", "head", None),
        P("batch", "head", None),
        P("batch", "head", None),
        P(),
        P(),
        P(None, None, "head"),
        P(None, "head"),
        P("head"),
        P("head", None),
        P(("head", "batch"), None),
        P(),
        P(),
        P(("head", "batch"), None),
    )
    out_specs = (
        P("batch", "head", None),
        P("batch", "head", None),
        P("batch", "head", None),
        P("batch", "head", None),
        P("batch", "head", None),
        P("batch", "head", None),
        P(),
        P(),
        P(None, None, "head"),
        P(None, "head"),
        P("head"),
        P("head", None),
        P(("head", "batch"), None),
        P(),
        P(),
        P(("head", "batch"), None),
    )
    return jax.shard_map(
        functools.partial(shards, mesh.shape["head"]),
        mesh=mesh,
        in_specs=in_specs,
        out_specs=out_specs,
        check_vma=False,
    )
```

```python
import functools

import jax
import jax.numpy as jnp
from jax import lax
from jax.experimental import pallas as pl
from jax.experimental.pallas import tpu as pltpu
from jax.sharding import PartitionSpec as P

EPSILON = 1e-05
ROW_PAIRS = (((0,), (0,)), ((), ()))
COLUMN_PAIRS = (((1,), (1,)), ((), ()))
LANES = 128
HEAD = 64
LOG2E = 1.4426950408889634
EXPONENT_SCALE = HEAD ** (-0.5) * LOG2E
MASKED = -1e30
GELU_SCALE = 0.7978845608028654
GELU_CUBE = 0.044715
BF = jnp.bfloat16
F32 = jnp.float32
MESH = pl.DeviceIdType.MESH


def dot(a, b, dims=(((1,), (0,)), ((), ()))):
    return lax.dot_general(a, b, dims, preferred_element_type=F32)


def normalize(value, gain, shift):
    centred = value - jnp.mean(value, axis=-1, keepdims=True)
    inverse = lax.rsqrt(jnp.mean(centred * centred, axis=-1, keepdims=True) + EPSILON)
    unit = centred * inverse
    return (unit * gain + shift, unit, inverse)


def normalize_back(grad, unit, inverse, gain):
    scaled = grad * gain
    inner = (
        scaled
        - jnp.mean(scaled, axis=-1, keepdims=True)
        - unit * jnp.mean(scaled * unit, axis=-1, keepdims=True)
    )
    return (inner * inverse, jnp.sum(grad * unit, axis=0), jnp.sum(grad, axis=0))


def place(me, slot, slots, part):
    return pl.multiple_of(lax.rem(me + slot, slots) * part, part)


def attend_forward_kernel(slots, span, block, kept, me_ref, len_ref, *refs):
    qkv = refs[:slots]
    scale_ref = refs[slots]
    refs = refs[kept:]
    outs = refs[slots + 1 : 2 * slots + 1]
    total_ref = refs[2 * slots + 1]
    query, keys, values, mixed = refs[2 * slots + 2 :]
    part = span // slots
    me = me_ref[0]
    length = len_ref[pl.program_id(0)]
    for slot in range(slots):
        at = pl.ds(place(me, slot, slots, part), part)
        query[at, :] = qkv[slot][:, :LANES]
        keys[at, :] = qkv[slot][:, LANES : 2 * LANES]
        values[at, :] = qkv[slot][:, 2 * LANES :]
    first = lax.broadcasted_iota(jnp.int32, (1, LANES), 1) < HEAD
    for i in range(span // block):
        rows = slice(i * block, (i + 1) * block)
        query_block = query[rows, :]
        halves = []
        for head in range(2):
            mine = first if head == 0 else jnp.logical_not(first)
            query_head = jnp.where(mine, query_block, jnp.zeros_like(query_block))
            scores = []
            for j in range(i + 1):
                key_block = keys[j * block : (j + 1) * block, :]
                score = dot(query_head, key_block, COLUMN_PAIRS)
                key_place = lax.broadcasted_iota(jnp.int32, (block, block), 1)
                allowed = None
                if i == j:
                    allowed = key_place <= lax.broadcasted_iota(jnp.int32, (block, block), 0)
                if (j + 1) * block > span // 2:
                    short = key_place < length - j * block
                    allowed = short if allowed is None else allowed & short
                if allowed is not None:
                    score = jnp.where(allowed, score, MASKED)
                scores.append(score)
            top = functools.reduce(jnp.maximum, scores)
            top = jnp.max(top, axis=-1, keepdims=True) * EXPONENT_SCALE
            weights = [jnp.exp2(score * EXPONENT_SCALE - top) for score in scores]
            total = jnp.sum(functools.reduce(jnp.add, weights), axis=-1, keepdims=True)
            result = None
            for j in range(i + 1):
                term = dot(weights[j].astype(BF), values[j * block : (j + 1) * block, :])
                result = term if result is None else result + term
            halves.append(result / total)
            log_total = jnp.broadcast_to(top + jnp.log2(total), (block, LANES))
            total_ref[0, 0, head : head + 1, rows] = jnp.transpose(log_total)[:1, :]
        mixed[rows, :] = (jnp.where(first, halves[0], halves[1]) * scale_ref[...]).astype(BF)
    for slot in range(slots):
        outs[slot][...] = mixed[pl.ds(place(me, slot, slots, part), part), :]


def attend_backward_kernel(slots, span, block, kept, me_ref, len_ref, *refs):
    qkv = refs[:slots]
    out = refs[slots : 2 * slots]
    grads = refs[2 * slots : 3 * slots]
    scale_ref, total_ref = refs[3 * slots : 3 * slots + 2]
    refs = refs[kept:]
    results = refs[3 * slots + 2 : 4 * slots + 2]
    sums_ref = refs[4 * slots + 2]
    query, keys, values, mixed_grad, product, query_grad, key_grad, value_grad = refs[4 * slots + 3 :]
    part = span // slots
    me = me_ref[0]
    length = len_ref[pl.program_id(0)]
    for slot in range(slots):
        at = pl.ds(place(me, slot, slots, part), part)
        query[at, :] = qkv[slot][:, :LANES]
        keys[at, :] = qkv[slot][:, LANES : 2 * LANES]
        values[at, :] = qkv[slot][:, 2 * LANES :]
        grad = grads[slot][...].astype(F32)
        mixed_grad[at, :] = (grad * scale_ref[...]).astype(BF)
        product[at, :] = grad * out[slot][...].astype(F32)
    first = lax.broadcasted_iota(jnp.int32, (1, LANES), 1) < HEAD
    which = lax.broadcasted_iota(jnp.int32, (8, LANES), 0)
    lane_head = lax.broadcasted_iota(jnp.int32, (8, LANES), 1) // HEAD
    picks = jnp.where(which == lane_head, 1.0, 0.0).astype(BF)
    inner = product[...]
    inner_high = inner.astype(BF)
    inner_low = (inner - inner_high.astype(F32)).astype(BF)
    inner_sum = dot(picks, inner_high, COLUMN_PAIRS) + dot(picks, inner_low, COLUMN_PAIRS)
    scale_sum = jnp.sum(inner, axis=0, keepdims=True) / scale_ref[...]
    count = span // block

    def tile(head, keys_from, keys_to, start, stop, key_head, value_head, key_turned):
        rows = slice(start, stop)
        query_block, grad_block = query[rows, :], mixed_grad[rows, :]
        score = dot(key_head, query_block, COLUMN_PAIRS)
        shares = jnp.exp2(score * EXPONENT_SCALE - total_ref[0, 0, head : head + 1, rows])
        key_place = keys_from + lax.broadcasted_iota(jnp.int32, score.shape, 0)
        allowed = None
        if start < keys_to:
            allowed = key_place <= start + lax.broadcasted_iota(jnp.int32, score.shape, 1)
        if keys_to > span // 2:
            short = key_place < length
            allowed = short if allowed is None else allowed & short
        if allowed is not None:
            shares = jnp.where(allowed, shares, 0.0)
        share_grad = dot(value_head, grad_block, COLUMN_PAIRS)
        score_grad = shares * (share_grad - inner_sum[head : head + 1, rows])
        score_grad = score_grad.astype(BF)
        value_term = dot(shares.astype(BF), grad_block)
        key_term = dot(score_grad, query_block)
        return value_term, key_term, dot(key_turned, score_grad)

    query_grad[...] = jnp.zeros_like(query_grad)
    for j in range(count):
        at = j * block
        cols = slice(at, at + block)
        key_block, value_block = keys[cols, :], values[cols, :]
        heads = []
        for head in range(2):
            mine = first if head == 0 else jnp.logical_not(first)
            key_head = jnp.where(mine, key_block, jnp.zeros_like(key_block))
            value_head = jnp.where(mine, value_block, jnp.zeros_like(value_block))
            key_turned = jnp.transpose(key_head.astype(F32)).astype(BF)
            heads.append((key_head, value_head, key_turned))
        sums = [None, None]
        half = block // 2

        def one(head, i):
            key_head, value_head, key_turned = heads[head]
            if i == j and True:
                parts = []
                for low, high in ((0, half), (half, block)):
                    value_term, key_term, query_term = tile(
                        head, at + low, at + high, at + low, at + block,
                        key_head[low:high], value_head[low:high], key_turned[:, low:high],
                    )
                    query_grad[:, at + low : at + block] += query_term
                    parts.append((value_term, key_term))
                terms = [jnp.concatenate(pair, 0) for pair in zip(*parts)]
            else:
                start = i * block
                value_term, key_term, query_term = tile(
                    head, at, at + block, start, start + block, key_head, value_head, key_turned
                )
                query_grad[:, start : start + block] += query_term
                terms = [value_term, key_term]
            if sums[head] is None:
                sums[head] = terms
            else:
                sums[head] = [x + y for x, y in zip(sums[head], terms)]

        for head in range(2):
            for i in range(j, count):
                one(head, i)
        value_grad[cols, :] = jnp.where(first, sums[0][0], sums[1][0]).astype(BF)
        key_grad[cols, :] = (jnp.where(first, sums[0][1], sums[1][1]) * HEAD ** (-0.5)).astype(BF)
    product[...] = jnp.transpose(query_grad[...])
    query_sum = value_sum = jnp.zeros((1, LANES), F32)
    for slot in range(slots):
        at = pl.ds(place(me, slot, slots, part), part)
        piece = (product[at, :] * HEAD ** (-0.5)).astype(BF)
        results[slot][:, :LANES] = piece
        results[slot][:, LANES : 2 * LANES] = key_grad[at, :]
        results[slot][:, 2 * LANES :] = value_grad[at, :]
        query_sum += jnp.sum(piece.astype(F32), axis=0, keepdims=True)
        value_sum += jnp.sum(value_grad[at, :].astype(F32), axis=0, keepdims=True)
    sums_ref[0, 0, 0:1, :] = query_sum
    sums_ref[0, 0, 1:2, :] = value_sum
    sums_ref[0, 0, 2:3, :] = scale_sum
    sums_ref[0, 0, 3:, :] = jnp.zeros((5, LANES), F32)


def attention_specs(slots, span, first_block, width):
    part = span // slots
    return pl.BlockSpec((part, width), lambda r, p, *_: (first_block + r, p))


def attend_forward(me, lengths, qkv, scale_lanes, kept, rows, span, first_block):
    slots = len(qkv)
    tokens = qkv[0].shape[0]
    pairs = qkv[0].shape[1] // (3 * LANES)
    block = min(512, span)
    call = pl.pallas_call(
        functools.partial(attend_forward_kernel, slots, span, block, len(kept)),
        grid_spec=pltpu.PrefetchScalarGridSpec(
            num_scalar_prefetch=2,
            grid=(rows, pairs),
            in_specs=[attention_specs(slots, span, first_block, 3 * LANES)] * slots
            + [pl.BlockSpec((1, LANES), lambda r, p, *_: (0, p))]
            + [pl.BlockSpec(memory_space=pl.ANY)] * len(kept),
            out_specs=[attention_specs(slots, span, first_block, LANES)] * slots
            + [pl.BlockSpec((1, 1, 2, span), lambda r, p, *_: (p, r, 0, 0))],
            scratch_shapes=[pltpu.VMEM((span, LANES), BF)] * 4,
        ),
        out_shape=[jax.ShapeDtypeStruct((tokens, pairs * LANES), BF)] * slots
        + [jax.ShapeDtypeStruct((pairs, rows, 2, span), F32)],
        input_output_aliases={3 + slots + k: k for k in range(len(kept))},
        compiler_params=pltpu.CompilerParams(vmem_limit_bytes=56 * 2**20),
        name="attend_forward",
    )
    *outs, log_total = call(me, lengths, *qkv, scale_lanes, *kept)
    return outs, log_total


def attend_backward(
    me, lengths, qkv, outs, grads, scale_lanes, log_total, kept, rows, span, first_block
):
    slots = len(qkv)
    tokens = qkv[0].shape[0]
    pairs = qkv[0].shape[1] // (3 * LANES)
    block = min(512, span)
    call = pl.pallas_call(
        functools.partial(attend_backward_kernel, slots, span, block, len(kept)),
        grid_spec=pltpu.PrefetchScalarGridSpec(
            num_scalar_prefetch=2,
            grid=(rows, pairs),
            in_specs=[attention_specs(slots, span, first_block, 3 * LANES)] * slots
            + [attention_specs(slots, span, first_block, LANES)] * (2 * slots)
            + [
                pl.BlockSpec((1, LANES), lambda r, p, *_: (0, p)),
                pl.BlockSpec((1, 1, 2, span), lambda r, p, *_: (p, r, 0, 0)),
            ]
            + [pl.BlockSpec(memory_space=pl.ANY)] * len(kept),
            out_specs=[attention_specs(slots, span, first_block, 3 * LANES)] * slots
            + [pl.BlockSpec((1, 1, 8, LANES), lambda r, p, *_: (r, p, 0, 0))],
            scratch_shapes=[pltpu.VMEM((span, LANES), BF)] * 4
            + [pltpu.VMEM((span, LANES), F32), pltpu.VMEM((LANES, span), F32)]
            + [pltpu.VMEM((span, LANES), BF)] * 2,
        ),
        out_shape=[jax.ShapeDtypeStruct((tokens, pairs * 3 * LANES), BF)] * slots
        + [jax.ShapeDtypeStruct((rows, pairs, 8, LANES), F32)],
        input_output_aliases={4 + 3 * slots + k: k for k in range(len(kept))},
        compiler_params=pltpu.CompilerParams(vmem_limit_bytes=56 * 2**20),
        name="attend_backward",
    )
    *results, sums = call(me, lengths, *qkv, *outs, *grads, scale_lanes, log_total, *kept)
    return results, sums


def fold(value):
    return functools.reduce(
        jnp.add, [value[:, k : k + LANES] for k in range(0, value.shape[1], LANES)]
    )


def row_sum(value):
    return jnp.sum(value, axis=-1, keepdims=True)


def column_sum(value):
    return jnp.sum(value, axis=0, keepdims=True)


def middle_kernel(slots, chunk, *refs):
    rows_ref, cot_ref = refs[:2]
    scaled = refs[2 : 2 + slots]
    out_weights = refs[2 + slots : 2 + 2 * slots]
    feed_ref, gains, shifts, mid_gain, mid_shifts = refs[2 + 2 * slots : 7 + 2 * slots]
    results = refs[7 + 2 * slots :]
    out_ref, residual_grad_ref, dense_ref, attended_grad_ref = results[:4]
    middle_ref, hidden_grad_ref, sums_ref, mid_sums_ref = results[4:8]
    scaled_grads = results[8 : 8 + slots]
    gelu_ref, slope_ref, grad_ref = results[8 + slots :]

    @pl.when(pl.program_id(0) == 0)
    def _():
        sums_ref[...] = jnp.zeros_like(sums_ref)
        mid_sums_ref[...] = jnp.zeros_like(mid_sums_ref)

    attended = shifts[3:4, :]
    for rows, matrix in zip(scaled, out_weights):
        attended = attended + dot(rows[...], matrix[...]).astype(BF).astype(F32)
    post, post_unit, post_inverse = normalize(attended, gains[1:2, :], shifts[1:2, :])
    residual = rows_ref[...].astype(F32) + post
    dense, dense_unit, dense_inverse = normalize(residual, gains[2:3, :], shifts[2:3, :])
    dense = dense.astype(BF)
    dense_ref[...] = dense
    cotangent = cot_ref[...]
    total = mid_gain.shape[1]

    def up(start):
        return feed_ref[2 * start : 2 * start + chunk, :]

    def down(start):
        return feed_ref[2 * start + chunk : 2 * start + 2 * chunk, :]

    base = first = second = third = fourth = None
    for start in range(0, total, chunk):
        cols = slice(start, start + chunk)
        hidden = dot(dense, up(start), COLUMN_PAIRS) + mid_shifts[0:1, cols]
        square = hidden * hidden
        bent = jnp.tanh(hidden * (GELU_SCALE + GELU_SCALE * GELU_CUBE * square))
        half = 0.5 * hidden
        active = half + half * bent
        slope = (0.5 + 0.5 * bent) + (half * (1.0 - bent * bent)) * (
            GELU_SCALE + 3.0 * GELU_SCALE * GELU_CUBE * square
        )
        grad = dot(cotangent, down(start), COLUMN_PAIRS)
        gelu_ref[:, cols] = active
        slope_ref[:, cols] = slope
        grad_ref[:, cols] = grad
        if base is None:
            base = row_sum(fold(active)) / chunk
        away = active - base
        weighted = grad * mid_gain[:, cols]
        terms = [fold(away), fold(away * away), fold(weighted), fold(weighted * away)]
        if first is None:
            first, second, third, fourth = terms
        else:
            first, second, third, fourth = [
                a + b for a, b in zip((first, second, third, fourth), terms)
            ]
    offset = row_sum(first) / total
    mean = base + offset
    inverse = lax.rsqrt(jnp.maximum(row_sum(second) / total - offset * offset, 0.0) + EPSILON)
    grad_mean = row_sum(third) / total
    grad_unit = inverse * (row_sum(fourth) / total - offset * grad_mean)
    branch = dense_grad = None
    for start in range(0, total, chunk):
        cols = slice(start, start + chunk)
        unit = (gelu_ref[:, cols] - mean) * inverse
        gain = mid_gain[:, cols]
        middle = (unit * gain + mid_shifts[1:2, cols]).astype(BF)
        middle_ref[:, cols] = middle
        term = dot(middle, down(start))
        branch = term if branch is None else branch + term
        grad = grad_ref[:, cols]
        inner = inverse * (grad * gain - grad_mean - unit * grad_unit)
        hidden_grad = (inner * slope_ref[:, cols]).astype(BF)
        hidden_grad_ref[:, cols] = hidden_grad
        mid_sums_ref[0:1, cols] += column_sum(grad * unit)
        mid_sums_ref[1:2, cols] += column_sum(grad)
        mid_sums_ref[2:3, cols] += column_sum(hidden_grad.astype(F32))
        term = dot(hidden_grad, up(start))
        dense_grad = term if dense_grad is None else dense_grad + term
    out_ref[...] = (residual + branch + shifts[4:5, :]).astype(BF)
    cot_wide = cotangent.astype(F32)

    def back(grad, unit, inverse, row):
        scaled = grad * gains[row : row + 1, :]
        inner = (
            scaled
            - jnp.mean(scaled, axis=-1, keepdims=True)
            - unit * jnp.mean(scaled * unit, axis=-1, keepdims=True)
        )
        sums_ref[row : row + 1, :] += column_sum(grad * unit)
        sums_ref[row + 2 : row + 3, :] += column_sum(grad)
        return inner * inverse

    residual_grad = cot_wide + back(dense_grad, dense_unit, dense_inverse, 2)
    residual_grad_ref[...] = residual_grad
    attended_grad = back(residual_grad, post_unit, post_inverse, 1)
    sums_ref[5:6, :] += column_sum(attended_grad)
    sums_ref[6:7, :] += column_sum(cot_wide)
    attended_grad = attended_grad.astype(BF)
    attended_grad_ref[...] = attended_grad
    for result, matrix in zip(scaled_grads, out_weights):
        result[...] = dot(attended_grad, matrix[...], COLUMN_PAIRS).astype(BF)


def middle_pass(
    chunk, rows, cotangent, scaled, out_weights, feed, gains, shifts, mid_gain, mid_shifts
):
    slots = len(scaled)
    tokens, width = rows.shape
    part = scaled[0].shape[1]
    hidden = mid_gain.shape[1]
    block = min(256, tokens)

    def tiles(columns):
        return pl.BlockSpec((block, columns), lambda i: (i, 0))

    def whole(array):
        return pl.BlockSpec(array.shape, lambda i: (0, 0), pipeline_mode=pl.Buffered(1))

    call = pl.pallas_call(
        functools.partial(middle_kernel, slots, chunk),
        grid=(tokens // block,),
        in_specs=[tiles(width), tiles(width)]
        + [tiles(part)] * slots
        + [whole(item) for item in (*out_weights, feed, gains, shifts, mid_gain, mid_shifts)],
        out_specs=[tiles(width)] * 4
        + [tiles(hidden)] * 2
        + [pl.BlockSpec((8, width), lambda i: (0, 0)), pl.BlockSpec((8, hidden), lambda i: (0, 0))]
        + [tiles(part)] * slots,
        out_shape=[
            jax.ShapeDtypeStruct((tokens, width), BF),
            jax.ShapeDtypeStruct((tokens, width), F32),
            jax.ShapeDtypeStruct((tokens, width), BF),
            jax.ShapeDtypeStruct((tokens, width), BF),
            jax.ShapeDtypeStruct((tokens, hidden), BF),
            jax.ShapeDtypeStruct((tokens, hidden), BF),
            jax.ShapeDtypeStruct((8, width), F32),
            jax.ShapeDtypeStruct((8, hidden), F32),
        ]
        + [jax.ShapeDtypeStruct((tokens, part), BF)] * slots,
        scratch_shapes=[pltpu.VMEM((block, hidden), F32)] * 3,
        compiler_params=pltpu.CompilerParams(vmem_limit_bytes=60 * 2**20),
        name="middle_pass",
    )
    return call(rows, cotangent, *scaled, *out_weights, feed, gains, shifts, mid_gain, mid_shifts)


def feed_grads_kernel(groups, *refs):
    middles, hidden_grads = refs[:groups], refs[groups : 2 * groups]
    cots, denses = refs[2 * groups : 3 * groups], refs[3 * groups : 4 * groups]
    result = refs[4 * groups]
    width = cots[0].shape[1]
    for at, lefts, rights in ((0, middles, cots), (width, hidden_grads, denses)):
        total = functools.reduce(
            jnp.add, [dot(a[...], b[...], ROW_PAIRS) for a, b in zip(lefts, rights)]
        )
        result[:, at : at + width] = total.astype(BF)


def feed_grads(middles, hidden_grads, cots, denses):
    groups = len(middles)
    hidden, width = middles[0].shape[1], cots[0].shape[1]
    block = min(256, hidden)

    def columns(array):
        return pl.BlockSpec((array.shape[0], block), lambda i: (0, i))

    def whole(array):
        return pl.BlockSpec(array.shape, lambda i: (0, 0), pipeline_mode=pl.Buffered(1))

    return pl.pallas_call(
        functools.partial(feed_grads_kernel, groups),
        grid=(hidden // block,),
        in_specs=[columns(item) for item in (*middles, *hidden_grads)]
        + [whole(item) for item in (*cots, *denses)],
        out_specs=pl.BlockSpec((block, 2 * width), lambda i: (i, 0)),
        out_shape=jax.ShapeDtypeStruct((hidden, 2 * width), BF),
        compiler_params=pltpu.CompilerParams(vmem_limit_bytes=56 * 2**20),
        name="feed_grads",
    )(*middles, *hidden_grads, *cots, *denses)


def head_grads_kernel(count, *refs):
    rows, grads = refs[:count], refs[count : 2 * count]
    *out_grads, result, total = refs[2 * count :]

    @pl.when(pl.program_id(0) == 0)
    def _():
        total[...] = jnp.zeros_like(total)

    wide = 2 * LANES
    for at in range(0, total.shape[1], wide):
        cols = slice(at, at + wide)
        total[:, cols] += functools.reduce(
            jnp.add,
            [dot(left[...], right[:, cols], ROW_PAIRS) for left, right in zip(rows, grads)],
        )

    @pl.when(pl.program_id(0) == pl.num_programs(0) - 1)
    def _():
        for at in range(0, total.shape[1], LANES):
            pair, kind = divmod(at // LANES, 3)
            result[kind, :, pair * LANES : (pair + 1) * LANES] = total[:, at : at + LANES].astype(BF)
        part, width = out_grads[0].shape
        out_grad = functools.reduce(jnp.add, [item[...].astype(F32) for item in out_grads])
        for at in range(0, width, part):
            result[3, at : at + part, :] = out_grad[:, at : at + part].astype(BF)


def head_grads(rows, grads, out_grads):
    tokens, width = rows[0].shape
    columns = grads[0].shape[1]
    block = min(512, tokens)
    return pl.pallas_call(
        functools.partial(head_grads_kernel, len(rows)),
        grid=(tokens // block,),
        in_specs=[pl.BlockSpec((block, width), lambda i: (i, 0))] * len(rows)
        + [pl.BlockSpec((block, columns), lambda i: (i, 0))] * len(grads)
        + [pl.BlockSpec(item.shape, lambda i: (0, 0)) for item in out_grads],
        out_specs=pl.BlockSpec((4, width, columns // 3), lambda i: (0, 0, 0)),
        out_shape=jax.ShapeDtypeStruct((4, width, columns // 3), BF),
        scratch_shapes=[pltpu.VMEM((width, columns), F32)],
        compiler_params=pltpu.CompilerParams(vmem_limit_bytes=56 * 2**20),
        name="head_grads",
    )(*rows, *grads, *out_grads)


def partner(name, bit):
    me = lax.axis_index(name)
    mine = lax.rem(me // (1 << bit), 2)
    return mine, {name: me + (1 - 2 * mine) * (1 << bit)}


def greet(places):
    barrier = pltpu.get_barrier_semaphore()
    for place_of in places:
        pl.semaphore_signal(barrier, inc=1, device_id=place_of, device_id_type=MESH)
    pl.semaphore_wait(barrier, len(places))


def batch_sum_kernel(bits, chunks, steps, source, extra, result, extra_result, *refs):
    levels, arrivals = refs[:bits], refs[bits : 2 * bits]
    extra_totals, extra_arrivals = refs[2 * bits : 2 * bits + 2]
    send_sems, recv_sems, extra_send_sems, extra_recv_sems = refs[2 * bits + 2 :]
    rows = source.shape[0] // chunks
    partners = [partner("batch", bit) for bit in range(bits)]
    extra_partners = [partner(name, bit)[1] for name, bit in steps]
    greet(extra_partners)
    offsets, offset = [], 0
    for bit in range(bits):
        offset = offset + partners[bit][0] * (rows >> (bit + 1))
        offsets.append(offset)

    def aligned(value, size):
        return pl.ds(pl.multiple_of(value, size), size)

    def piece(chunk, bit, mine):
        size = rows >> (bit + 1)
        if bit == 0:
            return source.at[aligned(chunk * rows + mine * size, size), :]
        return levels[bit - 1].at[chunk, aligned(mine * size, size), :]

    def final(chunk, bit):
        return result.at[aligned(chunk * rows + offsets[bit], rows >> (bit + 1)), :]

    copies = {}

    def start(chunk, stage):
        if stage < bits:
            mine, other = partners[stage]
            here, there = piece(chunk, stage, 1 - mine), arrivals[stage].at[chunk]
        else:
            bit = 2 * bits - 1 - stage
            other = partners[bit][1]
            here = there = final(chunk, bit)
        copies[chunk, stage] = pltpu.make_async_remote_copy(
            src_ref=here,
            dst_ref=there,
            send_sem=send_sems.at[chunk, stage],
            recv_sem=recv_sems.at[chunk, stage],
            device_id=other,
            device_id_type=MESH,
        )
        copies[chunk, stage].start()

    def finish(chunk, stage):
        copies[chunk, stage].wait_recv()
        if stage < bits:
            kept = piece(chunk, stage, partners[stage][0])[...].astype(F32)
            total = (kept + arrivals[stage][chunk].astype(F32)).astype(BF)
            if stage == bits - 1:
                final(chunk, stage)[...] = total
            else:
                levels[stage][chunk] = total

    def extra_total(step):
        if step == 0:
            return extra
        return extra_result if step == len(steps) else extra_totals.at[step - 1]

    def extra_copy(step):
        return pltpu.make_async_remote_copy(
            src_ref=extra_total(step),
            dst_ref=extra_arrivals.at[step],
            send_sem=extra_send_sems.at[step],
            recv_sem=extra_recv_sems.at[step],
            device_id=extra_partners[step],
            device_id_type=MESH,
        )

    extra_copies = []
    for tick in range(max(chunks + 2 * bits, len(steps) + 1)):
        if 0 < tick <= len(steps):
            extra_copies[tick - 1].wait_recv()
            extra_total(tick)[...] = extra_total(tick - 1)[...] + extra_arrivals[tick - 1]
        if tick < len(steps):
            extra_copies.append(extra_copy(tick))
            extra_copies[tick].start()
        for chunk in range(chunks):
            stage = tick - chunk
            if 0 < stage <= 2 * bits:
                finish(chunk, stage - 1)
            if 0 <= stage < 2 * bits:
                start(chunk, stage)
    for copy in (*copies.values(), *extra_copies):
        copy.wait_send()


def halving_steps(axes):
    return [(name, bit) for name, size in axes for bit in range(size.bit_length() - 1)]


def batch_sum(value, extra, axes):
    bits = axes[0][1].bit_length() - 1
    if bits == 0 or any(size & (size - 1) for _, size in axes):
        return lax.psum(value, "batch"), lax.psum(extra, tuple(name for name, _ in axes))
    steps = halving_steps(axes)
    rows, columns = value.shape
    chunks = 4
    halves = [
        pltpu.VMEM((chunks, rows // chunks >> (bit + 1), columns), BF) for bit in range(bits)
    ]
    return pl.pallas_call(
        functools.partial(batch_sum_kernel, bits, chunks, steps),
        in_specs=[pl.BlockSpec(memory_space=pltpu.VMEM)] * 2,
        out_specs=[pl.BlockSpec(memory_space=pltpu.VMEM)] * 2,
        out_shape=[
            jax.ShapeDtypeStruct(value.shape, BF),
            jax.ShapeDtypeStruct(extra.shape, F32),
        ],
        scratch_shapes=halves * 2
        + [pltpu.VMEM((len(steps), *extra.shape), F32)] * 2
        + [pltpu.SemaphoreType.DMA((chunks, 2 * bits))] * 2
        + [pltpu.SemaphoreType.DMA((len(steps),))] * 2,
        compiler_params=pltpu.CompilerParams(
            collective_id=0, has_side_effects=True, vmem_limit_bytes=40 * 2**20
        ),
        name="batch_sum",
    )(value, extra)


def small_sum_kernel(steps, source, result, *refs):
    totals, arrivals = refs[:-2][: len(steps) - 1], refs[:-2][len(steps) - 1 :]
    send_sems, recv_sems = refs[-2:]
    partners = [partner(name, bit)[1] for name, bit in steps]
    greet(partners)
    here = source
    copies = []
    for step, other in enumerate(partners):
        copy = pltpu.make_async_remote_copy(
            src_ref=here,
            dst_ref=arrivals[step],
            send_sem=send_sems.at[step],
            recv_sem=recv_sems.at[step],
            device_id=other,
            device_id_type=MESH,
        )
        copy.start()
        copies.append(copy)
        copy.wait_recv()
        there = result if step == len(partners) - 1 else totals[step]
        there[...] = here[...] + arrivals[step][...]
        here = there
    for copy in copies:
        copy.wait_send()


def small_sum(value, axes):
    steps = halving_steps(axes)
    if not steps or any(size & (size - 1) for _, size in axes):
        return lax.psum(value, tuple(name for name, _ in axes))
    return pl.pallas_call(
        functools.partial(small_sum_kernel, steps),
        in_specs=[pl.BlockSpec(memory_space=pltpu.VMEM)],
        out_specs=pl.BlockSpec(memory_space=pltpu.VMEM),
        out_shape=jax.ShapeDtypeStruct(value.shape, F32),
        scratch_shapes=[pltpu.VMEM(value.shape, F32)] * (2 * len(steps) - 1)
        + [pltpu.SemaphoreType.DMA((len(steps),))] * 2,
        compiler_params=pltpu.CompilerParams(
            collective_id=1, has_side_effects=True, vmem_limit_bytes=40 * 2**20
        ),
        name="small_sum",
    )(value)


def unproject(grads, weights):
    total = None
    for kind in range(3):
        pieces = [
            grads[:, at : at + LANES] for at in range(kind * LANES, grads.shape[1], 3 * LANES)
        ]
        piece = pieces[0] if len(pieces) == 1 else jnp.concatenate(pieces, 1)
        term = dot(piece, weights[kind], COLUMN_PAIRS)
        total = term if total is None else total + term
    return total.astype(BF)


def unproject_kernel(grads, weights, result):
    result[...] = unproject(grads, weights)


def unproject_pass(grads, weights):
    tokens, columns = grads.shape
    width = weights.shape[1]
    block = min(256, tokens)
    return pl.pallas_call(
        unproject_kernel,
        grid=(tokens // block,),
        in_specs=[
            pl.BlockSpec((block, columns), lambda i: (i, 0)),
            pl.BlockSpec(weights.shape, lambda i: (0, 0, 0), pipeline_mode=pl.Buffered(1)),
        ],
        out_specs=pl.BlockSpec((block, width), lambda i: (i, 0)),
        out_shape=jax.ShapeDtypeStruct((tokens, width), BF),
        compiler_params=pltpu.CompilerParams(vmem_limit_bytes=40 * 2**20),
        name="unproject",
    )(grads, weights)


def out_grads_kernel(groups, slots, *refs):
    grads, scaled, results = refs[:groups], refs[groups:-slots], refs[-slots:]
    for slot, result in enumerate(results):
        total = functools.reduce(
            jnp.add,
            [
                dot(scaled[group * slots + slot][...], grads[group][...], ROW_PAIRS)
                for group in range(groups)
            ],
        )
        result[...] = total.astype(BF)


def out_grads_pass(grads, scaled):
    slots = len(scaled[0])
    part, width = scaled[0][0].shape[1], grads[0].shape[1]
    items = [*grads, *[item for group in scaled for item in group]]
    return pl.pallas_call(
        functools.partial(out_grads_kernel, len(grads), slots),
        in_specs=[pl.BlockSpec(memory_space=pltpu.VMEM)] * len(items),
        out_specs=[pl.BlockSpec(memory_space=pltpu.VMEM)] * slots,
        out_shape=[jax.ShapeDtypeStruct((part, width), BF)] * slots,
        compiler_params=pltpu.CompilerParams(vmem_limit_bytes=40 * 2**20),
        name="out_grads",
    )(*items)


def first_back_kernel(count, rows_ref, grad_ref, weights, gains, shifts, residual_ref, *refs):
    arrived = refs[:count]
    result, sums_ref = refs[count:]

    @pl.when(pl.program_id(0) == 0)
    def _():
        sums_ref[...] = jnp.zeros_like(sums_ref)

    grad = unproject(grad_ref, weights).astype(F32)
    for term in arrived:
        grad = grad + term[...].astype(F32)
    gain = gains[0:1, :]
    _, unit, inverse = normalize(rows_ref[...].astype(F32), gain, shifts[0:1, :])
    scaled = grad * gain
    inner = (
        scaled
        - jnp.mean(scaled, axis=-1, keepdims=True)
        - unit * jnp.mean(scaled * unit, axis=-1, keepdims=True)
    )
    sums_ref[0:1, :] += column_sum(grad * unit)
    sums_ref[1:2, :] += column_sum(grad)
    result[...] = (residual_ref[...] + inner * inverse).astype(BF)


def first_back(rows, qkv_grad, weights, gains, shifts, residual_grad, arrived):
    tokens, width = rows.shape
    block = min(256, tokens)

    def tiles(columns):
        return pl.BlockSpec((block, columns), lambda i: (i, 0))

    def whole(array):
        zeros = (0,) * array.ndim
        return pl.BlockSpec(array.shape, lambda i: zeros, pipeline_mode=pl.Buffered(1))

    return pl.pallas_call(
        functools.partial(first_back_kernel, len(arrived)),
        grid=(tokens // block,),
        in_specs=[
            tiles(width),
            tiles(qkv_grad.shape[1]),
            whole(weights),
            whole(gains),
            whole(shifts),
            tiles(width),
        ]
        + [tiles(width)] * len(arrived),
        out_specs=[tiles(width), pl.BlockSpec((8, width), lambda i: (0, 0))],
        out_shape=[
            jax.ShapeDtypeStruct((tokens, width), BF),
            jax.ShapeDtypeStruct((8, width), F32),
        ],
        compiler_params=pltpu.CompilerParams(vmem_limit_bytes=40 * 2**20),
        name="first_back",
    )(rows, qkv_grad, weights, gains, shifts, residual_grad, *arrived)


def project_kernel(rows_ref, weights, biases, result):
    rows = rows_ref[...]
    for kind in range(3):
        value = (dot(rows, weights[kind]) + biases[kind : kind + 1, :]).astype(BF)
        for pair in range(value.shape[1] // LANES):
            at = (3 * pair + kind) * LANES
            result[:, at : at + LANES] = value[:, pair * LANES : (pair + 1) * LANES]


def project(rows, weights, biases):
    tokens, width = rows.shape
    columns = 3 * weights.shape[2]
    block = min(256, tokens)
    return pl.pallas_call(
        project_kernel,
        grid=(tokens // block,),
        in_specs=[
            pl.BlockSpec((block, width), lambda i: (i, 0)),
            pl.BlockSpec(weights.shape, lambda i: (0, 0, 0), pipeline_mode=pl.Buffered(1)),
            pl.BlockSpec(biases.shape, lambda i: (0, 0), pipeline_mode=pl.Buffered(1)),
        ],
        out_specs=pl.BlockSpec((block, columns), lambda i: (i, 0)),
        out_shape=jax.ShapeDtypeStruct((tokens, columns), BF),
        compiler_params=pltpu.CompilerParams(vmem_limit_bytes=40 * 2**20),
        name="project",
    )(rows, weights, biases)


def shards(
    slots,
    short_rows,
    medium_rows,
    long_rows,
    short_len,
    medium_len,
    long_len,
    short_cotangent,
    medium_cotangent,
    long_cotangent,
    norm_gains,
    norm_shifts,
    head_weights,
    head_biases,
    head_scale,
    out_weight,
    up_weight,
    mid_gain,
    mid_shifts,
    down_weight,
):
    shapes = tuple((item.shape for item in (short_rows, medium_rows, long_rows)))
    width = short_rows.shape[2]
    part = head_weights.shape[2]
    me = lax.axis_index("head").astype(jnp.int32).reshape(1)

    def fetch(value, slot):
        return lax.ppermute(value, "head", [((d + slot) % slots, d) for d in range(slots)])

    def deliver(value, slot):
        return lax.ppermute(value, "head", [(d, (d + slot) % slots) for d in range(slots)])

    def spread(own, move):
        return [own[slot] if slot == 0 else move(own[slot], slot) for slot in range(slots)]

    def grouped(short, medium, long):
        return [
            long.reshape(-1, width),
            jnp.concatenate([short.reshape(-1, width), medium.reshape(-1, width)], 0),
        ]

    inputs = grouped(short_rows, medium_rows, long_rows)
    cots = grouped(short_cotangent, medium_cotangent, long_cotangent)
    short_tokens = shapes[0][0] * shapes[0][1]
    spans = tuple(shape[1] * slots for shape in shapes)
    counts = tuple(shape[0] for shape in shapes)
    long_job = (long_len, counts[2], spans[2], 0)
    short_job = (short_len, counts[0], spans[0], 0)
    medium_job = (medium_len, counts[1], spans[1], short_tokens // shapes[1][1])
    jobs = ([long_job], [short_job, medium_job])

    biases = jnp.stack([head_biases[0], jnp.zeros_like(head_biases[0]), head_biases[1]])
    scale_lanes = jnp.repeat(head_scale, HEAD).reshape(1, part)

    share = up_weight.shape[0]
    batches = mid_gain.shape[0] // (slots * share)
    own_feed = jnp.stack([up_weight, down_weight])
    feed_slots = [own_feed] + [fetch(own_feed, slot) for slot in range(1, slots)]
    feed = jnp.stack(feed_slots, 1).reshape(2 * slots * share, width)

    def turn(values, places):
        return jnp.roll(values, places, axis=1)

    mid_rows = jnp.concatenate([mid_gain[None], mid_shifts], 0).reshape(3, slots, batches, share)
    mid_rows = turn(mid_rows, -me[0]).transpose(0, 2, 1, 3).reshape(3, -1)

    lows = []
    for rows in inputs:
        value, _, _ = normalize(rows.astype(F32), norm_gains[0], norm_shifts[0])
        lows.append(value.astype(BF))
    lows[0], feed = lax.optimization_barrier((lows[0], feed))
    feed = lax.all_gather(feed, "batch", axis=0, tiled=True)
    own_qkv = [project(rows, head_weights, biases) for rows in lows]
    arrived = [fetch(lows[0], slot) for slot in range(1, slots)]
    own_qkv, arrived, lows[1] = lax.optimization_barrier((own_qkv, arrived, lows[1]))
    normed_slots = [
        [lows[0], *arrived],
        [lows[1]] + [fetch(lows[1], slot) for slot in range(1, slots)],
    ]
    out_weights, _ = lax.optimization_barrier((out_weight, normed_slots[-1][1:]))
    out_weights = [out_weight] + [deliver(out_weights, slot) for slot in range(1, slots)]

    qkv, saved, scaled = [], [], []
    for group in range(2):
        projected = [own_qkv[group]]
        projected += [project(rows, head_weights, biases) for rows in normed_slots[group][1:]]
        qkv.append(projected)
        outs, totals = [], []
        for job in jobs[group]:
            outs, log_total = attend_forward(me, job[0], projected, scale_lanes, outs, *job[1:])
            totals.append(log_total)
        saved.append((outs, totals))
        scaled.append(spread(outs, deliver))

    outputs, residual_grads, grad_slots, sums, mid_sums, attended_grads = [], [], [], [], [], []
    middles, hidden_grads, denses = [], [], []
    for group in range(2):
        results = middle_pass(
            slots * share,
            inputs[group],
            cots[group],
            scaled[group],
            out_weights,
            feed,
            norm_gains,
            norm_shifts,
            mid_rows[:1],
            mid_rows[1:],
        )
        outputs.append(results[0])
        residual_grads.append(results[1])
        denses.append(results[2])
        middles.append(results[4])
        hidden_grads.append(results[5])
        sums.append(results[6])
        mid_sums.append(results[7])
        grad_slots.append(spread(results[8:], fetch))
        attended_grads.append(results[3])
    both = feed_grads(middles, hidden_grads, cots, denses)
    out_grads = spread(out_grads_pass(attended_grads, scaled), fetch)
    grad_slots, both = lax.optimization_barrier((grad_slots, both))
    both = lax.psum_scatter(both, "batch", scatter_dimension=0, tiled=True)

    bias_sums = jnp.zeros((8, part), F32)
    grads, first_sums, qkv_grads = [], [], []

    def send_back(qkv_grad):
        return [
            deliver(unproject_pass(qkv_grad[slot], head_weights), slot)
            for slot in range(1, slots)
        ]

    def finish_back(group, arrived):
        grad, group_sums = first_back(
            inputs[group],
            qkv_grads[group][0],
            head_weights,
            norm_gains,
            norm_shifts,
            residual_grads[group],
            arrived,
        )
        grads.append(grad)
        first_sums.append(group_sums)

    for group in range(2):
        if group == 1:
            grad_slots[1], qkv_grads[0] = lax.optimization_barrier((grad_slots[1], qkv_grads[0]))
        qkv_grad = []
        outs, totals = saved[group]
        for job, log_total in zip(jobs[group], totals):
            qkv_grad, back_sums = attend_backward(
                me,
                job[0],
                qkv[group],
                outs,
                grad_slots[group],
                scale_lanes,
                log_total,
                qkv_grad,
                *job[1:],
            )
            bias_sums = bias_sums + jnp.sum(back_sums, axis=0).transpose(1, 0, 2).reshape(8, part)
        qkv_grads.append(qkv_grad)
        if group == 0:
            arrived = send_back(qkv_grad)
    weight_grad = head_grads(
        [rows for group in normed_slots for rows in group],
        [piece for group in qkv_grads for piece in group],
        out_grads,
    )
    qkv_grads[1], weight_grad = lax.optimization_barrier((qkv_grads[1], weight_grad))
    arrived_last = send_back(qkv_grads[1])
    finish_back(0, arrived)
    mid_terms = (mid_sums[0] + mid_sums[1])[:3].reshape(3, batches, slots, share)
    mid_terms = turn(mid_terms.transpose(0, 2, 1, 3), me[0])
    norm_sums = sums[0] + sums[1]
    own_sums = lax.dynamic_update_slice(
        jnp.zeros((slots, 3 * part), F32), bias_sums[:3].reshape(1, -1), (me[0], jnp.int32(0))
    )
    shared = jnp.concatenate(
        [norm_sums[1:7].reshape(-1), mid_terms.reshape(-1), own_sums.reshape(-1)]
    ).reshape(-1, LANES)
    axes = (("batch", batches), ("head", slots))
    weight_grad, shared, grads[0] = lax.optimization_barrier((weight_grad, shared, grads[0]))
    summed_weight, summed = batch_sum(weight_grad.reshape(4 * width, part), shared, axes)
    arrived_last, summed_weight, both = lax.optimization_barrier(
        (arrived_last, summed_weight, both)
    )
    summed_weight = summed_weight.reshape(4, width, part)
    both = both.reshape(slots, share, 2 * width)
    both_grads = both[0].astype(F32)
    for slot in range(1, slots):
        both_grads = both_grads + deliver(both[slot], slot).astype(F32)
    finish_back(1, arrived_last)
    late = first_sums[0] + first_sums[1]
    late, both_grads = lax.optimization_barrier((late, both_grads))
    late = small_sum(late[:2].reshape(-1, LANES), axes).reshape(2, width)
    summed = summed.reshape(-1)
    norm_sums, mid_terms, own_sums = jnp.split(
        summed, [6 * width, 6 * width + 3 * mid_gain.shape[0]]
    )
    norm_sums = norm_sums.reshape(6, width)
    mid_terms = mid_terms.reshape(3, -1)
    own_sums = lax.dynamic_slice(
        own_sums.reshape(slots, 3 * part), (me[0], jnp.int32(0)), (1, 3 * part)
    ).reshape(3, part)
    return (
        outputs[1][:short_tokens].reshape(shapes[0]),
        outputs[1][short_tokens:].reshape(shapes[1]),
        outputs[0].reshape(shapes[2]),
        grads[1][:short_tokens].reshape(shapes[0]),
        grads[1][short_tokens:].reshape(shapes[1]),
        grads[0].reshape(shapes[2]),
        jnp.concatenate([late[:1], norm_sums[:2]], 0),
        jnp.concatenate([late[1:], norm_sums[2:]], 0),
        summed_weight[:3].astype(F32),
        own_sums[:2],
        jnp.sum(own_sums[2].reshape(-1, HEAD), axis=1),
        jnp.concatenate(
            [summed_weight[3, at : at + part] for at in range(0, width, part)], 1
        ).astype(F32),
        both_grads[:, width:],
        mid_terms[0],
        jnp.stack([mid_terms[2], mid_terms[1]]),
        both_grads[:, :width],
    )


def solution(mesh):
    in_specs = (
        P("batch", "head", None),
        P("batch", "head", None),
        P("batch", "head", None),
        P("batch"),
        P("batch"),
        P("batch"),
        P("batch", "head", None),
        P("batch", "head", None),
        P("batch", "head", None),
        P(),
        P(),
        P(None, None, "head"),
        P(None, "head"),
        P("head"),
        P("head", None),
        P(("head", "batch"), None),
        P(),
        P(),
        P(("head", "batch"), None),
    )
    out_specs = (
        P("batch", "head", None),
        P("batch", "head", None),
        P("batch", "head", None),
        P("batch", "head", None),
        P("batch", "head", None),
        P("batch", "head", None),
        P(),
        P(),
        P(None, None, "head"),
        P(None, "head"),
        P("head"),
        P("head", None),
        P(("head", "batch"), None),
        P(),
        P(),
        P(("head", "batch"), None),
    )
    return jax.shard_map(
        functools.partial(shards, mesh.shape["head"]),
        mesh=mesh,
        in_specs=in_specs,
        out_specs=out_specs,
        check_vma=False,
    )
```

```python
import functools

import jax
import jax.numpy as jnp
from jax import lax
from jax.experimental import pallas as pl
from jax.experimental.pallas import tpu as pltpu
from jax.sharding import PartitionSpec as P

EPSILON = 1e-05
ROW_PAIRS = (((0,), (0,)), ((), ()))
COLUMN_PAIRS = (((1,), (1,)), ((), ()))
LANES = 128
HEAD = 64
LOG2E = 1.4426950408889634
EXPONENT_SCALE = HEAD ** (-0.5) * LOG2E
MASKED = -1e30
GELU_SCALE = 0.7978845608028654
GELU_CUBE = 0.044715
BF = jnp.bfloat16
F32 = jnp.float32
MESH = pl.DeviceIdType.MESH


def dot(a, b, dims=(((1,), (0,)), ((), ()))):
    return lax.dot_general(a, b, dims, preferred_element_type=F32)


def normalize(value, gain, shift):
    centred = value - jnp.mean(value, axis=-1, keepdims=True)
    inverse = lax.rsqrt(jnp.mean(centred * centred, axis=-1, keepdims=True) + EPSILON)
    unit = centred * inverse
    return (unit * gain + shift, unit, inverse)


def normalize_back(grad, unit, inverse, gain):
    scaled = grad * gain
    inner = (
        scaled
        - jnp.mean(scaled, axis=-1, keepdims=True)
        - unit * jnp.mean(scaled * unit, axis=-1, keepdims=True)
    )
    return (inner * inverse, jnp.sum(grad * unit, axis=0), jnp.sum(grad, axis=0))


def place(me, slot, slots, part):
    return pl.multiple_of(lax.rem(me + slot, slots) * part, part)


def attend_forward_kernel(slots, span, block, kept, me_ref, len_ref, *refs):
    qkv = refs[:slots]
    scale_ref = refs[slots]
    refs = refs[kept:]
    outs = refs[slots + 1 : 2 * slots + 1]
    total_ref = refs[2 * slots + 1]
    query, keys, values, mixed = refs[2 * slots + 2 :]
    part = span // slots
    me = me_ref[0]
    length = len_ref[pl.program_id(0)]
    for slot in range(slots):
        at = pl.ds(place(me, slot, slots, part), part)
        query[at, :] = qkv[slot][:, :LANES]
        keys[at, :] = qkv[slot][:, LANES : 2 * LANES]
        values[at, :] = qkv[slot][:, 2 * LANES :]
    first = lax.broadcasted_iota(jnp.int32, (1, LANES), 1) < HEAD
    for i in range(span // block):
        rows = slice(i * block, (i + 1) * block)
        query_block = query[rows, :]
        halves = []
        for head in range(2):
            mine = first if head == 0 else jnp.logical_not(first)
            query_head = jnp.where(mine, query_block, jnp.zeros_like(query_block))
            scores = []
            for j in range(i + 1):
                key_block = keys[j * block : (j + 1) * block, :]
                score = dot(query_head, key_block, COLUMN_PAIRS)
                key_place = lax.broadcasted_iota(jnp.int32, (block, block), 1)
                allowed = None
                if i == j:
                    allowed = key_place <= lax.broadcasted_iota(jnp.int32, (block, block), 0)
                if (j + 1) * block > span // 2:
                    short = key_place < length - j * block
                    allowed = short if allowed is None else allowed & short
                if allowed is not None:
                    score = jnp.where(allowed, score, MASKED)
                scores.append(score)
            top = functools.reduce(jnp.maximum, scores)
            top = jnp.max(top, axis=-1, keepdims=True) * EXPONENT_SCALE
            weights = [jnp.exp2(score * EXPONENT_SCALE - top) for score in scores]
            total = jnp.sum(functools.reduce(jnp.add, weights), axis=-1, keepdims=True)
            result = None
            for j in range(i + 1):
                term = dot(weights[j].astype(BF), values[j * block : (j + 1) * block, :])
                result = term if result is None else result + term
            halves.append(result / total)
            log_total = jnp.broadcast_to(top + jnp.log2(total), (block, LANES))
            total_ref[0, 0, head : head + 1, rows] = jnp.transpose(log_total)[:1, :]
        mixed[rows, :] = (jnp.where(first, halves[0], halves[1]) * scale_ref[...]).astype(BF)
    for slot in range(slots):
        outs[slot][...] = mixed[pl.ds(place(me, slot, slots, part), part), :]


def attend_backward_kernel(slots, span, block, kept, me_ref, len_ref, *refs):
    qkv = refs[:slots]
    out = refs[slots : 2 * slots]
    grads = refs[2 * slots : 3 * slots]
    scale_ref, total_ref = refs[3 * slots : 3 * slots + 2]
    refs = refs[kept:]
    results = refs[3 * slots + 2 : 4 * slots + 2]
    sums_ref = refs[4 * slots + 2]
    query, keys, values, mixed_grad, product, query_grad, key_grad, value_grad = refs[4 * slots + 3 :]
    part = span // slots
    me = me_ref[0]
    length = len_ref[pl.program_id(0)]
    for slot in range(slots):
        at = pl.ds(place(me, slot, slots, part), part)
        query[at, :] = qkv[slot][:, :LANES]
        keys[at, :] = qkv[slot][:, LANES : 2 * LANES]
        values[at, :] = qkv[slot][:, 2 * LANES :]
        grad = grads[slot][...].astype(F32)
        mixed_grad[at, :] = (grad * scale_ref[...]).astype(BF)
        product[at, :] = grad * out[slot][...].astype(F32)
    first = lax.broadcasted_iota(jnp.int32, (1, LANES), 1) < HEAD
    which = lax.broadcasted_iota(jnp.int32, (8, LANES), 0)
    lane_head = lax.broadcasted_iota(jnp.int32, (8, LANES), 1) // HEAD
    picks = jnp.where(which == lane_head, 1.0, 0.0).astype(BF)
    inner = product[...]
    inner_high = inner.astype(BF)
    inner_low = (inner - inner_high.astype(F32)).astype(BF)
    inner_sum = dot(picks, inner_high, COLUMN_PAIRS) + dot(picks, inner_low, COLUMN_PAIRS)
    scale_sum = jnp.sum(inner, axis=0, keepdims=True) / scale_ref[...]
    count = span // block

    def tile(head, keys_from, keys_to, start, stop, key_head, value_head, key_turned):
        rows = slice(start, stop)
        query_block, grad_block = query[rows, :], mixed_grad[rows, :]
        score = dot(key_head, query_block, COLUMN_PAIRS)
        shares = jnp.exp2(score * EXPONENT_SCALE - total_ref[0, 0, head : head + 1, rows])
        key_place = keys_from + lax.broadcasted_iota(jnp.int32, score.shape, 0)
        allowed = None
        if start < keys_to:
            allowed = key_place <= start + lax.broadcasted_iota(jnp.int32, score.shape, 1)
        if keys_to > span // 2:
            short = key_place < length
            allowed = short if allowed is None else allowed & short
        if allowed is not None:
            shares = jnp.where(allowed, shares, 0.0)
        share_grad = dot(value_head, grad_block, COLUMN_PAIRS)
        score_grad = shares * (share_grad - inner_sum[head : head + 1, rows])
        score_grad = score_grad.astype(BF)
        value_term = dot(shares.astype(BF), grad_block)
        key_term = dot(score_grad, query_block)
        return value_term, key_term, dot(key_turned, score_grad)

    query_grad[...] = jnp.zeros_like(query_grad)
    for j in range(count):
        at = j * block
        cols = slice(at, at + block)
        key_block, value_block = keys[cols, :], values[cols, :]
        heads = []
        for head in range(2):
            mine = first if head == 0 else jnp.logical_not(first)
            key_head = jnp.where(mine, key_block, jnp.zeros_like(key_block))
            value_head = jnp.where(mine, value_block, jnp.zeros_like(value_block))
            key_turned = jnp.transpose(key_head.astype(F32)).astype(BF)
            heads.append((key_head, value_head, key_turned))
        sums = [None, None]
        half = block // 2

        def one(head, i):
            key_head, value_head, key_turned = heads[head]
            if i == j and True:
                parts = []
                for low, high in ((0, half), (half, block)):
                    value_term, key_term, query_term = tile(
                        head, at + low, at + high, at + low, at + block,
                        key_head[low:high], value_head[low:high], key_turned[:, low:high],
                    )
                    query_grad[:, at + low : at + block] += query_term
                    parts.append((value_term, key_term))
                terms = [jnp.concatenate(pair, 0) for pair in zip(*parts)]
            else:
                start = i * block
                value_term, key_term, query_term = tile(
                    head, at, at + block, start, start + block, key_head, value_head, key_turned
                )
                query_grad[:, start : start + block] += query_term
                terms = [value_term, key_term]
            if sums[head] is None:
                sums[head] = terms
            else:
                sums[head] = [x + y for x, y in zip(sums[head], terms)]

        for head in range(2):
            for i in range(j, count):
                one(head, i)
        value_grad[cols, :] = jnp.where(first, sums[0][0], sums[1][0]).astype(BF)
        key_grad[cols, :] = (jnp.where(first, sums[0][1], sums[1][1]) * HEAD ** (-0.5)).astype(BF)
    product[...] = jnp.transpose(query_grad[...])
    query_sum = value_sum = jnp.zeros((1, LANES), F32)
    for slot in range(slots):
        at = pl.ds(place(me, slot, slots, part), part)
        piece = (product[at, :] * HEAD ** (-0.5)).astype(BF)
        results[slot][:, :LANES] = piece
        results[slot][:, LANES : 2 * LANES] = key_grad[at, :]
        results[slot][:, 2 * LANES :] = value_grad[at, :]
        query_sum += jnp.sum(piece.astype(F32), axis=0, keepdims=True)
        value_sum += jnp.sum(value_grad[at, :].astype(F32), axis=0, keepdims=True)
    sums_ref[0, 0, 0:1, :] = query_sum
    sums_ref[0, 0, 1:2, :] = value_sum
    sums_ref[0, 0, 2:3, :] = scale_sum
    sums_ref[0, 0, 3:, :] = jnp.zeros((5, LANES), F32)


def attention_specs(slots, span, first_block, width):
    part = span // slots
    return pl.BlockSpec((part, width), lambda r, p, *_: (first_block + r, p))


def attend_forward(me, lengths, qkv, scale_lanes, kept, rows, span, first_block):
    slots = len(qkv)
    tokens = qkv[0].shape[0]
    pairs = qkv[0].shape[1] // (3 * LANES)
    block = min(512, span)
    call = pl.pallas_call(
        functools.partial(attend_forward_kernel, slots, span, block, len(kept)),
        grid_spec=pltpu.PrefetchScalarGridSpec(
            num_scalar_prefetch=2,
            grid=(rows, pairs),
            in_specs=[attention_specs(slots, span, first_block, 3 * LANES)] * slots
            + [pl.BlockSpec((1, LANES), lambda r, p, *_: (0, p))]
            + [pl.BlockSpec(memory_space=pl.ANY)] * len(kept),
            out_specs=[attention_specs(slots, span, first_block, LANES)] * slots
            + [pl.BlockSpec((1, 1, 2, span), lambda r, p, *_: (p, r, 0, 0))],
            scratch_shapes=[pltpu.VMEM((span, LANES), BF)] * 4,
        ),
        out_shape=[jax.ShapeDtypeStruct((tokens, pairs * LANES), BF)] * slots
        + [jax.ShapeDtypeStruct((pairs, rows, 2, span), F32)],
        input_output_aliases={3 + slots + k: k for k in range(len(kept))},
        compiler_params=pltpu.CompilerParams(vmem_limit_bytes=56 * 2**20),
        name="attend_forward",
    )
    *outs, log_total = call(me, lengths, *qkv, scale_lanes, *kept)
    return outs, log_total


def attend_backward(
    me, lengths, qkv, outs, grads, scale_lanes, log_total, kept, rows, span, first_block
):
    slots = len(qkv)
    tokens = qkv[0].shape[0]
    pairs = qkv[0].shape[1] // (3 * LANES)
    block = min(512, span)
    call = pl.pallas_call(
        functools.partial(attend_backward_kernel, slots, span, block, len(kept)),
        grid_spec=pltpu.PrefetchScalarGridSpec(
            num_scalar_prefetch=2,
            grid=(rows, pairs),
            in_specs=[attention_specs(slots, span, first_block, 3 * LANES)] * slots
            + [attention_specs(slots, span, first_block, LANES)] * (2 * slots)
            + [
                pl.BlockSpec((1, LANES), lambda r, p, *_: (0, p)),
                pl.BlockSpec((1, 1, 2, span), lambda r, p, *_: (p, r, 0, 0)),
            ]
            + [pl.BlockSpec(memory_space=pl.ANY)] * len(kept),
            out_specs=[attention_specs(slots, span, first_block, 3 * LANES)] * slots
            + [pl.BlockSpec((1, 1, 8, LANES), lambda r, p, *_: (r, p, 0, 0))],
            scratch_shapes=[pltpu.VMEM((span, LANES), BF)] * 4
            + [pltpu.VMEM((span, LANES), F32), pltpu.VMEM((LANES, span), F32)]
            + [pltpu.VMEM((span, LANES), BF)] * 2,
        ),
        out_shape=[jax.ShapeDtypeStruct((tokens, pairs * 3 * LANES), BF)] * slots
        + [jax.ShapeDtypeStruct((rows, pairs, 8, LANES), F32)],
        input_output_aliases={4 + 3 * slots + k: k for k in range(len(kept))},
        compiler_params=pltpu.CompilerParams(vmem_limit_bytes=56 * 2**20),
        name="attend_backward",
    )
    *results, sums = call(me, lengths, *qkv, *outs, *grads, scale_lanes, log_total, *kept)
    return results, sums


def fold(value):
    return functools.reduce(
        jnp.add, [value[:, k : k + LANES] for k in range(0, value.shape[1], LANES)]
    )


def row_sum(value):
    return jnp.sum(value, axis=-1, keepdims=True)


def column_sum(value):
    return jnp.sum(value, axis=0, keepdims=True)


def middle_kernel(slots, chunk, *refs):
    rows_ref, cot_ref = refs[:2]
    scaled = refs[2 : 2 + slots]
    out_weights = refs[2 + slots : 2 + 2 * slots]
    feed_ref, gains, shifts, mid_gain, mid_shifts = refs[2 + 2 * slots : 7 + 2 * slots]
    results = refs[7 + 2 * slots :]
    out_ref, residual_grad_ref, dense_ref, attended_grad_ref = results[:4]
    middle_ref, hidden_grad_ref, sums_ref, mid_sums_ref = results[4:8]
    scaled_grads = results[8 : 8 + slots]
    gelu_ref, slope_ref, grad_ref = results[8 + slots :]

    @pl.when(pl.program_id(0) == 0)
    def _():
        sums_ref[...] = jnp.zeros_like(sums_ref)
        mid_sums_ref[...] = jnp.zeros_like(mid_sums_ref)

    attended = shifts[3:4, :]
    for rows, matrix in zip(scaled, out_weights):
        attended = attended + dot(rows[...], matrix[...]).astype(BF).astype(F32)
    post, post_unit, post_inverse = normalize(attended, gains[1:2, :], shifts[1:2, :])
    residual = rows_ref[...].astype(F32) + post
    dense, dense_unit, dense_inverse = normalize(residual, gains[2:3, :], shifts[2:3, :])
    dense = dense.astype(BF)
    dense_ref[...] = dense
    cotangent = cot_ref[...]
    total = mid_gain.shape[1]

    def up(start):
        return feed_ref[2 * start : 2 * start + chunk, :]

    def down(start):
        return feed_ref[2 * start + chunk : 2 * start + 2 * chunk, :]

    base = first = second = third = fourth = None
    for start in range(0, total, chunk):
        cols = slice(start, start + chunk)
        hidden = dot(dense, up(start), COLUMN_PAIRS) + mid_shifts[0:1, cols]
        square = hidden * hidden
        bent = jnp.tanh(hidden * (GELU_SCALE + GELU_SCALE * GELU_CUBE * square))
        half = 0.5 * hidden
        active = half + half * bent
        slope = (0.5 + 0.5 * bent) + (half * (1.0 - bent * bent)) * (
            GELU_SCALE + 3.0 * GELU_SCALE * GELU_CUBE * square
        )
        grad = dot(cotangent, down(start), COLUMN_PAIRS)
        gelu_ref[:, cols] = active
        slope_ref[:, cols] = slope
        grad_ref[:, cols] = grad
        if base is None:
            base = row_sum(fold(active)) / chunk
        away = active - base
        weighted = grad * mid_gain[:, cols]
        terms = [fold(away), fold(away * away), fold(weighted), fold(weighted * away)]
        if first is None:
            first, second, third, fourth = terms
        else:
            first, second, third, fourth = [
                a + b for a, b in zip((first, second, third, fourth), terms)
            ]
    offset = row_sum(first) / total
    mean = base + offset
    inverse = lax.rsqrt(jnp.maximum(row_sum(second) / total - offset * offset, 0.0) + EPSILON)
    grad_mean = row_sum(third) / total
    grad_unit = inverse * (row_sum(fourth) / total - offset * grad_mean)
    branch = dense_grad = None
    for start in range(0, total, chunk):
        cols = slice(start, start + chunk)
        unit = (gelu_ref[:, cols] - mean) * inverse
        gain = mid_gain[:, cols]
        middle = (unit * gain + mid_shifts[1:2, cols]).astype(BF)
        middle_ref[:, cols] = middle
        term = dot(middle, down(start))
        branch = term if branch is None else branch + term
        grad = grad_ref[:, cols]
        inner = inverse * (grad * gain - grad_mean - unit * grad_unit)
        hidden_grad = (inner * slope_ref[:, cols]).astype(BF)
        hidden_grad_ref[:, cols] = hidden_grad
        mid_sums_ref[0:1, cols] += column_sum(grad * unit)
        mid_sums_ref[1:2, cols] += column_sum(grad)
        mid_sums_ref[2:3, cols] += column_sum(hidden_grad.astype(F32))
        term = dot(hidden_grad, up(start))
        dense_grad = term if dense_grad is None else dense_grad + term
    out_ref[...] = (residual + branch + shifts[4:5, :]).astype(BF)
    cot_wide = cotangent.astype(F32)

    def back(grad, unit, inverse, row):
        scaled = grad * gains[row : row + 1, :]
        inner = (
            scaled
            - jnp.mean(scaled, axis=-1, keepdims=True)
            - unit * jnp.mean(scaled * unit, axis=-1, keepdims=True)
        )
        sums_ref[row : row + 1, :] += column_sum(grad * unit)
        sums_ref[row + 2 : row + 3, :] += column_sum(grad)
        return inner * inverse

    residual_grad = cot_wide + back(dense_grad, dense_unit, dense_inverse, 2)
    residual_grad_ref[...] = residual_grad
    attended_grad = back(residual_grad, post_unit, post_inverse, 1)
    sums_ref[5:6, :] += column_sum(attended_grad)
    sums_ref[6:7, :] += column_sum(cot_wide)
    attended_grad = attended_grad.astype(BF)
    attended_grad_ref[...] = attended_grad
    for result, matrix in zip(scaled_grads, out_weights):
        result[...] = dot(attended_grad, matrix[...], COLUMN_PAIRS).astype(BF)


def middle_pass(
    chunk, rows, cotangent, scaled, out_weights, feed, gains, shifts, mid_gain, mid_shifts
):
    slots = len(scaled)
    tokens, width = rows.shape
    part = scaled[0].shape[1]
    hidden = mid_gain.shape[1]
    block = min(256, tokens)

    def tiles(columns):
        return pl.BlockSpec((block, columns), lambda i: (i, 0))

    def whole(array):
        return pl.BlockSpec(array.shape, lambda i: (0, 0), pipeline_mode=pl.Buffered(1))

    call = pl.pallas_call(
        functools.partial(middle_kernel, slots, chunk),
        grid=(tokens // block,),
        in_specs=[tiles(width), tiles(width)]
        + [tiles(part)] * slots
        + [whole(item) for item in (*out_weights, feed, gains, shifts, mid_gain, mid_shifts)],
        out_specs=[tiles(width)] * 4
        + [tiles(hidden)] * 2
        + [pl.BlockSpec((8, width), lambda i: (0, 0)), pl.BlockSpec((8, hidden), lambda i: (0, 0))]
        + [tiles(part)] * slots,
        out_shape=[
            jax.ShapeDtypeStruct((tokens, width), BF),
            jax.ShapeDtypeStruct((tokens, width), F32),
            jax.ShapeDtypeStruct((tokens, width), BF),
            jax.ShapeDtypeStruct((tokens, width), BF),
            jax.ShapeDtypeStruct((tokens, hidden), BF),
            jax.ShapeDtypeStruct((tokens, hidden), BF),
            jax.ShapeDtypeStruct((8, width), F32),
            jax.ShapeDtypeStruct((8, hidden), F32),
        ]
        + [jax.ShapeDtypeStruct((tokens, part), BF)] * slots,
        scratch_shapes=[pltpu.VMEM((block, hidden), F32)] * 3,
        compiler_params=pltpu.CompilerParams(vmem_limit_bytes=60 * 2**20),
        name="middle_pass",
    )
    return call(rows, cotangent, *scaled, *out_weights, feed, gains, shifts, mid_gain, mid_shifts)


def feed_grads_kernel(groups, *refs):
    middles, hidden_grads = refs[:groups], refs[groups : 2 * groups]
    cots, denses = refs[2 * groups : 3 * groups], refs[3 * groups : 4 * groups]
    result = refs[4 * groups]
    width = cots[0].shape[1]
    for at, lefts, rights in ((0, middles, cots), (width, hidden_grads, denses)):
        total = functools.reduce(
            jnp.add, [dot(a[...], b[...], ROW_PAIRS) for a, b in zip(lefts, rights)]
        )
        result[:, at : at + width] = total.astype(BF)


def feed_grads(middles, hidden_grads, cots, denses):
    groups = len(middles)
    hidden, width = middles[0].shape[1], cots[0].shape[1]
    block = min(256, hidden)

    def columns(array):
        return pl.BlockSpec((array.shape[0], block), lambda i: (0, i))

    def whole(array):
        return pl.BlockSpec(array.shape, lambda i: (0, 0), pipeline_mode=pl.Buffered(1))

    return pl.pallas_call(
        functools.partial(feed_grads_kernel, groups),
        grid=(hidden // block,),
        in_specs=[columns(item) for item in (*middles, *hidden_grads)]
        + [whole(item) for item in (*cots, *denses)],
        out_specs=pl.BlockSpec((block, 2 * width), lambda i: (i, 0)),
        out_shape=jax.ShapeDtypeStruct((hidden, 2 * width), BF),
        compiler_params=pltpu.CompilerParams(vmem_limit_bytes=56 * 2**20),
        name="feed_grads",
    )(*middles, *hidden_grads, *cots, *denses)


def head_grads_kernel(count, *refs):
    rows, grads = refs[:count], refs[count : 2 * count]
    *out_grads, result, total = refs[2 * count :]

    @pl.when(pl.program_id(0) == 0)
    def _():
        total[...] = jnp.zeros_like(total)

    wide = 2 * LANES
    for at in range(0, total.shape[1], wide):
        cols = slice(at, at + wide)
        total[:, cols] += functools.reduce(
            jnp.add,
            [dot(left[...], right[:, cols], ROW_PAIRS) for left, right in zip(rows, grads)],
        )

    @pl.when(pl.program_id(0) == pl.num_programs(0) - 1)
    def _():
        for at in range(0, total.shape[1], LANES):
            pair, kind = divmod(at // LANES, 3)
            result[kind, :, pair * LANES : (pair + 1) * LANES] = total[:, at : at + LANES].astype(BF)
        part, width = out_grads[0].shape
        out_grad = functools.reduce(jnp.add, [item[...].astype(F32) for item in out_grads])
        for at in range(0, width, part):
            result[3, at : at + part, :] = out_grad[:, at : at + part].astype(BF)


def head_grads(rows, grads, out_grads):
    tokens, width = rows[0].shape
    columns = grads[0].shape[1]
    block = min(512, tokens)
    return pl.pallas_call(
        functools.partial(head_grads_kernel, len(rows)),
        grid=(tokens // block,),
        in_specs=[pl.BlockSpec((block, width), lambda i: (i, 0))] * len(rows)
        + [pl.BlockSpec((block, columns), lambda i: (i, 0))] * len(grads)
        + [pl.BlockSpec(item.shape, lambda i: (0, 0)) for item in out_grads],
        out_specs=pl.BlockSpec((4, width, columns // 3), lambda i: (0, 0, 0)),
        out_shape=jax.ShapeDtypeStruct((4, width, columns // 3), BF),
        scratch_shapes=[pltpu.VMEM((width, columns), F32)],
        compiler_params=pltpu.CompilerParams(vmem_limit_bytes=56 * 2**20),
        name="head_grads",
    )(*rows, *grads, *out_grads)


def partner(name, bit):
    me = lax.axis_index(name)
    mine = lax.rem(me // (1 << bit), 2)
    return mine, {name: me + (1 - 2 * mine) * (1 << bit)}


def greet(places):
    barrier = pltpu.get_barrier_semaphore()
    for place_of in places:
        pl.semaphore_signal(barrier, inc=1, device_id=place_of, device_id_type=MESH)
    pl.semaphore_wait(barrier, len(places))


def batch_sum_kernel(bits, chunks, steps, source, extra, result, extra_result, *refs):
    levels, arrivals = refs[:bits], refs[bits : 2 * bits]
    extra_totals, extra_arrivals = refs[2 * bits : 2 * bits + 2]
    send_sems, recv_sems, extra_send_sems, extra_recv_sems = refs[2 * bits + 2 :]
    rows = source.shape[0] // chunks
    partners = [partner("batch", bit) for bit in range(bits)]
    extra_partners = [partner(name, bit)[1] for name, bit in steps]
    greet(extra_partners)
    offsets, offset = [], 0
    for bit in range(bits):
        offset = offset + partners[bit][0] * (rows >> (bit + 1))
        offsets.append(offset)

    def aligned(value, size):
        return pl.ds(pl.multiple_of(value, size), size)

    def piece(chunk, bit, mine):
        size = rows >> (bit + 1)
        if bit == 0:
            return source.at[aligned(chunk * rows + mine * size, size), :]
        return levels[bit - 1].at[chunk, aligned(mine * size, size), :]

    def final(chunk, bit):
        return result.at[aligned(chunk * rows + offsets[bit], rows >> (bit + 1)), :]

    copies = {}

    def start(chunk, stage):
        if stage < bits:
            mine, other = partners[stage]
            here, there = piece(chunk, stage, 1 - mine), arrivals[stage].at[chunk]
        else:
            bit = 2 * bits - 1 - stage
            other = partners[bit][1]
            here = there = final(chunk, bit)
        copies[chunk, stage] = pltpu.make_async_remote_copy(
            src_ref=here,
            dst_ref=there,
            send_sem=send_sems.at[chunk, stage],
            recv_sem=recv_sems.at[chunk, stage],
            device_id=other,
            device_id_type=MESH,
        )
        copies[chunk, stage].start()

    def finish(chunk, stage):
        copies[chunk, stage].wait_recv()
        if stage < bits:
            kept = piece(chunk, stage, partners[stage][0])[...].astype(F32)
            total = (kept + arrivals[stage][chunk].astype(F32)).astype(BF)
            if stage == bits - 1:
                final(chunk, stage)[...] = total
            else:
                levels[stage][chunk] = total

    def extra_total(step):
        if step == 0:
            return extra
        return extra_result if step == len(steps) else extra_totals.at[step - 1]

    def extra_copy(step):
        return pltpu.make_async_remote_copy(
            src_ref=extra_total(step),
            dst_ref=extra_arrivals.at[step],
            send_sem=extra_send_sems.at[step],
            recv_sem=extra_recv_sems.at[step],
            device_id=extra_partners[step],
            device_id_type=MESH,
        )

    extra_copies = []
    for tick in range(max(chunks + 2 * bits, len(steps) + 1)):
        if 0 < tick <= len(steps):
            extra_copies[tick - 1].wait_recv()
            extra_total(tick)[...] = extra_total(tick - 1)[...] + extra_arrivals[tick - 1]
        if tick < len(steps):
            extra_copies.append(extra_copy(tick))
            extra_copies[tick].start()
        for chunk in range(chunks):
            stage = tick - chunk
            if 0 < stage <= 2 * bits:
                finish(chunk, stage - 1)
            if 0 <= stage < 2 * bits:
                start(chunk, stage)
    for copy in (*copies.values(), *extra_copies):
        copy.wait_send()


def halving_steps(axes):
    return [(name, bit) for name, size in axes for bit in range(size.bit_length() - 1)]


def batch_sum(value, extra, axes):
    bits = axes[0][1].bit_length() - 1
    if bits == 0 or any(size & (size - 1) for _, size in axes):
        return lax.psum(value, "batch"), lax.psum(extra, tuple(name for name, _ in axes))
    steps = halving_steps(axes)
    rows, columns = value.shape
    chunks = 4
    halves = [
        pltpu.VMEM((chunks, rows // chunks >> (bit + 1), columns), BF) for bit in range(bits)
    ]
    return pl.pallas_call(
        functools.partial(batch_sum_kernel, bits, chunks, steps),
        in_specs=[pl.BlockSpec(memory_space=pltpu.VMEM)] * 2,
        out_specs=[pl.BlockSpec(memory_space=pltpu.VMEM)] * 2,
        out_shape=[
            jax.ShapeDtypeStruct(value.shape, BF),
            jax.ShapeDtypeStruct(extra.shape, F32),
        ],
        scratch_shapes=halves * 2
        + [pltpu.VMEM((len(steps), *extra.shape), F32)] * 2
        + [pltpu.SemaphoreType.DMA((chunks, 2 * bits))] * 2
        + [pltpu.SemaphoreType.DMA((len(steps),))] * 2,
        compiler_params=pltpu.CompilerParams(
            collective_id=0, has_side_effects=True, vmem_limit_bytes=40 * 2**20
        ),
        name="batch_sum",
    )(value, extra)


def small_sum_kernel(steps, source, result, *refs):
    totals, arrivals = refs[:-2][: len(steps) - 1], refs[:-2][len(steps) - 1 :]
    send_sems, recv_sems = refs[-2:]
    partners = [partner(name, bit)[1] for name, bit in steps]
    greet(partners)
    here = source
    copies = []
    for step, other in enumerate(partners):
        copy = pltpu.make_async_remote_copy(
            src_ref=here,
            dst_ref=arrivals[step],
            send_sem=send_sems.at[step],
            recv_sem=recv_sems.at[step],
            device_id=other,
            device_id_type=MESH,
        )
        copy.start()
        copies.append(copy)
        copy.wait_recv()
        there = result if step == len(partners) - 1 else totals[step]
        there[...] = here[...] + arrivals[step][...]
        here = there
    for copy in copies:
        copy.wait_send()


def small_sum(value, axes):
    steps = halving_steps(axes)
    if not steps or any(size & (size - 1) for _, size in axes):
        return lax.psum(value, tuple(name for name, _ in axes))
    return pl.pallas_call(
        functools.partial(small_sum_kernel, steps),
        in_specs=[pl.BlockSpec(memory_space=pltpu.VMEM)],
        out_specs=pl.BlockSpec(memory_space=pltpu.VMEM),
        out_shape=jax.ShapeDtypeStruct(value.shape, F32),
        scratch_shapes=[pltpu.VMEM(value.shape, F32)] * (2 * len(steps) - 1)
        + [pltpu.SemaphoreType.DMA((len(steps),))] * 2,
        compiler_params=pltpu.CompilerParams(
            collective_id=1, has_side_effects=True, vmem_limit_bytes=40 * 2**20
        ),
        name="small_sum",
    )(value)


def unproject(grads, weights):
    total = None
    for kind in range(3):
        pieces = [
            grads[:, at : at + LANES] for at in range(kind * LANES, grads.shape[1], 3 * LANES)
        ]
        piece = pieces[0] if len(pieces) == 1 else jnp.concatenate(pieces, 1)
        term = dot(piece, weights[kind], COLUMN_PAIRS)
        total = term if total is None else total + term
    return total.astype(BF)


def unproject_kernel(grads, weights, result):
    result[...] = unproject(grads, weights)


def unproject_pass(grads, weights):
    tokens, columns = grads.shape
    width = weights.shape[1]
    block = min(256, tokens)
    return pl.pallas_call(
        unproject_kernel,
        grid=(tokens // block,),
        in_specs=[
            pl.BlockSpec((block, columns), lambda i: (i, 0)),
            pl.BlockSpec(weights.shape, lambda i: (0, 0, 0), pipeline_mode=pl.Buffered(1)),
        ],
        out_specs=pl.BlockSpec((block, width), lambda i: (i, 0)),
        out_shape=jax.ShapeDtypeStruct((tokens, width), BF),
        compiler_params=pltpu.CompilerParams(vmem_limit_bytes=40 * 2**20),
        name="unproject",
    )(grads, weights)


def out_grads_kernel(groups, slots, *refs):
    grads, scaled, results = refs[:groups], refs[groups:-slots], refs[-slots:]
    for slot, result in enumerate(results):
        total = functools.reduce(
            jnp.add,
            [
                dot(scaled[group * slots + slot][...], grads[group][...], ROW_PAIRS)
                for group in range(groups)
            ],
        )
        result[...] = total.astype(BF)


def out_grads_pass(grads, scaled):
    slots = len(scaled[0])
    part, width = scaled[0][0].shape[1], grads[0].shape[1]
    items = [*grads, *[item for group in scaled for item in group]]
    return pl.pallas_call(
        functools.partial(out_grads_kernel, len(grads), slots),
        in_specs=[pl.BlockSpec(memory_space=pltpu.VMEM)] * len(items),
        out_specs=[pl.BlockSpec(memory_space=pltpu.VMEM)] * slots,
        out_shape=[jax.ShapeDtypeStruct((part, width), BF)] * slots,
        compiler_params=pltpu.CompilerParams(vmem_limit_bytes=40 * 2**20),
        name="out_grads",
    )(*items)


def first_back_kernel(count, rows_ref, grad_ref, weights, gains, shifts, residual_ref, *refs):
    arrived = refs[:count]
    result, sums_ref = refs[count:]

    @pl.when(pl.program_id(0) == 0)
    def _():
        sums_ref[...] = jnp.zeros_like(sums_ref)

    grad = unproject(grad_ref, weights).astype(F32)
    for term in arrived:
        grad = grad + term[...].astype(F32)
    gain = gains[0:1, :]
    _, unit, inverse = normalize(rows_ref[...].astype(F32), gain, shifts[0:1, :])
    scaled = grad * gain
    inner = (
        scaled
        - jnp.mean(scaled, axis=-1, keepdims=True)
        - unit * jnp.mean(scaled * unit, axis=-1, keepdims=True)
    )
    sums_ref[0:1, :] += column_sum(grad * unit)
    sums_ref[1:2, :] += column_sum(grad)
    result[...] = (residual_ref[...] + inner * inverse).astype(BF)


def first_back(rows, qkv_grad, weights, gains, shifts, residual_grad, arrived):
    tokens, width = rows.shape
    block = min(256, tokens)

    def tiles(columns):
        return pl.BlockSpec((block, columns), lambda i: (i, 0))

    def whole(array):
        zeros = (0,) * array.ndim
        return pl.BlockSpec(array.shape, lambda i: zeros, pipeline_mode=pl.Buffered(1))

    return pl.pallas_call(
        functools.partial(first_back_kernel, len(arrived)),
        grid=(tokens // block,),
        in_specs=[
            tiles(width),
            tiles(qkv_grad.shape[1]),
            whole(weights),
            whole(gains),
            whole(shifts),
            tiles(width),
        ]
        + [tiles(width)] * len(arrived),
        out_specs=[tiles(width), pl.BlockSpec((8, width), lambda i: (0, 0))],
        out_shape=[
            jax.ShapeDtypeStruct((tokens, width), BF),
            jax.ShapeDtypeStruct((8, width), F32),
        ],
        compiler_params=pltpu.CompilerParams(vmem_limit_bytes=40 * 2**20),
        name="first_back",
    )(rows, qkv_grad, weights, gains, shifts, residual_grad, *arrived)


def project_kernel(rows_ref, weights, biases, result):
    rows = rows_ref[...]
    for kind in range(3):
        value = (dot(rows, weights[kind]) + biases[kind : kind + 1, :]).astype(BF)
        for pair in range(value.shape[1] // LANES):
            at = (3 * pair + kind) * LANES
            result[:, at : at + LANES] = value[:, pair * LANES : (pair + 1) * LANES]


def project(rows, weights, biases):
    tokens, width = rows.shape
    columns = 3 * weights.shape[2]
    block = min(256, tokens)
    return pl.pallas_call(
        project_kernel,
        grid=(tokens // block,),
        in_specs=[
            pl.BlockSpec((block, width), lambda i: (i, 0)),
            pl.BlockSpec(weights.shape, lambda i: (0, 0, 0), pipeline_mode=pl.Buffered(1)),
            pl.BlockSpec(biases.shape, lambda i: (0, 0), pipeline_mode=pl.Buffered(1)),
        ],
        out_specs=pl.BlockSpec((block, columns), lambda i: (i, 0)),
        out_shape=jax.ShapeDtypeStruct((tokens, columns), BF),
        compiler_params=pltpu.CompilerParams(vmem_limit_bytes=40 * 2**20),
        name="project",
    )(rows, weights, biases)


def shards(
    slots,
    short_rows,
    medium_rows,
    long_rows,
    short_len,
    medium_len,
    long_len,
    short_cotangent,
    medium_cotangent,
    long_cotangent,
    norm_gains,
    norm_shifts,
    head_weights,
    head_biases,
    head_scale,
    out_weight,
    up_weight,
    mid_gain,
    mid_shifts,
    down_weight,
):
    shapes = tuple((item.shape for item in (short_rows, medium_rows, long_rows)))
    width = short_rows.shape[2]
    part = head_weights.shape[2]
    me = lax.axis_index("head").astype(jnp.int32).reshape(1)

    def fetch(value, slot):
        return lax.ppermute(value, "head", [((d + slot) % slots, d) for d in range(slots)])

    def deliver(value, slot):
        return lax.ppermute(value, "head", [(d, (d + slot) % slots) for d in range(slots)])

    def deliver_shared(value, slot):
        size = lax.axis_size("batch")
        half = value.shape[0] // 2
        if size % 2 or half % 16:
            return deliver(value, slot)
        odd = lax.rem(lax.axis_index("batch"), 2).astype(jnp.int32)
        mine = deliver(lax.dynamic_slice_in_dim(value, odd * half, half, 0), slot)
        other = lax.ppermute(mine, "batch", [(d, d ^ 1) for d in range(size)])
        return jnp.where(
            odd == 0, jnp.concatenate([mine, other], 0), jnp.concatenate([other, mine], 0)
        )

    def spread(own, move):
        return [own[slot] if slot == 0 else move(own[slot], slot) for slot in range(slots)]

    def grouped(short, medium, long):
        return [
            long.reshape(-1, width),
            jnp.concatenate([short.reshape(-1, width), medium.reshape(-1, width)], 0),
        ]

    inputs = grouped(short_rows, medium_rows, long_rows)
    cots = grouped(short_cotangent, medium_cotangent, long_cotangent)
    short_tokens = shapes[0][0] * shapes[0][1]
    spans = tuple(shape[1] * slots for shape in shapes)
    counts = tuple(shape[0] for shape in shapes)
    long_job = (long_len, counts[2], spans[2], 0)
    short_job = (short_len, counts[0], spans[0], 0)
    medium_job = (medium_len, counts[1], spans[1], short_tokens // shapes[1][1])
    jobs = ([long_job], [short_job, medium_job])

    biases = jnp.stack([head_biases[0], jnp.zeros_like(head_biases[0]), head_biases[1]])
    scale_lanes = jnp.repeat(head_scale, HEAD).reshape(1, part)

    share = up_weight.shape[0]
    batches = mid_gain.shape[0] // (slots * share)
    own_feed = jnp.stack([up_weight, down_weight])
    feed_slots = [own_feed] + [fetch(own_feed, slot) for slot in range(1, slots)]
    feed = jnp.stack(feed_slots, 1).reshape(2 * slots * share, width)

    def turn(values, places):
        return jnp.roll(values, places, axis=1)

    mid_rows = jnp.concatenate([mid_gain[None], mid_shifts], 0).reshape(3, slots, batches, share)
    mid_rows = turn(mid_rows, -me[0]).transpose(0, 2, 1, 3).reshape(3, -1)

    lows = []
    for rows in inputs:
        value, _, _ = normalize(rows.astype(F32), norm_gains[0], norm_shifts[0])
        lows.append(value.astype(BF))
    lows[0], feed = lax.optimization_barrier((lows[0], feed))
    feed = lax.all_gather(feed, "batch", axis=0, tiled=True)
    own_qkv = [project(rows, head_weights, biases) for rows in lows]
    arrived = [fetch(lows[0], slot) for slot in range(1, slots)]
    own_qkv, arrived, lows[1], inputs[1], cots[1] = lax.optimization_barrier(
        (own_qkv, arrived, lows[1], inputs[1], cots[1])
    )
    normed_slots = [
        [lows[0], *arrived],
        [lows[1]] + [fetch(lows[1], slot) for slot in range(1, slots)],
    ]
    qkv, saved, scaled = [], [], []
    for group in range(2):
        projected = [own_qkv[group]]
        projected += [project(rows, head_weights, biases) for rows in normed_slots[group][1:]]
        qkv.append(projected)
        outs, totals = [], []
        for job in jobs[group]:
            outs, log_total = attend_forward(me, job[0], projected, scale_lanes, outs, *job[1:])
            totals.append(log_total)
        saved.append((outs, totals))
        if group == 0:
            outs, other_weight = lax.optimization_barrier((outs, out_weight))
            out_weights = [out_weight] + [
                deliver_shared(other_weight, slot) for slot in range(1, slots)
            ]
        scaled.append(spread(outs, deliver))

    outputs, residual_grads, grad_slots, sums, mid_sums, attended_grads = [], [], [], [], [], []
    middles, hidden_grads, denses = [], [], []
    for group in range(2):
        results = middle_pass(
            slots * share,
            inputs[group],
            cots[group],
            scaled[group],
            out_weights,
            feed,
            norm_gains,
            norm_shifts,
            mid_rows[:1],
            mid_rows[1:],
        )
        outputs.append(results[0])
        residual_grads.append(results[1])
        denses.append(results[2])
        middles.append(results[4])
        hidden_grads.append(results[5])
        sums.append(results[6])
        mid_sums.append(results[7])
        grad_slots.append(spread(results[8:], fetch))
        attended_grads.append(results[3])
    both = feed_grads(middles, hidden_grads, cots, denses)
    out_grads = spread(out_grads_pass(attended_grads, scaled), fetch)
    grad_slots, both = lax.optimization_barrier((grad_slots, both))
    both = lax.psum_scatter(both, "batch", scatter_dimension=0, tiled=True)

    bias_sums = jnp.zeros((8, part), F32)
    grads, first_sums, qkv_grads = [], [], []

    def send_back(qkv_grad):
        return [
            deliver(unproject_pass(qkv_grad[slot], head_weights), slot)
            for slot in range(1, slots)
        ]

    def finish_back(group, arrived):
        grad, group_sums = first_back(
            inputs[group],
            qkv_grads[group][0],
            head_weights,
            norm_gains,
            norm_shifts,
            residual_grads[group],
            arrived,
        )
        grads.append(grad)
        first_sums.append(group_sums)

    for group in range(2):
        if group == 1:
            grad_slots[1], qkv_grads[0] = lax.optimization_barrier((grad_slots[1], qkv_grads[0]))
        qkv_grad = []
        outs, totals = saved[group]
        for job, log_total in zip(jobs[group], totals):
            qkv_grad, back_sums = attend_backward(
                me,
                job[0],
                qkv[group],
                outs,
                grad_slots[group],
                scale_lanes,
                log_total,
                qkv_grad,
                *job[1:],
            )
            bias_sums = bias_sums + jnp.sum(back_sums, axis=0).transpose(1, 0, 2).reshape(8, part)
        qkv_grads.append(qkv_grad)
        if group == 0:
            arrived = send_back(qkv_grad)
    weight_grad = head_grads(
        [rows for group in normed_slots for rows in group],
        [piece for group in qkv_grads for piece in group],
        out_grads,
    )
    qkv_grads[1], weight_grad = lax.optimization_barrier((qkv_grads[1], weight_grad))
    arrived_last = send_back(qkv_grads[1])
    finish_back(0, arrived)
    mid_terms = (mid_sums[0] + mid_sums[1])[:3].reshape(3, batches, slots, share)
    mid_terms = turn(mid_terms.transpose(0, 2, 1, 3), me[0])
    norm_sums = sums[0] + sums[1]
    own_sums = lax.dynamic_update_slice(
        jnp.zeros((slots, 3 * part), F32), bias_sums[:3].reshape(1, -1), (me[0], jnp.int32(0))
    )
    shared = jnp.concatenate(
        [norm_sums[1:7].reshape(-1), mid_terms.reshape(-1), own_sums.reshape(-1)]
    ).reshape(-1, LANES)
    axes = (("batch", batches), ("head", slots))
    weight_grad, shared, grads[0] = lax.optimization_barrier((weight_grad, shared, grads[0]))
    summed_weight, summed = batch_sum(weight_grad.reshape(4 * width, part), shared, axes)
    arrived_last, summed_weight, both = lax.optimization_barrier(
        (arrived_last, summed_weight, both)
    )
    summed_weight = summed_weight.reshape(4, width, part)
    both = both.reshape(slots, share, 2 * width)
    both_grads = both[0].astype(F32)
    for slot in range(1, slots):
        both_grads = both_grads + deliver(both[slot], slot).astype(F32)
    finish_back(1, arrived_last)
    late = first_sums[0] + first_sums[1]
    late, both_grads = lax.optimization_barrier((late, both_grads))
    late = small_sum(late[:2].reshape(-1, LANES), axes).reshape(2, width)
    summed = summed.reshape(-1)
    norm_sums, mid_terms, own_sums = jnp.split(
        summed, [6 * width, 6 * width + 3 * mid_gain.shape[0]]
    )
    norm_sums = norm_sums.reshape(6, width)
    mid_terms = mid_terms.reshape(3, -1)
    own_sums = lax.dynamic_slice(
        own_sums.reshape(slots, 3 * part), (me[0], jnp.int32(0)), (1, 3 * part)
    ).reshape(3, part)
    return (
        outputs[1][:short_tokens].reshape(shapes[0]),
        outputs[1][short_tokens:].reshape(shapes[1]),
        outputs[0].reshape(shapes[2]),
        grads[1][:short_tokens].reshape(shapes[0]),
        grads[1][short_tokens:].reshape(shapes[1]),
        grads[0].reshape(shapes[2]),
        jnp.concatenate([late[:1], norm_sums[:2]], 0),
        jnp.concatenate([late[1:], norm_sums[2:]], 0),
        summed_weight[:3].astype(F32),
        own_sums[:2],
        jnp.sum(own_sums[2].reshape(-1, HEAD), axis=1),
        jnp.concatenate(
            [summed_weight[3, at : at + part] for at in range(0, width, part)], 1
        ).astype(F32),
        both_grads[:, width:],
        mid_terms[0],
        jnp.stack([mid_terms[2], mid_terms[1]]),
        both_grads[:, :width],
    )


def solution(mesh):
    in_specs = (
        P("batch", "head", None),
        P("batch", "head", None),
        P("batch", "head", None),
        P("batch"),
        P("batch"),
        P("batch"),
        P("batch", "head", None),
        P("batch", "head", None),
        P("batch", "head", None),
        P(),
        P(),
        P(None, None, "head"),
        P(None, "head"),
        P("head"),
        P("head", None),
        P(("head", "batch"), None),
        P(),
        P(),
        P(("head", "batch"), None),
    )
    out_specs = (
        P("batch", "head", None),
        P("batch", "head", None),
        P("batch", "head", None),
        P("batch", "head", None),
        P("batch", "head", None),
        P("batch", "head", None),
        P(),
        P(),
        P(None, None, "head"),
        P(None, "head"),
        P("head"),
        P("head", None),
        P(("head", "batch"), None),
        P(),
        P(),
        P(("head", "batch"), None),
    )
    return jax.shard_map(
        functools.partial(shards, mesh.shape["head"]),
        mesh=mesh,
        in_specs=in_specs,
        out_specs=out_specs,
        check_vma=False,
    )
```

```python
import functools

import jax
import jax.numpy as jnp
from jax import lax
from jax.experimental import pallas as pl
from jax.experimental.pallas import tpu as pltpu
from jax.sharding import PartitionSpec as P

EPSILON = 1e-05
ROW_PAIRS = (((0,), (0,)), ((), ()))
COLUMN_PAIRS = (((1,), (1,)), ((), ()))
LANES = 128
HEAD = 64
LOG2E = 1.4426950408889634
EXPONENT_SCALE = HEAD ** (-0.5) * LOG2E
MASKED = -1e30
GELU_SCALE = 0.7978845608028654
GELU_CUBE = 0.044715
BF = jnp.bfloat16
F32 = jnp.float32
MESH = pl.DeviceIdType.MESH


def dot(a, b, dims=(((1,), (0,)), ((), ()))):
    return lax.dot_general(a, b, dims, preferred_element_type=F32)


def normalize(value, gain, shift):
    centred = value - jnp.mean(value, axis=-1, keepdims=True)
    inverse = lax.rsqrt(jnp.mean(centred * centred, axis=-1, keepdims=True) + EPSILON)
    unit = centred * inverse
    return (unit * gain + shift, unit, inverse)


def normalize_back(grad, unit, inverse, gain):
    scaled = grad * gain
    inner = (
        scaled
        - jnp.mean(scaled, axis=-1, keepdims=True)
        - unit * jnp.mean(scaled * unit, axis=-1, keepdims=True)
    )
    return (inner * inverse, jnp.sum(grad * unit, axis=0), jnp.sum(grad, axis=0))


def place(me, slot, slots, part):
    return pl.multiple_of(lax.rem(me + slot, slots) * part, part)


def attend_forward_kernel(slots, span, block, kept, me_ref, len_ref, *refs):
    qkv = refs[:slots]
    scale_ref = refs[slots]
    refs = refs[kept:]
    outs = refs[slots + 1 : 2 * slots + 1]
    total_ref = refs[2 * slots + 1]
    query, keys, values, mixed = refs[2 * slots + 2 :]
    part = span // slots
    me = me_ref[0]
    length = len_ref[pl.program_id(0)]
    for slot in range(slots):
        at = pl.ds(place(me, slot, slots, part), part)
        query[at, :] = qkv[slot][:, :LANES]
        keys[at, :] = qkv[slot][:, LANES : 2 * LANES]
        values[at, :] = qkv[slot][:, 2 * LANES :]
    first = lax.broadcasted_iota(jnp.int32, (1, LANES), 1) < HEAD
    for i in range(span // block):
        rows = slice(i * block, (i + 1) * block)
        query_block = query[rows, :]
        halves = []
        for head in range(2):
            mine = first if head == 0 else jnp.logical_not(first)
            query_head = jnp.where(mine, query_block, jnp.zeros_like(query_block))
            scores = []
            for j in range(i + 1):
                key_block = keys[j * block : (j + 1) * block, :]
                score = dot(query_head, key_block, COLUMN_PAIRS)
                key_place = lax.broadcasted_iota(jnp.int32, (block, block), 1)
                allowed = None
                if i == j:
                    allowed = key_place <= lax.broadcasted_iota(jnp.int32, (block, block), 0)
                if (j + 1) * block > span // 2:
                    short = key_place < length - j * block
                    allowed = short if allowed is None else allowed & short
                if allowed is not None:
                    score = jnp.where(allowed, score, MASKED)
                scores.append(score)
            top = functools.reduce(jnp.maximum, scores)
            top = jnp.max(top, axis=-1, keepdims=True) * EXPONENT_SCALE
            weights = [jnp.exp2(score * EXPONENT_SCALE - top) for score in scores]
            total = jnp.sum(functools.reduce(jnp.add, weights), axis=-1, keepdims=True)
            result = None
            for j in range(i + 1):
                term = dot(weights[j].astype(BF), values[j * block : (j + 1) * block, :])
                result = term if result is None else result + term
            halves.append(result / total)
            log_total = jnp.broadcast_to(top + jnp.log2(total), (block, LANES))
            total_ref[0, 0, head : head + 1, rows] = jnp.transpose(log_total)[:1, :]
        mixed[rows, :] = (jnp.where(first, halves[0], halves[1]) * scale_ref[...]).astype(BF)
    for slot in range(slots):
        outs[slot][...] = mixed[pl.ds(place(me, slot, slots, part), part), :]


def attend_backward_kernel(slots, span, block, kept, me_ref, len_ref, *refs):
    qkv = refs[:slots]
    out = refs[slots : 2 * slots]
    grads = refs[2 * slots : 3 * slots]
    scale_ref, total_ref = refs[3 * slots : 3 * slots + 2]
    refs = refs[kept:]
    results = refs[3 * slots + 2 : 4 * slots + 2]
    sums_ref = refs[4 * slots + 2]
    query, keys, values, mixed_grad, product, query_grad, key_grad, value_grad = refs[4 * slots + 3 :]
    part = span // slots
    me = me_ref[0]
    length = len_ref[pl.program_id(0)]
    for slot in range(slots):
        at = pl.ds(place(me, slot, slots, part), part)
        query[at, :] = qkv[slot][:, :LANES]
        keys[at, :] = qkv[slot][:, LANES : 2 * LANES]
        values[at, :] = qkv[slot][:, 2 * LANES :]
        grad = grads[slot][...].astype(F32)
        mixed_grad[at, :] = (grad * scale_ref[...]).astype(BF)
        product[at, :] = grad * out[slot][...].astype(F32)
    first = lax.broadcasted_iota(jnp.int32, (1, LANES), 1) < HEAD
    which = lax.broadcasted_iota(jnp.int32, (8, LANES), 0)
    lane_head = lax.broadcasted_iota(jnp.int32, (8, LANES), 1) // HEAD
    picks = jnp.where(which == lane_head, 1.0, 0.0).astype(BF)
    inner = product[...]
    inner_high = inner.astype(BF)
    inner_low = (inner - inner_high.astype(F32)).astype(BF)
    inner_sum = dot(picks, inner_high, COLUMN_PAIRS) + dot(picks, inner_low, COLUMN_PAIRS)
    scale_sum = jnp.sum(inner, axis=0, keepdims=True) / scale_ref[...]
    count = span // block

    def tile(head, keys_from, keys_to, start, stop, key_head, value_head, key_turned):
        rows = slice(start, stop)
        query_block, grad_block = query[rows, :], mixed_grad[rows, :]
        score = dot(key_head, query_block, COLUMN_PAIRS)
        shares = jnp.exp2(score * EXPONENT_SCALE - total_ref[0, 0, head : head + 1, rows])
        key_place = keys_from + lax.broadcasted_iota(jnp.int32, score.shape, 0)
        allowed = None
        if start < keys_to:
            allowed = key_place <= start + lax.broadcasted_iota(jnp.int32, score.shape, 1)
        if keys_to > span // 2:
            short = key_place < length
            allowed = short if allowed is None else allowed & short
        if allowed is not None:
            shares = jnp.where(allowed, shares, 0.0)
        share_grad = dot(value_head, grad_block, COLUMN_PAIRS)
        score_grad = shares * (share_grad - inner_sum[head : head + 1, rows])
        score_grad = score_grad.astype(BF)
        value_term = dot(shares.astype(BF), grad_block)
        key_term = dot(score_grad, query_block)
        return value_term, key_term, dot(key_turned, score_grad)

    query_grad[...] = jnp.zeros_like(query_grad)
    for j in range(count):
        at = j * block
        cols = slice(at, at + block)
        key_block, value_block = keys[cols, :], values[cols, :]
        heads = []
        for head in range(2):
            mine = first if head == 0 else jnp.logical_not(first)
            key_head = jnp.where(mine, key_block, jnp.zeros_like(key_block))
            value_head = jnp.where(mine, value_block, jnp.zeros_like(value_block))
            key_turned = jnp.transpose(key_head.astype(F32)).astype(BF)
            heads.append((key_head, value_head, key_turned))
        sums = [None, None]
        half = block // 2

        def one(head, i):
            key_head, value_head, key_turned = heads[head]
            if i == j and True:
                parts = []
                for low, high in ((0, half), (half, block)):
                    value_term, key_term, query_term = tile(
                        head, at + low, at + high, at + low, at + block,
                        key_head[low:high], value_head[low:high], key_turned[:, low:high],
                    )
                    query_grad[:, at + low : at + block] += query_term
                    parts.append((value_term, key_term))
                terms = [jnp.concatenate(pair, 0) for pair in zip(*parts)]
            else:
                start = i * block
                value_term, key_term, query_term = tile(
                    head, at, at + block, start, start + block, key_head, value_head, key_turned
                )
                query_grad[:, start : start + block] += query_term
                terms = [value_term, key_term]
            if sums[head] is None:
                sums[head] = terms
            else:
                sums[head] = [x + y for x, y in zip(sums[head], terms)]

        for head in range(2):
            for i in range(j, count):
                one(head, i)
        value_grad[cols, :] = jnp.where(first, sums[0][0], sums[1][0]).astype(BF)
        key_grad[cols, :] = (jnp.where(first, sums[0][1], sums[1][1]) * HEAD ** (-0.5)).astype(BF)
    product[...] = jnp.transpose(query_grad[...])
    query_sum = value_sum = jnp.zeros((1, LANES), F32)
    for slot in range(slots):
        at = pl.ds(place(me, slot, slots, part), part)
        piece = (product[at, :] * HEAD ** (-0.5)).astype(BF)
        results[slot][:, :LANES] = piece
        results[slot][:, LANES : 2 * LANES] = key_grad[at, :]
        results[slot][:, 2 * LANES :] = value_grad[at, :]
        query_sum += jnp.sum(piece.astype(F32), axis=0, keepdims=True)
        value_sum += jnp.sum(value_grad[at, :].astype(F32), axis=0, keepdims=True)
    sums_ref[0, 0, 0:1, :] = query_sum
    sums_ref[0, 0, 1:2, :] = value_sum
    sums_ref[0, 0, 2:3, :] = scale_sum
    sums_ref[0, 0, 3:, :] = jnp.zeros((5, LANES), F32)


def attention_specs(slots, span, first_block, width):
    part = span // slots
    return pl.BlockSpec((part, width), lambda r, p, *_: (first_block + r, p))


def attend_forward(me, lengths, qkv, scale_lanes, kept, rows, span, first_block):
    slots = len(qkv)
    tokens = qkv[0].shape[0]
    pairs = qkv[0].shape[1] // (3 * LANES)
    block = min(512, span)
    call = pl.pallas_call(
        functools.partial(attend_forward_kernel, slots, span, block, len(kept)),
        grid_spec=pltpu.PrefetchScalarGridSpec(
            num_scalar_prefetch=2,
            grid=(rows, pairs),
            in_specs=[attention_specs(slots, span, first_block, 3 * LANES)] * slots
            + [pl.BlockSpec((1, LANES), lambda r, p, *_: (0, p))]
            + [pl.BlockSpec(memory_space=pl.ANY)] * len(kept),
            out_specs=[attention_specs(slots, span, first_block, LANES)] * slots
            + [pl.BlockSpec((1, 1, 2, span), lambda r, p, *_: (p, r, 0, 0))],
            scratch_shapes=[pltpu.VMEM((span, LANES), BF)] * 4,
        ),
        out_shape=[jax.ShapeDtypeStruct((tokens, pairs * LANES), BF)] * slots
        + [jax.ShapeDtypeStruct((pairs, rows, 2, span), F32)],
        input_output_aliases={3 + slots + k: k for k in range(len(kept))},
        compiler_params=pltpu.CompilerParams(vmem_limit_bytes=56 * 2**20),
        name="attend_forward",
    )
    *outs, log_total = call(me, lengths, *qkv, scale_lanes, *kept)
    return outs, log_total


def attend_backward(
    me, lengths, qkv, outs, grads, scale_lanes, log_total, kept, rows, span, first_block
):
    slots = len(qkv)
    tokens = qkv[0].shape[0]
    pairs = qkv[0].shape[1] // (3 * LANES)
    block = min(512, span)
    call = pl.pallas_call(
        functools.partial(attend_backward_kernel, slots, span, block, len(kept)),
        grid_spec=pltpu.PrefetchScalarGridSpec(
            num_scalar_prefetch=2,
            grid=(rows, pairs),
            in_specs=[attention_specs(slots, span, first_block, 3 * LANES)] * slots
            + [attention_specs(slots, span, first_block, LANES)] * (2 * slots)
            + [
                pl.BlockSpec((1, LANES), lambda r, p, *_: (0, p)),
                pl.BlockSpec((1, 1, 2, span), lambda r, p, *_: (p, r, 0, 0)),
            ]
            + [pl.BlockSpec(memory_space=pl.ANY)] * len(kept),
            out_specs=[attention_specs(slots, span, first_block, 3 * LANES)] * slots
            + [pl.BlockSpec((1, 1, 8, LANES), lambda r, p, *_: (r, p, 0, 0))],
            scratch_shapes=[pltpu.VMEM((span, LANES), BF)] * 4
            + [pltpu.VMEM((span, LANES), F32), pltpu.VMEM((LANES, span), F32)]
            + [pltpu.VMEM((span, LANES), BF)] * 2,
        ),
        out_shape=[jax.ShapeDtypeStruct((tokens, pairs * 3 * LANES), BF)] * slots
        + [jax.ShapeDtypeStruct((rows, pairs, 8, LANES), F32)],
        input_output_aliases={4 + 3 * slots + k: k for k in range(len(kept))},
        compiler_params=pltpu.CompilerParams(vmem_limit_bytes=56 * 2**20),
        name="attend_backward",
    )
    *results, sums = call(me, lengths, *qkv, *outs, *grads, scale_lanes, log_total, *kept)
    return results, sums


def fold(value):
    return functools.reduce(
        jnp.add, [value[:, k : k + LANES] for k in range(0, value.shape[1], LANES)]
    )


def row_sum(value):
    return jnp.sum(value, axis=-1, keepdims=True)


def column_sum(value):
    return jnp.sum(value, axis=0, keepdims=True)


def middle_kernel(slots, chunk, *refs):
    rows_ref, cot_ref = refs[:2]
    scaled = refs[2 : 2 + slots]
    out_weights = refs[2 + slots : 2 + 2 * slots]
    feed_ref, gains, shifts, mid_gain, mid_shifts = refs[2 + 2 * slots : 7 + 2 * slots]
    results = refs[7 + 2 * slots :]
    out_ref, residual_grad_ref, dense_ref, attended_grad_ref = results[:4]
    middle_ref, hidden_grad_ref, sums_ref, mid_sums_ref = results[4:8]
    scaled_grads = results[8 : 8 + slots]
    gelu_ref, slope_ref, grad_ref = results[8 + slots :]

    @pl.when(pl.program_id(0) == 0)
    def _():
        sums_ref[...] = jnp.zeros_like(sums_ref)
        mid_sums_ref[...] = jnp.zeros_like(mid_sums_ref)

    attended = shifts[3:4, :]
    for rows, matrix in zip(scaled, out_weights):
        attended = attended + dot(rows[...], matrix[...]).astype(BF).astype(F32)
    post, post_unit, post_inverse = normalize(attended, gains[1:2, :], shifts[1:2, :])
    residual = rows_ref[...].astype(F32) + post
    dense, dense_unit, dense_inverse = normalize(residual, gains[2:3, :], shifts[2:3, :])
    dense = dense.astype(BF)
    dense_ref[...] = dense
    cotangent = cot_ref[...]
    total = mid_gain.shape[1]

    def up(start):
        return feed_ref[2 * start : 2 * start + chunk, :]

    def down(start):
        return feed_ref[2 * start + chunk : 2 * start + 2 * chunk, :]

    base = first = second = third = fourth = None
    for start in range(0, total, chunk):
        cols = slice(start, start + chunk)
        hidden = dot(dense, up(start), COLUMN_PAIRS) + mid_shifts[0:1, cols]
        square = hidden * hidden
        bent = jnp.tanh(hidden * (GELU_SCALE + GELU_SCALE * GELU_CUBE * square))
        half = 0.5 * hidden
        active = half + half * bent
        slope = (0.5 + 0.5 * bent) + (half * (1.0 - bent * bent)) * (
            GELU_SCALE + 3.0 * GELU_SCALE * GELU_CUBE * square
        )
        grad = dot(cotangent, down(start), COLUMN_PAIRS)
        gelu_ref[:, cols] = active
        slope_ref[:, cols] = slope
        grad_ref[:, cols] = grad
        if base is None:
            base = row_sum(fold(active)) / chunk
        away = active - base
        weighted = grad * mid_gain[:, cols]
        terms = [fold(away), fold(away * away), fold(weighted), fold(weighted * away)]
        if first is None:
            first, second, third, fourth = terms
        else:
            first, second, third, fourth = [
                a + b for a, b in zip((first, second, third, fourth), terms)
            ]
    offset = row_sum(first) / total
    mean = base + offset
    inverse = lax.rsqrt(jnp.maximum(row_sum(second) / total - offset * offset, 0.0) + EPSILON)
    grad_mean = row_sum(third) / total
    grad_unit = inverse * (row_sum(fourth) / total - offset * grad_mean)
    branch = dense_grad = None
    for start in range(0, total, chunk):
        cols = slice(start, start + chunk)
        unit = (gelu_ref[:, cols] - mean) * inverse
        gain = mid_gain[:, cols]
        middle = (unit * gain + mid_shifts[1:2, cols]).astype(BF)
        middle_ref[:, cols] = middle
        term = dot(middle, down(start))
        branch = term if branch is None else branch + term
        grad = grad_ref[:, cols]
        inner = inverse * (grad * gain - grad_mean - unit * grad_unit)
        hidden_grad = (inner * slope_ref[:, cols]).astype(BF)
        hidden_grad_ref[:, cols] = hidden_grad
        mid_sums_ref[0:1, cols] += column_sum(grad * unit)
        mid_sums_ref[1:2, cols] += column_sum(grad)
        mid_sums_ref[2:3, cols] += column_sum(hidden_grad.astype(F32))
        term = dot(hidden_grad, up(start))
        dense_grad = term if dense_grad is None else dense_grad + term
    out_ref[...] = (residual + branch + shifts[4:5, :]).astype(BF)
    cot_wide = cotangent.astype(F32)

    def back(grad, unit, inverse, row):
        scaled = grad * gains[row : row + 1, :]
        inner = (
            scaled
            - jnp.mean(scaled, axis=-1, keepdims=True)
            - unit * jnp.mean(scaled * unit, axis=-1, keepdims=True)
        )
        sums_ref[row : row + 1, :] += column_sum(grad * unit)
        sums_ref[row + 2 : row + 3, :] += column_sum(grad)
        return inner * inverse

    residual_grad = cot_wide + back(dense_grad, dense_unit, dense_inverse, 2)
    residual_grad_ref[...] = residual_grad.astype(BF)
    attended_grad = back(residual_grad, post_unit, post_inverse, 1)
    sums_ref[5:6, :] += column_sum(attended_grad)
    sums_ref[6:7, :] += column_sum(cot_wide)
    attended_grad = attended_grad.astype(BF)
    attended_grad_ref[...] = attended_grad
    for result, matrix in zip(scaled_grads, out_weights):
        result[...] = dot(attended_grad, matrix[...], COLUMN_PAIRS).astype(BF)


def middle_pass(
    chunk, rows, cotangent, scaled, out_weights, feed, gains, shifts, mid_gain, mid_shifts
):
    slots = len(scaled)
    tokens, width = rows.shape
    part = scaled[0].shape[1]
    hidden = mid_gain.shape[1]
    block = min(256, tokens)

    def tiles(columns):
        return pl.BlockSpec((block, columns), lambda i: (i, 0))

    def whole(array):
        return pl.BlockSpec(array.shape, lambda i: (0, 0), pipeline_mode=pl.Buffered(1))

    call = pl.pallas_call(
        functools.partial(middle_kernel, slots, chunk),
        grid=(tokens // block,),
        in_specs=[tiles(width), tiles(width)]
        + [tiles(part)] * slots
        + [whole(item) for item in (*out_weights, feed, gains, shifts, mid_gain, mid_shifts)],
        out_specs=[tiles(width)] * 4
        + [tiles(hidden)] * 2
        + [pl.BlockSpec((8, width), lambda i: (0, 0)), pl.BlockSpec((8, hidden), lambda i: (0, 0))]
        + [tiles(part)] * slots,
        out_shape=[
            jax.ShapeDtypeStruct((tokens, width), BF),
            jax.ShapeDtypeStruct((tokens, width), BF),
            jax.ShapeDtypeStruct((tokens, width), BF),
            jax.ShapeDtypeStruct((tokens, width), BF),
            jax.ShapeDtypeStruct((tokens, hidden), BF),
            jax.ShapeDtypeStruct((tokens, hidden), BF),
            jax.ShapeDtypeStruct((8, width), F32),
            jax.ShapeDtypeStruct((8, hidden), F32),
        ]
        + [jax.ShapeDtypeStruct((tokens, part), BF)] * slots,
        scratch_shapes=[pltpu.VMEM((block, hidden), F32)] * 3,
        compiler_params=pltpu.CompilerParams(vmem_limit_bytes=60 * 2**20),
        name="middle_pass",
    )
    return call(rows, cotangent, *scaled, *out_weights, feed, gains, shifts, mid_gain, mid_shifts)


def feed_grads_kernel(groups, *refs):
    middles, hidden_grads = refs[:groups], refs[groups : 2 * groups]
    cots, denses = refs[2 * groups : 3 * groups], refs[3 * groups : 4 * groups]
    result = refs[4 * groups]
    width = cots[0].shape[1]
    for at, lefts, rights in ((0, middles, cots), (width, hidden_grads, denses)):
        total = functools.reduce(
            jnp.add, [dot(a[...], b[...], ROW_PAIRS) for a, b in zip(lefts, rights)]
        )
        result[:, at : at + width] = total.astype(BF)


def feed_grads(middles, hidden_grads, cots, denses):
    groups = len(middles)
    hidden, width = middles[0].shape[1], cots[0].shape[1]
    block = min(256, hidden)

    def columns(array):
        return pl.BlockSpec((array.shape[0], block), lambda i: (0, i))

    def whole(array):
        return pl.BlockSpec(array.shape, lambda i: (0, 0), pipeline_mode=pl.Buffered(1))

    return pl.pallas_call(
        functools.partial(feed_grads_kernel, groups),
        grid=(hidden // block,),
        in_specs=[columns(item) for item in (*middles, *hidden_grads)]
        + [whole(item) for item in (*cots, *denses)],
        out_specs=pl.BlockSpec((block, 2 * width), lambda i: (i, 0)),
        out_shape=jax.ShapeDtypeStruct((hidden, 2 * width), BF),
        compiler_params=pltpu.CompilerParams(vmem_limit_bytes=56 * 2**20),
        name="feed_grads",
    )(*middles, *hidden_grads, *cots, *denses)


def head_grads_kernel(count, *refs):
    rows, grads = refs[:count], refs[count : 2 * count]
    *out_grads, result, total = refs[2 * count :]

    @pl.when(pl.program_id(0) == 0)
    def _():
        total[...] = jnp.zeros_like(total)

    wide = 2 * LANES
    for at in range(0, total.shape[1], wide):
        cols = slice(at, at + wide)
        total[:, cols] += functools.reduce(
            jnp.add,
            [dot(left[...], right[:, cols], ROW_PAIRS) for left, right in zip(rows, grads)],
        )

    @pl.when(pl.program_id(0) == pl.num_programs(0) - 1)
    def _():
        for at in range(0, total.shape[1], LANES):
            pair, kind = divmod(at // LANES, 3)
            result[kind, :, pair * LANES : (pair + 1) * LANES] = total[:, at : at + LANES].astype(BF)
        part, width = out_grads[0].shape
        out_grad = functools.reduce(jnp.add, [item[...].astype(F32) for item in out_grads])
        for at in range(0, width, part):
            result[3, at : at + part, :] = out_grad[:, at : at + part].astype(BF)


def head_grads(rows, grads, out_grads):
    tokens, width = rows[0].shape
    columns = grads[0].shape[1]
    block = min(512, tokens)
    return pl.pallas_call(
        functools.partial(head_grads_kernel, len(rows)),
        grid=(tokens // block,),
        in_specs=[pl.BlockSpec((block, width), lambda i: (i, 0))] * len(rows)
        + [pl.BlockSpec((block, columns), lambda i: (i, 0))] * len(grads)
        + [pl.BlockSpec(item.shape, lambda i: (0, 0)) for item in out_grads],
        out_specs=pl.BlockSpec((4, width, columns // 3), lambda i: (0, 0, 0)),
        out_shape=jax.ShapeDtypeStruct((4, width, columns // 3), BF),
        scratch_shapes=[pltpu.VMEM((width, columns), F32)],
        compiler_params=pltpu.CompilerParams(vmem_limit_bytes=56 * 2**20),
        name="head_grads",
    )(*rows, *grads, *out_grads)


def partner(name, bit):
    me = lax.axis_index(name)
    mine = lax.rem(me // (1 << bit), 2)
    return mine, {name: me + (1 - 2 * mine) * (1 << bit)}


def greet(places):
    barrier = pltpu.get_barrier_semaphore()
    for place_of in places:
        pl.semaphore_signal(barrier, inc=1, device_id=place_of, device_id_type=MESH)
    pl.semaphore_wait(barrier, len(places))


def batch_sum_kernel(bits, chunks, steps, source, extra, result, extra_result, *refs):
    levels, arrivals = refs[:bits], refs[bits : 2 * bits]
    extra_totals, extra_arrivals = refs[2 * bits : 2 * bits + 2]
    send_sems, recv_sems, extra_send_sems, extra_recv_sems = refs[2 * bits + 2 :]
    rows = source.shape[0] // chunks
    partners = [partner("batch", bit) for bit in range(bits)]
    extra_partners = [partner(name, bit)[1] for name, bit in steps]
    greet(extra_partners)
    offsets, offset = [], 0
    for bit in range(bits):
        offset = offset + partners[bit][0] * (rows >> (bit + 1))
        offsets.append(offset)

    def aligned(value, size):
        return pl.ds(pl.multiple_of(value, size), size)

    def piece(chunk, bit, mine):
        size = rows >> (bit + 1)
        if bit == 0:
            return source.at[aligned(chunk * rows + mine * size, size), :]
        return levels[bit - 1].at[chunk, aligned(mine * size, size), :]

    def final(chunk, bit):
        return result.at[aligned(chunk * rows + offsets[bit], rows >> (bit + 1)), :]

    copies = {}

    def start(chunk, stage):
        if stage < bits:
            mine, other = partners[stage]
            here, there = piece(chunk, stage, 1 - mine), arrivals[stage].at[chunk]
        else:
            bit = 2 * bits - 1 - stage
            other = partners[bit][1]
            here = there = final(chunk, bit)
        copies[chunk, stage] = pltpu.make_async_remote_copy(
            src_ref=here,
            dst_ref=there,
            send_sem=send_sems.at[chunk, stage],
            recv_sem=recv_sems.at[chunk, stage],
            device_id=other,
            device_id_type=MESH,
        )
        copies[chunk, stage].start()

    def finish(chunk, stage):
        copies[chunk, stage].wait_recv()
        if stage < bits:
            kept = piece(chunk, stage, partners[stage][0])[...].astype(F32)
            total = (kept + arrivals[stage][chunk].astype(F32)).astype(BF)
            if stage == bits - 1:
                final(chunk, stage)[...] = total
            else:
                levels[stage][chunk] = total

    def extra_total(step):
        if step == 0:
            return extra
        return extra_result if step == len(steps) else extra_totals.at[step - 1]

    def extra_copy(step):
        return pltpu.make_async_remote_copy(
            src_ref=extra_total(step),
            dst_ref=extra_arrivals.at[step],
            send_sem=extra_send_sems.at[step],
            recv_sem=extra_recv_sems.at[step],
            device_id=extra_partners[step],
            device_id_type=MESH,
        )

    extra_copies = []
    for tick in range(max(chunks + 2 * bits, len(steps) + 1)):
        if 0 < tick <= len(steps):
            extra_copies[tick - 1].wait_recv()
            extra_total(tick)[...] = extra_total(tick - 1)[...] + extra_arrivals[tick - 1]
        if tick < len(steps):
            extra_copies.append(extra_copy(tick))
            extra_copies[tick].start()
        for chunk in range(chunks):
            stage = tick - chunk
            if 0 < stage <= 2 * bits:
                finish(chunk, stage - 1)
            if 0 <= stage < 2 * bits:
                start(chunk, stage)
    for copy in (*copies.values(), *extra_copies):
        copy.wait_send()


def halving_steps(axes):
    return [(name, bit) for name, size in axes for bit in range(size.bit_length() - 1)]


def batch_sum(value, extra, axes):
    bits = axes[0][1].bit_length() - 1
    if bits == 0 or any(size & (size - 1) for _, size in axes):
        return lax.psum(value, "batch"), lax.psum(extra, tuple(name for name, _ in axes))
    steps = halving_steps(axes)
    rows, columns = value.shape
    chunks = 4
    halves = [
        pltpu.VMEM((chunks, rows // chunks >> (bit + 1), columns), BF) for bit in range(bits)
    ]
    return pl.pallas_call(
        functools.partial(batch_sum_kernel, bits, chunks, steps),
        in_specs=[pl.BlockSpec(memory_space=pltpu.VMEM)] * 2,
        out_specs=[pl.BlockSpec(memory_space=pltpu.VMEM)] * 2,
        out_shape=[
            jax.ShapeDtypeStruct(value.shape, BF),
            jax.ShapeDtypeStruct(extra.shape, F32),
        ],
        scratch_shapes=halves * 2
        + [pltpu.VMEM((len(steps), *extra.shape), F32)] * 2
        + [pltpu.SemaphoreType.DMA((chunks, 2 * bits))] * 2
        + [pltpu.SemaphoreType.DMA((len(steps),))] * 2,
        compiler_params=pltpu.CompilerParams(
            collective_id=0, has_side_effects=True, vmem_limit_bytes=40 * 2**20
        ),
        name="batch_sum",
    )(value, extra)


def small_sum_kernel(steps, source, result, *refs):
    totals, arrivals = refs[:-2][: len(steps) - 1], refs[:-2][len(steps) - 1 :]
    send_sems, recv_sems = refs[-2:]
    partners = [partner(name, bit)[1] for name, bit in steps]
    greet(partners)
    here = source
    copies = []
    for step, other in enumerate(partners):
        copy = pltpu.make_async_remote_copy(
            src_ref=here,
            dst_ref=arrivals[step],
            send_sem=send_sems.at[step],
            recv_sem=recv_sems.at[step],
            device_id=other,
            device_id_type=MESH,
        )
        copy.start()
        copies.append(copy)
        copy.wait_recv()
        there = result if step == len(partners) - 1 else totals[step]
        there[...] = here[...] + arrivals[step][...]
        here = there
    for copy in copies:
        copy.wait_send()


def small_sum(value, axes):
    steps = halving_steps(axes)
    if not steps or any(size & (size - 1) for _, size in axes):
        return lax.psum(value, tuple(name for name, _ in axes))
    return pl.pallas_call(
        functools.partial(small_sum_kernel, steps),
        in_specs=[pl.BlockSpec(memory_space=pltpu.VMEM)],
        out_specs=pl.BlockSpec(memory_space=pltpu.VMEM),
        out_shape=jax.ShapeDtypeStruct(value.shape, F32),
        scratch_shapes=[pltpu.VMEM(value.shape, F32)] * (2 * len(steps) - 1)
        + [pltpu.SemaphoreType.DMA((len(steps),))] * 2,
        compiler_params=pltpu.CompilerParams(
            collective_id=1, has_side_effects=True, vmem_limit_bytes=40 * 2**20
        ),
        name="small_sum",
    )(value)


def unproject(grads, weights):
    total = None
    for kind in range(3):
        pieces = [
            grads[:, at : at + LANES] for at in range(kind * LANES, grads.shape[1], 3 * LANES)
        ]
        piece = pieces[0] if len(pieces) == 1 else jnp.concatenate(pieces, 1)
        term = dot(piece, weights[kind], COLUMN_PAIRS)
        total = term if total is None else total + term
    return total.astype(BF)


def unproject_kernel(grads, weights, result):
    result[...] = unproject(grads, weights)


def unproject_pass(grads, weights):
    tokens, columns = grads.shape
    width = weights.shape[1]
    block = min(256, tokens)
    return pl.pallas_call(
        unproject_kernel,
        grid=(tokens // block,),
        in_specs=[
            pl.BlockSpec((block, columns), lambda i: (i, 0)),
            pl.BlockSpec(weights.shape, lambda i: (0, 0, 0), pipeline_mode=pl.Buffered(1)),
        ],
        out_specs=pl.BlockSpec((block, width), lambda i: (i, 0)),
        out_shape=jax.ShapeDtypeStruct((tokens, width), BF),
        compiler_params=pltpu.CompilerParams(vmem_limit_bytes=40 * 2**20),
        name="unproject",
    )(grads, weights)


def out_grads_kernel(groups, slots, *refs):
    grads, scaled, results = refs[:groups], refs[groups:-slots], refs[-slots:]
    for slot, result in enumerate(results):
        total = functools.reduce(
            jnp.add,
            [
                dot(scaled[group * slots + slot][...], grads[group][...], ROW_PAIRS)
                for group in range(groups)
            ],
        )
        result[...] = total.astype(BF)


def out_grads_pass(grads, scaled):
    slots = len(scaled[0])
    part, width = scaled[0][0].shape[1], grads[0].shape[1]
    items = [*grads, *[item for group in scaled for item in group]]
    return pl.pallas_call(
        functools.partial(out_grads_kernel, len(grads), slots),
        in_specs=[pl.BlockSpec(memory_space=pltpu.VMEM)] * len(items),
        out_specs=[pl.BlockSpec(memory_space=pltpu.VMEM)] * slots,
        out_shape=[jax.ShapeDtypeStruct((part, width), BF)] * slots,
        compiler_params=pltpu.CompilerParams(vmem_limit_bytes=40 * 2**20),
        name="out_grads",
    )(*items)


def first_back_kernel(count, rows_ref, grad_ref, weights, gains, shifts, residual_ref, *refs):
    arrived = refs[:count]
    result, sums_ref = refs[count:]

    @pl.when(pl.program_id(0) == 0)
    def _():
        sums_ref[...] = jnp.zeros_like(sums_ref)

    grad = unproject(grad_ref, weights).astype(F32)
    for term in arrived:
        grad = grad + term[...].astype(F32)
    gain = gains[0:1, :]
    _, unit, inverse = normalize(rows_ref[...].astype(F32), gain, shifts[0:1, :])
    scaled = grad * gain
    inner = (
        scaled
        - jnp.mean(scaled, axis=-1, keepdims=True)
        - unit * jnp.mean(scaled * unit, axis=-1, keepdims=True)
    )
    sums_ref[0:1, :] += column_sum(grad * unit)
    sums_ref[1:2, :] += column_sum(grad)
    result[...] = (residual_ref[...].astype(F32) + inner * inverse).astype(BF)


def first_back(rows, qkv_grad, weights, gains, shifts, residual_grad, arrived):
    tokens, width = rows.shape
    block = min(256, tokens)

    def tiles(columns):
        return pl.BlockSpec((block, columns), lambda i: (i, 0))

    def whole(array):
        zeros = (0,) * array.ndim
        return pl.BlockSpec(array.shape, lambda i: zeros, pipeline_mode=pl.Buffered(1))

    return pl.pallas_call(
        functools.partial(first_back_kernel, len(arrived)),
        grid=(tokens // block,),
        in_specs=[
            tiles(width),
            tiles(qkv_grad.shape[1]),
            whole(weights),
            whole(gains),
            whole(shifts),
            tiles(width),
        ]
        + [tiles(width)] * len(arrived),
        out_specs=[tiles(width), pl.BlockSpec((8, width), lambda i: (0, 0))],
        out_shape=[
            jax.ShapeDtypeStruct((tokens, width), BF),
            jax.ShapeDtypeStruct((8, width), F32),
        ],
        compiler_params=pltpu.CompilerParams(vmem_limit_bytes=40 * 2**20),
        name="first_back",
    )(rows, qkv_grad, weights, gains, shifts, residual_grad, *arrived)


def project_kernel(rows_ref, weights, biases, result):
    rows = rows_ref[...]
    for kind in range(3):
        value = (dot(rows, weights[kind]) + biases[kind : kind + 1, :]).astype(BF)
        for pair in range(value.shape[1] // LANES):
            at = (3 * pair + kind) * LANES
            result[:, at : at + LANES] = value[:, pair * LANES : (pair + 1) * LANES]


def project(rows, weights, biases):
    tokens, width = rows.shape
    columns = 3 * weights.shape[2]
    block = min(256, tokens)
    return pl.pallas_call(
        project_kernel,
        grid=(tokens // block,),
        in_specs=[
            pl.BlockSpec((block, width), lambda i: (i, 0)),
            pl.BlockSpec(weights.shape, lambda i: (0, 0, 0), pipeline_mode=pl.Buffered(1)),
            pl.BlockSpec(biases.shape, lambda i: (0, 0), pipeline_mode=pl.Buffered(1)),
        ],
        out_specs=pl.BlockSpec((block, columns), lambda i: (i, 0)),
        out_shape=jax.ShapeDtypeStruct((tokens, columns), BF),
        compiler_params=pltpu.CompilerParams(vmem_limit_bytes=40 * 2**20),
        name="project",
    )(rows, weights, biases)


def shards(
    slots,
    short_rows,
    medium_rows,
    long_rows,
    short_len,
    medium_len,
    long_len,
    short_cotangent,
    medium_cotangent,
    long_cotangent,
    norm_gains,
    norm_shifts,
    head_weights,
    head_biases,
    head_scale,
    out_weight,
    up_weight,
    mid_gain,
    mid_shifts,
    down_weight,
):
    shapes = tuple((item.shape for item in (short_rows, medium_rows, long_rows)))
    width = short_rows.shape[2]
    part = head_weights.shape[2]
    me = lax.axis_index("head").astype(jnp.int32).reshape(1)

    def fetch(value, slot):
        return lax.ppermute(value, "head", [((d + slot) % slots, d) for d in range(slots)])

    def deliver(value, slot):
        return lax.ppermute(value, "head", [(d, (d + slot) % slots) for d in range(slots)])

    def deliver_shared(value, slot):
        size = lax.axis_size("batch")
        half = value.shape[0] // 2
        if size % 2 or half % 16:
            return deliver(value, slot)
        odd = lax.rem(lax.axis_index("batch"), 2).astype(jnp.int32)
        mine = deliver(lax.dynamic_slice_in_dim(value, odd * half, half, 0), slot)
        other = lax.ppermute(mine, "batch", [(d, d ^ 1) for d in range(size)])
        return jnp.where(
            odd == 0, jnp.concatenate([mine, other], 0), jnp.concatenate([other, mine], 0)
        )

    def spread(own, move):
        return [own[slot] if slot == 0 else move(own[slot], slot) for slot in range(slots)]

    def grouped(short, medium, long):
        return [
            long.reshape(-1, width),
            jnp.concatenate([short.reshape(-1, width), medium.reshape(-1, width)], 0),
        ]

    inputs = grouped(short_rows, medium_rows, long_rows)
    cots = grouped(short_cotangent, medium_cotangent, long_cotangent)
    short_tokens = shapes[0][0] * shapes[0][1]
    spans = tuple(shape[1] * slots for shape in shapes)
    counts = tuple(shape[0] for shape in shapes)
    long_job = (long_len, counts[2], spans[2], 0)
    short_job = (short_len, counts[0], spans[0], 0)
    medium_job = (medium_len, counts[1], spans[1], short_tokens // shapes[1][1])
    jobs = ([long_job], [short_job, medium_job])

    biases = jnp.stack([head_biases[0], jnp.zeros_like(head_biases[0]), head_biases[1]])
    scale_lanes = jnp.repeat(head_scale, HEAD).reshape(1, part)

    share = up_weight.shape[0]
    batches = mid_gain.shape[0] // (slots * share)
    own_feed = jnp.stack([up_weight, down_weight])
    feed_slots = [own_feed] + [fetch(own_feed, slot) for slot in range(1, slots)]
    feed = jnp.stack(feed_slots, 1).reshape(2 * slots * share, width)

    def turn(values, places):
        return jnp.roll(values, places, axis=1)

    mid_rows = jnp.concatenate([mid_gain[None], mid_shifts], 0).reshape(3, slots, batches, share)
    mid_rows = turn(mid_rows, -me[0]).transpose(0, 2, 1, 3).reshape(3, -1)

    lows = []
    for rows in inputs:
        value, _, _ = normalize(rows.astype(F32), norm_gains[0], norm_shifts[0])
        lows.append(value.astype(BF))
    lows[0], feed = lax.optimization_barrier((lows[0], feed))
    feed = lax.all_gather(feed, "batch", axis=0, tiled=True)
    own_qkv = [project(rows, head_weights, biases) for rows in lows]
    arrived = [fetch(lows[0], slot) for slot in range(1, slots)]
    own_qkv, arrived, lows[1], inputs[1], cots[1] = lax.optimization_barrier(
        (own_qkv, arrived, lows[1], inputs[1], cots[1])
    )
    normed_slots = [
        [lows[0], *arrived],
        [lows[1]] + [fetch(lows[1], slot) for slot in range(1, slots)],
    ]
    qkv, saved, scaled = [], [], []
    for group in range(2):
        projected = [own_qkv[group]]
        projected += [project(rows, head_weights, biases) for rows in normed_slots[group][1:]]
        qkv.append(projected)
        outs, totals = [], []
        for job in jobs[group]:
            outs, log_total = attend_forward(me, job[0], projected, scale_lanes, outs, *job[1:])
            totals.append(log_total)
        saved.append((outs, totals))
        if group == 0:
            outs, other_weight = lax.optimization_barrier((outs, out_weight))
            out_weights = [out_weight] + [
                deliver_shared(other_weight, slot) for slot in range(1, slots)
            ]
        scaled.append(spread(outs, deliver))

    outputs, residual_grads, grad_slots, sums, mid_sums, attended_grads = [], [], [], [], [], []
    middles, hidden_grads, denses = [], [], []
    for group in range(2):
        results = middle_pass(
            slots * share,
            inputs[group],
            cots[group],
            scaled[group],
            out_weights,
            feed,
            norm_gains,
            norm_shifts,
            mid_rows[:1],
            mid_rows[1:],
        )
        outputs.append(results[0])
        residual_grads.append(results[1])
        denses.append(results[2])
        middles.append(results[4])
        hidden_grads.append(results[5])
        sums.append(results[6])
        mid_sums.append(results[7])
        grad_slots.append(spread(results[8:], fetch))
        attended_grads.append(results[3])
    both = feed_grads(middles, hidden_grads, cots, denses)
    out_grads = spread(out_grads_pass(attended_grads, scaled), fetch)
    grad_slots, both = lax.optimization_barrier((grad_slots, both))
    both = lax.psum_scatter(both, "batch", scatter_dimension=0, tiled=True)

    bias_sums = jnp.zeros((8, part), F32)
    grads, first_sums, qkv_grads = [], [], []

    def send_back(qkv_grad):
        return [
            deliver(unproject_pass(qkv_grad[slot], head_weights), slot)
            for slot in range(1, slots)
        ]

    def finish_back(group, arrived):
        grad, group_sums = first_back(
            inputs[group],
            qkv_grads[group][0],
            head_weights,
            norm_gains,
            norm_shifts,
            residual_grads[group],
            arrived,
        )
        grads.append(grad)
        first_sums.append(group_sums)

    for group in range(2):
        if group == 1:
            grad_slots[1], qkv_grads[0] = lax.optimization_barrier((grad_slots[1], qkv_grads[0]))
        qkv_grad = []
        outs, totals = saved[group]
        for job, log_total in zip(jobs[group], totals):
            qkv_grad, back_sums = attend_backward(
                me,
                job[0],
                qkv[group],
                outs,
                grad_slots[group],
                scale_lanes,
                log_total,
                qkv_grad,
                *job[1:],
            )
            bias_sums = bias_sums + jnp.sum(back_sums, axis=0).transpose(1, 0, 2).reshape(8, part)
        qkv_grads.append(qkv_grad)
        if group == 0:
            arrived = send_back(qkv_grad)
    weight_grad = head_grads(
        [rows for group in normed_slots for rows in group],
        [piece for group in qkv_grads for piece in group],
        out_grads,
    )
    qkv_grads[1], weight_grad = lax.optimization_barrier((qkv_grads[1], weight_grad))
    arrived_last = send_back(qkv_grads[1])
    finish_back(0, arrived)
    mid_terms = (mid_sums[0] + mid_sums[1])[:3].reshape(3, batches, slots, share)
    mid_terms = turn(mid_terms.transpose(0, 2, 1, 3), me[0])
    norm_sums = sums[0] + sums[1]
    own_sums = lax.dynamic_update_slice(
        jnp.zeros((slots, 3 * part), F32), bias_sums[:3].reshape(1, -1), (me[0], jnp.int32(0))
    )
    shared = jnp.concatenate(
        [norm_sums[1:7].reshape(-1), mid_terms.reshape(-1), own_sums.reshape(-1)]
    ).reshape(-1, LANES)
    axes = (("batch", batches), ("head", slots))
    weight_grad, shared, grads[0] = lax.optimization_barrier((weight_grad, shared, grads[0]))
    summed_weight, summed = batch_sum(weight_grad.reshape(4 * width, part), shared, axes)
    arrived_last, summed_weight, both = lax.optimization_barrier(
        (arrived_last, summed_weight, both)
    )
    summed_weight = summed_weight.reshape(4, width, part)
    both = both.reshape(slots, share, 2 * width)
    both_grads = both[0].astype(F32)
    for slot in range(1, slots):
        both_grads = both_grads + deliver(both[slot], slot).astype(F32)
    finish_back(1, arrived_last)
    late = first_sums[0] + first_sums[1]
    late, both_grads = lax.optimization_barrier((late, both_grads))
    late = small_sum(late[:2].reshape(-1, LANES), axes).reshape(2, width)
    summed = summed.reshape(-1)
    norm_sums, mid_terms, own_sums = jnp.split(
        summed, [6 * width, 6 * width + 3 * mid_gain.shape[0]]
    )
    norm_sums = norm_sums.reshape(6, width)
    mid_terms = mid_terms.reshape(3, -1)
    own_sums = lax.dynamic_slice(
        own_sums.reshape(slots, 3 * part), (me[0], jnp.int32(0)), (1, 3 * part)
    ).reshape(3, part)
    return (
        outputs[1][:short_tokens].reshape(shapes[0]),
        outputs[1][short_tokens:].reshape(shapes[1]),
        outputs[0].reshape(shapes[2]),
        grads[1][:short_tokens].reshape(shapes[0]),
        grads[1][short_tokens:].reshape(shapes[1]),
        grads[0].reshape(shapes[2]),
        jnp.concatenate([late[:1], norm_sums[:2]], 0),
        jnp.concatenate([late[1:], norm_sums[2:]], 0),
        summed_weight[:3].astype(F32),
        own_sums[:2],
        jnp.sum(own_sums[2].reshape(-1, HEAD), axis=1),
        jnp.concatenate(
            [summed_weight[3, at : at + part] for at in range(0, width, part)], 1
        ).astype(F32),
        both_grads[:, width:],
        mid_terms[0],
        jnp.stack([mid_terms[2], mid_terms[1]]),
        both_grads[:, :width],
    )


def solution(mesh):
    in_specs = (
        P("batch", "head", None),
        P("batch", "head", None),
        P("batch", "head", None),
        P("batch"),
        P("batch"),
        P("batch"),
        P("batch", "head", None),
        P("batch", "head", None),
        P("batch", "head", None),
        P(),
        P(),
        P(None, None, "head"),
        P(None, "head"),
        P("head"),
        P("head", None),
        P(("head", "batch"), None),
        P(),
        P(),
        P(("head", "batch"), None),
    )
    out_specs = (
        P("batch", "head", None),
        P("batch", "head", None),
        P("batch", "head", None),
        P("batch", "head", None),
        P("batch", "head", None),
        P("batch", "head", None),
        P(),
        P(),
        P(None, None, "head"),
        P(None, "head"),
        P("head"),
        P("head", None),
        P(("head", "batch"), None),
        P(),
        P(),
        P(("head", "batch"), None),
    )
    return jax.shard_map(
        functools.partial(shards, mesh.shape["head"]),
        mesh=mesh,
        in_specs=in_specs,
        out_specs=out_specs,
        check_vma=False,
    )
```
